128 devices in a mesh: pb: 4 (over x), db: 32 (over z, y, core).
Axes of the slice: x: 4, y: 4, z: 4, core: 2. Of those that a mesh axis runs over, the one named last changes fastest.
Arguments:
- database: bfloat16 [8192, 768], P('db')
- neighbours: int32 [8192, 16], P('db'), may hold values from 0 to 8191, as said below
- valid_count: int32 [8192], P('db'), may hold values from 9 to 16, as said below
- queries: bfloat16 [65536, 768], P('pb'), may hold values from -6 to 6
Outputs:
- augmented: bfloat16 [8192, 768], P('db')
- best_score: float32 [65536], P('pb')
The draws below stay inside these ranges and needn't reach their ends.
Inputs may be any that keep to these rules, and one draw needn't show every extreme that they name: `neighbours`: every entry is a row number of the whole database, also in slots at or past valid_count (those carry no weight). The owner of row r is r // 256. In each aligned block of 64 rows, at most 64 of its 1024 entries name rows of one owner, and in every block some owner is named by exactly 64 entries. `valid_count`: every aligned block of 64 rows holds a row with 16 valid slots.
All inputs are finite; a program needn't handle non-finite values.
Results may differ from the reference program's by a relative error of at most 0.0028.
Values may be sent and summed in bfloat16 or wider, within the bound.
A program may use at most 128 MiB of HBM per device.

```python
import math
import jax
import jax.numpy as jnp
from jax import lax

D = 768
K = 16
ROW_DEV = 256
QROWS = 64
OWNERS = 32
CAP = 64
ROWS = 8192
QUERIES = 65536


def draw_database(key, part):
    key = jax.random.fold_in(key, 1)
    key_main, key_rows, key_cols = jax.random.split(key, 3)
    row_scale = jnp.exp(jax.random.uniform(key_rows, (ROWS, 1), jnp.float32, 0.0, math.log(10.0)))
    col_scale = jnp.exp(jax.random.uniform(key_cols, (1, D), jnp.float32, 0.0, math.log(10.0)))
    values = jax.random.normal(key_main, (ROWS, D), jnp.float32) * row_scale * col_scale / 3.0
    return values.astype(jnp.bfloat16)


def owner_block(block_key):
    key_rank, key_spread, key_order, key_local = jax.random.split(block_key, 4)
    total = K * QROWS
    base_count = (total - CAP) // (OWNERS - 1)
    extra_count = total - CAP - base_count * (OWNERS - 1)
    positions = jnp.arange(OWNERS, dtype=jnp.int32)
    rank_of = jax.random.permutation(key_rank, OWNERS).astype(jnp.int32)
    spread = jax.random.randint(key_spread, (OWNERS,), 0, base_count // 2 + 1, dtype=jnp.int32)
    next_rank = jnp.where(positions < OWNERS - 1, positions + 1, 1)
    change = spread[rank_of] - spread[next_rank[rank_of]]
    drawn = base_count + (rank_of <= extra_count).astype(jnp.int32) + change
    counts = jnp.where(rank_of == 0, CAP, drawn)
    ends = jnp.cumsum(counts)
    slots = jnp.arange(total, dtype=jnp.int32)
    owner_of = jnp.sum((slots[:, None] >= ends[None, :]).astype(jnp.int32), axis=1)
    order = jax.random.permutation(key_order, total)
    owner_of = owner_of[order]
    local_row = jax.random.randint(key_local, (total,), 0, ROW_DEV, dtype=jnp.int32)
    return (owner_of * ROW_DEV + local_row).reshape(QROWS, K)


def draw_neighbours(key, part):
    key = jax.random.fold_in(key, 2)
    block_keys = jax.random.split(key, ROWS // QROWS)
    return jax.vmap(owner_block)(block_keys).reshape(ROWS, K)


def draw_valid_count(key, part):
    key = jax.random.fold_in(key, 3)
    key_counts, key_place = jax.random.split(key, 2)
    counts = jax.random.randint(key_counts, (ROWS // QROWS, QROWS), K // 2 + 1, K + 1, dtype=jnp.int32)
    place = jax.random.randint(key_place, (ROWS // QROWS, 1), 0, QROWS, dtype=jnp.int32)
    counts = jnp.where(jnp.arange(QROWS, dtype=jnp.int32)[None, :] == place, K, counts)
    return counts.reshape(ROWS)


def steps_of(stream_key, shape, shards, smallest, high):
    gain, own = 1.0, jax.random.fold_in(stream_key, 6)
    for axis_at, shards_of in shards:
        steps = jnp.exp(jax.random.uniform(jax.random.fold_in(own, axis_at), (shards_of,), jnp.float32, smallest / len(shards), high / len(shards)))
        gain = gain * jnp.repeat(steps, shape[axis_at] // shards_of).reshape([-1 if axis == axis_at else 1 for axis in range(len(shape))])
    return gain


def normal_values(own_key, dims, scale, reach, cuts=(), kind=jnp.bfloat16):
    result = scale * jax.random.normal(own_key, dims, jnp.float32)
    if cuts:
        result = result * steps_of(own_key, dims, cuts, -0.22, 0.18)
    return jnp.clip(result, -reach, reach).astype(kind)


def setup_inputs(seed: int = 0) -> dict:
    arg_keys = jax.random.split(jax.random.key(seed), 5)
    database = draw_database(jax.random.fold_in(arg_keys[4], 71), 0)
    neighbours = draw_neighbours(jax.random.fold_in(arg_keys[4], 71), 0)
    valid_count = draw_valid_count(jax.random.fold_in(arg_keys[4], 71), 0)
    queries = normal_values(arg_keys[3], (QUERIES, D), 1.0, 6.0, ((0, 4),))
    return {"database": database, "neighbours": neighbours, "valid_count": valid_count, "queries": queries}


epsilon = 1e-06

def inverse_norms(values):
    squares = lax.optimization_barrier(jnp.sum(values * values, axis=-1))
    return lax.rsqrt(squares + epsilon)

def augment_rows(own_rows, fetched, valid_here):
    own_float = own_rows.astype(jnp.float32)
    fetched_float = fetched.astype(jnp.float32)
    own_inverse = inverse_norms(own_float)
    far_inverse = inverse_norms(fetched_float)
    cosine = jnp.einsum('rd,rkd->rk', own_float, fetched_float) * own_inverse[:, None] * far_inverse
    halfway = (1.0 + cosine) * 0.5
    mask_on = jnp.arange(fetched.shape[1], dtype=jnp.int32)[None, :] < valid_here[:, None]
    weight = jnp.where(mask_on, halfway * halfway * halfway, jnp.zeros_like(halfway))
    coefficient = (weight * far_inverse).astype(jnp.bfloat16)
    summed = own_float * own_inverse[:, None] + jnp.einsum('rk,rkd->rd', coefficient.astype(jnp.float32), fetched_float)
    return (summed * inverse_norms(summed)[:, None]).astype(jnp.bfloat16)

def reference(database, neighbours, valid_count, queries):

    def one_shard(shard_index):
        first_row = shard_index * ROW_DEV
        own_rows = lax.dynamic_slice_in_dim(database, first_row, ROW_DEV, 0)
        wanted_ids = lax.dynamic_slice_in_dim(neighbours, first_row, ROW_DEV, 0)
        valid_here = lax.dynamic_slice_in_dim(valid_count, first_row, ROW_DEV, 0)
        fetched = database[wanted_ids]
        return augment_rows(own_rows, fetched, valid_here)
    shard_list = jnp.arange(OWNERS, dtype=jnp.int32)
    augmented = lax.map(one_shard, shard_list).reshape(ROWS, D)

    def best_of(shard_index):
        block_rows = lax.dynamic_slice_in_dim(augmented, shard_index * ROW_DEV, ROW_DEV, 0)
        scores = jnp.dot(queries, block_rows.T, preferred_element_type=jnp.float32)
        return lax.optimization_barrier(jnp.max(scores, axis=1))
    best_score = lax.optimization_barrier(jnp.max(lax.map(best_of, shard_list), axis=0))
    return (augmented, best_score)
```

```python
import functools

import jax
import jax.numpy as jnp
from jax import lax
from jax.experimental import pallas as pl
from jax.experimental.pallas import tpu as pltpu
from jax.sharding import PartitionSpec as P

epsilon = 1e-06
MESH = pl.DeviceIdType.MESH
SIDE = 4
CORES = 2
CHIPS = SIDE * SIDE
SLOTS = (
    (0, 0), (0, 1), (0, 3), (1, 0), (3, 0), (0, 2), (2, 0), (1, 1),
    (1, 3), (3, 1), (3, 3), (1, 2), (2, 1), (3, 2), (2, 3), (2, 2),
)
SLOT_AT = {offset: place for place, offset in enumerate(SLOTS)}
RING = (1, 3, 2)


def inverse_norm(values):
    return lax.rsqrt(jnp.sum(values * values, axis=-1, keepdims=True) + epsilon)


def dot_rows(left, right):
    return lax.dot_general(
        left, right, (((1,), (1,)), ((), ())), preferred_element_type=jnp.float32
    )


def kernel(
    db_ref, nb_ref, vc_ref, q_ref, aug_ref, best_ref,
    q_v, pool, mask_ref, wanted, total, part_in, everyone, tops, rivals, bases,
    q_sem, a_send, a_recv, b_send, b_recv, c_send, c_recv, p_send, p_recv,
    g_send, g_recv, s_send, s_recv, m_send, m_recv, f_send, f_recv, e_send, e_recv,
):
    rows_dev, features = db_ref.shape
    fanout = nb_ref.shape[1]
    own_rows = rows_dev // SIDE
    half = own_rows // 2
    slot_rows = CORES * own_rows
    x = lax.axis_index("pb")
    d = lax.axis_index("db")
    c = d % CORES
    chip = d // CORES
    y = chip % SIDE
    z = chip // SIDE
    mine = pl.multiple_of(x * own_rows, own_rows)

    def plane(dz, dy):
        return (x, ((z + dz) % SIDE * SIDE + (y + dy) % SIDE) * CORES + c)

    sibling = (x, chip * CORES + (1 - c))

    def across(dx):
        return ((x + dx) % SIDE, d)

    def remote(src, dst, send, recv, to):
        return pltpu.make_async_remote_copy(
            src_ref=src, dst_ref=dst, send_sem=send, recv_sem=recv, device_id=to,
            device_id_type=MESH,
        )

    barrier = pltpu.get_barrier_semaphore()
    partners = [plane(dz, dy) for dz, dy in SLOTS[1:]]
    partners += [sibling] + [across(dx) for dx in RING]
    for partner in partners:
        pl.semaphore_signal(barrier, inc=1, device_id=partner, device_id_type=MESH)

    queries_here = q_v.shape[0]
    piece = queries_here // 4
    for k in range(4):
        pltpu.make_async_copy(
            q_ref.at[pl.ds(pl.multiple_of(c * queries_here + k * piece, piece), piece)],
            q_v.at[pl.ds(k * piece, piece)],
            q_sem.at[k],
        ).start()

    pool[pl.ds(0, own_rows), :] = db_ref[pl.ds(mine, own_rows), :]
    pl.semaphore_wait(barrier, len(partners))

    def block(place, core, start, rows):
        return pool.at[pl.ds(place * slot_rows + core * own_rows + start, rows)]

    def copy_a(dz, dy):
        src = SLOT_AT[(0, dy if dz else 0)]
        dst = SLOT_AT[(dz, dy)]
        to = plane(dz, 0) if dz else plane(0, dy)
        return remote(
            block(src, 0, 0, half), block(dst, 0, 0, half), a_send.at[dst], a_recv.at[dst], to
        )

    def copy_b(dz, dy):
        src = SLOT_AT[(dz if dy else 0, 0)]
        dst = SLOT_AT[(dz, dy)]
        to = plane(0, dy) if dy else plane(dz, 0)
        return remote(
            block(src, 0, half, half), block(dst, 0, half, half), b_send.at[dst],
            b_recv.at[dst], to,
        )

    def copy_c(place):
        return remote(
            block(place, 0, 0, own_rows), block(place, 1, 0, own_rows), c_send.at[place],
            c_recv.at[place], sibling,
        )

    def arrival(place, start, sems, recvs):
        spot = block(place, 0, start, half)
        return remote(spot, spot, sems.at[place], recvs.at[place], sibling)

    for step in RING:
        copy_a(0, step).start()
        copy_b(step, 0).start()
    copy_c(0).start()
    for step in RING:
        copy_a(step, 0).start()
        copy_b(0, step).start()

    eye = (
        lax.broadcasted_iota(jnp.int32, (fanout, fanout), 0)
        == lax.broadcasted_iota(jnp.int32, (fanout, fanout), 1)
    ).astype(jnp.float32).astype(jnp.bfloat16)
    ids = nb_ref[...]
    high = dot_rows(eye, (ids // 64).astype(jnp.float32).astype(jnp.bfloat16))
    low = dot_rows(eye, (ids % 64).astype(jnp.float32).astype(jnp.bfloat16))
    place_of = lax.broadcasted_iota(jnp.int32, (fanout, rows_dev), 0)
    wanted[...] = jnp.where(place_of < vc_ref[...], high * 64.0 + low, -1.0)
    for place, (dz, dy) in enumerate(SLOTS):
        for core in range(CORES):
            owner = ((z - dz) % SIDE * SIDE + (y - dy) % SIDE) * CORES + (c + core) % CORES
            bases[place * CORES + core] = owner * rows_dev + x * own_rows

    def build_mask(g, _):
        for u in range(2):
            counts = []
            for core in range(CORES):
                base = bases[(g * 2 + u) * CORES + core]
                number = base + lax.broadcasted_iota(jnp.int32, (own_rows, rows_dev), 0)
                number = number.astype(jnp.float32)
                count = jnp.zeros((own_rows, rows_dev), jnp.float32)
                for k in range(fanout):
                    count = count + jnp.where(wanted[pl.ds(k, 1), :] == number, 1.0, 0.0)
                counts.append(count)
            both = jnp.concatenate(counts, axis=0)
            mask_ref[g, :, pl.ds(u * slot_rows, slot_rows)] = both.T.astype(jnp.bfloat16)
        return 0

    groups = len(SLOTS) // 2
    lax.fori_loop(0, 2, build_mask, 0)

    for step in RING:
        copy_a(0, step).wait_recv()
        for far in RING:
            copy_a(far, step).start()
        copy_b(step, 0).wait_recv()
        for far in RING:
            copy_b(step, far).start()

    lax.fori_loop(2, groups, build_mask, 0)

    for step in RING:
        copy_b(0, step).wait_recv()
        copy_c(SLOT_AT[(0, step)]).start()
        copy_a(step, 0).wait_recv()
        copy_c(SLOT_AT[(step, 0)]).start()
    arrival(7, 0, a_send, a_recv).wait_recv()
    arrival(7, half, b_send, b_recv).wait_recv()
    copy_c(7).start()

    total[...] = jnp.zeros_like(total)
    own = db_ref[...]
    own_inverse = inverse_norm(own.astype(jnp.float32))
    span = 2 * slot_rows

    def take(g, _):
        place = groups + g
        arrival(place, 0, a_send, a_recv).wait_recv()
        arrival(place, half, b_send, b_recv).wait_recv()
        copy_c(place).start()
        copy_c(2 * g).wait_recv()
        copy_c(2 * g + 1).wait_recv()
        rows = pool[pl.ds(pl.multiple_of(g * span, span), span), :]
        squares = rows.astype(jnp.float32)
        squares = squares * squares
        folded = squares[:, 0:128]
        for k in range(1, features // 128):
            folded = folded + squares[:, k * 128 : (k + 1) * 128]
        far_inverse = lax.rsqrt(jnp.sum(folded.T, axis=0, keepdims=True) + epsilon)
        cosine = dot_rows(own, rows) * own_inverse * far_inverse
        halfway = (1.0 + cosine) * 0.5
        weight = halfway * halfway * halfway
        coefficient = (weight * far_inverse).astype(jnp.bfloat16).astype(jnp.float32)
        count = mask_ref[g].astype(jnp.float32)
        spread = jnp.where(count > 0.0, count * coefficient, 0.0)
        spread_high = spread.astype(jnp.bfloat16)
        spread_low = (spread - spread_high.astype(jnp.float32)).astype(jnp.bfloat16)
        total[...] += jnp.dot(spread_high, rows, preferred_element_type=jnp.float32) + jnp.dot(
            spread_low, rows, preferred_element_type=jnp.float32
        )
        return 0

    lax.fori_loop(0, groups, take, 0)

    def quarter(dx):
        return pl.ds(pl.multiple_of((x + dx) % SIDE * own_rows, own_rows), own_rows)

    def copy_p(dx):
        return remote(
            total.at[quarter(dx)], part_in.at[dx - 1], p_send.at[dx], p_recv.at[dx], across(dx)
        )

    for dx in RING:
        copy_p(dx).start()
    kept = db_ref[pl.ds(mine, own_rows), :].astype(jnp.float32)
    summed = kept * inverse_norm(kept) + total[pl.ds(mine, own_rows), :]
    for dx in RING:
        copy_p(dx).wait_recv()
        summed = summed + part_in[dx - 1]
    everyone[pl.ds(mine, own_rows), :] = (summed * inverse_norm(summed)).astype(jnp.bfloat16)

    def copy_g(dx):
        spot = everyone.at[pl.ds(mine, own_rows)]
        return remote(spot, spot, g_send.at[dx], g_recv.at[dx], across(dx))

    def copy_s(dx):
        return remote(
            everyone.at[quarter(-dx)],
            everyone.at[pl.ds(pl.multiple_of(rows_dev + (x - dx) % SIDE * own_rows, own_rows), own_rows)],
            s_send.at[dx], s_recv.at[dx], sibling,
        )

    for dx in RING:
        copy_g(dx).start()
    copy_s(0).start()
    for dx in RING:
        copy_g(dx).wait_recv()
        copy_s(dx).start()
    for dx in range(SIDE):
        copy_s(dx).wait_recv()

    for k in range(4):
        pltpu.make_async_copy(
            q_ref.at[pl.ds(pl.multiple_of(c * queries_here + k * piece, piece), piece)],
            q_v.at[pl.ds(k * piece, piece)],
            q_sem.at[k],
        ).wait()

    share = queries_here // CHIPS
    lines = share // 128

    def chip_at(k):
        return (x, (chip + k) % CHIPS * CORES + c)

    def copy_m(k):
        return remote(tops.at[k], rivals.at[k], m_send.at[k], m_recv.at[k], chip_at(k))

    unroll = 4

    def score(i, _):
        for u in range(unroll):
            k = (i * unroll + u + 1) % CHIPS
            owner = (chip + k) % CHIPS
            panel = q_v[pl.ds(pl.multiple_of(owner * share, share), share), :]
            top = jnp.max(dot_rows(everyone[...], panel), axis=0, keepdims=True)
            for line in range(lines):
                tops[k, pl.ds(line, 1), :] = top[:, line * 128 : (line + 1) * 128]
            if u < unroll - 1:
                copy_m(k).start()
            else:
                @pl.when(i < CHIPS // unroll - 1)
                def _():
                    copy_m(k).start()
        return 0

    lax.fori_loop(0, CHIPS // unroll, score, 0)
    aug_ref[...] = everyone[pl.ds(0, rows_dev), :]
    best = tops[0]
    for k in range(1, CHIPS):
        copy_m(k).wait_recv()
        best = jnp.maximum(best, rivals[k])
    spot = c * CHIPS + chip
    best_ref[spot] = best

    def copy_f(k):
        return remote(
            best_ref.at[spot], best_ref.at[spot], f_send.at[k], f_recv.at[k], chip_at(k)
        )

    for k in range(1, CHIPS):
        copy_f(k).start()
    for k in range(1, CHIPS):
        copy_f(k).wait_recv()
    side = best_ref.at[pl.ds(c * CHIPS, CHIPS)]
    copy_e = remote(side, side, e_send, e_recv, sibling)
    copy_e.start()

    for place in range(1, CHIPS):
        arrival(place, 0, a_send, a_recv).wait_send()
        arrival(place, half, b_send, b_recv).wait_send()
    for place in range(CHIPS):
        copy_c(place).wait_send()
    for dx in RING:
        copy_p(dx).wait_send()
        copy_g(dx).wait_send()
    for dx in range(SIDE):
        copy_s(dx).wait_send()
    for k in range(1, CHIPS):
        copy_m(k).wait_send()
        copy_f(k).wait_send()
    copy_e.wait()


def local(database, neighbours, valid_count, queries):
    rows_dev, features = database.shape
    queries_here = queries.shape[0] // CORES
    own_rows = rows_dev // SIDE
    pool_rows = rows_dev * CHIPS * CORES // SIDE
    share = queries_here // CHIPS
    vmem = pl.BlockSpec(memory_space=pltpu.VMEM)
    dma = pltpu.SemaphoreType.DMA
    augmented, best = pl.pallas_call(
        kernel,
        out_shape=(
            jax.ShapeDtypeStruct((rows_dev, features), jnp.bfloat16),
            jax.ShapeDtypeStruct((CORES * CHIPS, share // 128, 128), jnp.float32),
        ),
        in_specs=[vmem, vmem, vmem, pl.BlockSpec(memory_space=pl.ANY)],
        out_specs=(vmem, vmem),
        scratch_shapes=[
            pltpu.VMEM((queries_here, features), jnp.bfloat16),
            pltpu.VMEM((pool_rows, features), jnp.bfloat16),
            pltpu.VMEM((8, rows_dev, pool_rows // 8), jnp.bfloat16),
            pltpu.VMEM((neighbours.shape[1], rows_dev), jnp.float32),
            pltpu.VMEM((rows_dev, features), jnp.float32),
            pltpu.VMEM((SIDE - 1, own_rows, features), jnp.float32),
            pltpu.VMEM((CORES * rows_dev, features), jnp.bfloat16),
            pltpu.VMEM((CHIPS, share // 128, 128), jnp.float32),
            pltpu.VMEM((CHIPS, share // 128, 128), jnp.float32),
            pltpu.SMEM((CHIPS * CORES,), jnp.int32),
            dma((4,)),
        ]
        + [dma((CHIPS,))] * 6
        + [dma((SIDE,))] * 6
        + [dma((CHIPS,))] * 4
        + [dma, dma],
        compiler_params=pltpu.CompilerParams(
            collective_id=0, has_side_effects=True, vmem_limit_bytes=56 * 2**20
        ),
        name="expand_and_score",
    )(database, neighbours, valid_count.reshape(1, rows_dev), queries)
    return augmented, best.reshape(queries.shape[0])


def solution(mesh):
    return jax.shard_map(
        local,
        mesh=mesh,
        in_specs=(P("db", None), P("db", None), P("db"), P("pb", None)),
        out_specs=(P("db", None), P("pb")),
        check_vma=False,
    )
```

```python
import functools

import jax
import jax.numpy as jnp
from jax import lax
from jax.experimental import pallas as pl
from jax.experimental.pallas import tpu as pltpu
from jax.sharding import PartitionSpec as P

epsilon = 1e-06
MESH = pl.DeviceIdType.MESH
SIDE = 4
CORES = 2
CHIPS = SIDE * SIDE
SLOTS = (
    (0, 0), (0, 1), (0, 3), (1, 0), (3, 0), (0, 2), (2, 0), (1, 1),
    (1, 3), (3, 1), (3, 3), (1, 2), (2, 1), (3, 2), (2, 3), (2, 2),
)
SLOT_AT = {offset: place for place, offset in enumerate(SLOTS)}
RING = (1, 3, 2)


def inverse_norm(values):
    return lax.rsqrt(jnp.sum(values * values, axis=-1, keepdims=True) + epsilon)


def dot_rows(left, right):
    return lax.dot_general(
        left, right, (((1,), (1,)), ((), ())), preferred_element_type=jnp.float32
    )


def kernel(
    db_hbm, nb_hbm, vc_hbm, q_ref, aug_ref, best_ref,
    q_v, db_ref, nb_ref, vc_ref, pool, mask_ref, wanted, total, coded, coded_in, ranges, ranges_in, ranges_of,
    everyone, first_top, tops, rivals, bases,
    q_sem, l_sem, a_send, a_recv, b_send, b_recv, c_send, c_recv, p_send, p_recv, r_send, r_recv,
    g_send, g_recv, s_send, s_recv, m_send, m_recv, f_send, f_recv,
):
    rows_dev, features = db_ref.shape
    fanout = nb_ref.shape[0]
    own_rows = rows_dev // SIDE
    half = own_rows // 2
    slot_rows = CORES * own_rows
    x = lax.axis_index("pb")
    d = lax.axis_index("db")
    c = d % CORES
    chip = d // CORES
    y = chip % SIDE
    z = chip // SIDE
    mine = pl.multiple_of(x * own_rows, own_rows)

    def plane(dz, dy):
        return (x, ((z + dz) % SIDE * SIDE + (y + dy) % SIDE) * CORES + c)

    sibling = (x, chip * CORES + (1 - c))

    def across(dx):
        return ((x + dx) % SIDE, d)

    def remote(src, dst, send, recv, to):
        return pltpu.make_async_remote_copy(
            src_ref=src, dst_ref=dst, send_sem=send, recv_sem=recv, device_id=to,
            device_id_type=MESH,
        )

    barrier = pltpu.get_barrier_semaphore()
    partners = [plane(0, step) for step in RING] + [plane(step, 0) for step in RING]
    partners += [sibling] + [across(step) for step in RING]
    for partner in partners:
        pl.semaphore_signal(barrier, inc=1, device_id=partner, device_id_type=MESH)

    loads = [
        pltpu.make_async_copy(
            db_hbm.at[pl.ds(mine, own_rows)], pool.at[pl.ds(0, own_rows)], l_sem.at[0]
        ),
        pltpu.make_async_copy(nb_hbm, nb_ref, l_sem.at[1]),
        pltpu.make_async_copy(vc_hbm, vc_ref, l_sem.at[2]),
        pltpu.make_async_copy(db_hbm, db_ref, l_sem.at[3]),
    ]
    for load in loads:
        load.start()

    queries_here = q_v.shape[0]
    piece = queries_here // 4
    query_loads = [
        pltpu.make_async_copy(
            q_ref.at[pl.ds(pl.multiple_of(c * queries_here + k * piece, piece), piece)],
            q_v.at[pl.ds(k * piece, piece)],
            q_sem.at[k],
        )
        for k in range(4)
    ]
    for load in query_loads:
        load.start()
    for load in loads:
        load.wait()
    pl.semaphore_wait(barrier, len(partners))

    def block(place, core, start, rows):
        return pool.at[pl.ds(place * slot_rows + core * own_rows + start, rows)]

    def copy_a(dz, dy):
        src = SLOT_AT[(0, dy if dz else 0)]
        dst = SLOT_AT[(dz, dy)]
        to = plane(dz, 0) if dz else plane(0, dy)
        return remote(
            block(src, 0, 0, half), block(dst, 0, 0, half), a_send.at[dst], a_recv.at[dst], to
        )

    def copy_b(dz, dy):
        src = SLOT_AT[(dz if dy else 0, 0)]
        dst = SLOT_AT[(dz, dy)]
        to = plane(0, dy) if dy else plane(dz, 0)
        return remote(
            block(src, 0, half, half), block(dst, 0, half, half), b_send.at[dst],
            b_recv.at[dst], to,
        )

    def copy_c(place):
        return remote(
            block(place, 0, 0, own_rows), block(place, 1, 0, own_rows), c_send.at[place],
            c_recv.at[place], sibling,
        )

    def arrival(place, start, sems, recvs):
        spot = block(place, 0, start, half)
        return remote(spot, spot, sems.at[place], recvs.at[place], sibling)

    for step in RING:
        copy_a(0, step).start()
        copy_b(step, 0).start()
    copy_c(0).start()
    for step in RING:
        copy_a(step, 0).start()
        copy_b(0, step).start()

    place_of = lax.broadcasted_iota(jnp.int32, (fanout, rows_dev), 0)
    wanted[...] = jnp.where(place_of < vc_ref[...], nb_ref[...], -1)
    for place, (dz, dy) in enumerate(SLOTS):
        for core in range(CORES):
            owner = ((z - dz) % SIDE * SIDE + (y - dy) % SIDE) * CORES + (c + core) % CORES
            bases[place * CORES + core] = owner * rows_dev + x * own_rows

    def build_mask(g, _):
        for u in range(2):
            counts = []
            for core in range(CORES):
                base = bases[(g * 2 + u) * CORES + core]
                number = base + lax.broadcasted_iota(jnp.int32, (own_rows, rows_dev), 0)
                count = jnp.zeros((own_rows, rows_dev), jnp.float32)
                for k in range(fanout):
                    count = count + jnp.where(wanted[pl.ds(k, 1), :] == number, 1.0, 0.0)
                counts.append(count)
            both = jnp.concatenate(counts, axis=0)
            mask_ref[g, :, pl.ds(u * slot_rows, slot_rows)] = both.T.astype(jnp.bfloat16)
        return 0

    groups = len(SLOTS) // 2
    lax.fori_loop(0, 2, build_mask, 0)

    for step in RING:
        copy_a(0, step).wait_recv()
        for far in RING:
            copy_a(far, step).start()
        copy_b(step, 0).wait_recv()
        for far in RING:
            copy_b(step, far).start()

    lax.fori_loop(2, groups, build_mask, 0)

    for step in RING:
        copy_b(0, step).wait_recv()
        copy_c(SLOT_AT[(0, step)]).start()
        copy_a(step, 0).wait_recv()
        copy_c(SLOT_AT[(step, 0)]).start()

    def pass_on(place):
        arrival(place, 0, a_send, a_recv).wait_recv()
        arrival(place, half, b_send, b_recv).wait_recv()
        copy_c(place).start()

    total[...] = jnp.zeros_like(total)
    own = db_ref[...]
    own_inverse = inverse_norm(own.astype(jnp.float32))
    span = 2 * slot_rows

    def take(g):
        copy_c(2 * g).wait_recv()
        copy_c(2 * g + 1).wait_recv()
        rows = pool[pl.ds(pl.multiple_of(g * span, span), span), :]
        squares = rows.astype(jnp.float32)
        squares = squares * squares
        folded = squares[:, 0:128]
        for k in range(1, features // 128):
            folded = folded + squares[:, k * 128 : (k + 1) * 128]
        far_inverse = lax.rsqrt(jnp.sum(folded.T, axis=0, keepdims=True) + epsilon)
        cosine = dot_rows(own, rows) * own_inverse * far_inverse
        halfway = (1.0 + cosine) * 0.5
        weight = halfway * halfway * halfway
        coefficient = (weight * far_inverse).astype(jnp.bfloat16).astype(jnp.float32)
        count = mask_ref[g].astype(jnp.float32)
        spread = jnp.where(count > 0.0, count * coefficient, 0.0)
        spread_high = spread.astype(jnp.bfloat16)
        spread_low = (spread - spread_high.astype(jnp.float32)).astype(jnp.bfloat16)
        total[...] += jnp.dot(spread_high, rows, preferred_element_type=jnp.float32) + jnp.dot(
            spread_low, rows, preferred_element_type=jnp.float32
        )

    def take_early(g, _):
        take(g)
        return 0

    def take_late(g, _):
        for ahead in (3, 4):
            place = 2 * g + ahead

            @pl.when(place < CHIPS)
            def _():
                pass_on(place)

        take(g)
        return 0

    lax.fori_loop(0, 3, take_early, 0)
    pass_on(7)
    pass_on(8)
    lax.fori_loop(3, groups, take_late, 0)

    partial = total[...]
    largest = jnp.max(jnp.abs(partial), axis=-1, keepdims=True)
    largest = jnp.maximum(largest, 1e-30)
    coded[...] = jnp.round(partial * (32760.0 / largest)).astype(jnp.int32).astype(jnp.int16)
    spread_range = jnp.broadcast_to(largest * (1.0 / 32760.0), (rows_dev, 128))
    ranges[...] = spread_range.T[0:8, :]

    def quarter(dx, h):
        start = (x + dx) % SIDE * own_rows + h * half
        return pl.ds(pl.multiple_of(start, half), half)

    def copy_r(dx):
        return remote(ranges, ranges_in.at[dx - 1], r_send.at[dx], r_recv.at[dx], across(dx))

    def copy_p(dx, h):
        at = h * SIDE + dx
        return remote(
            coded.at[quarter(dx, h)], coded_in.at[dx - 1, pl.ds(h * half, half)],
            p_send.at[at], p_recv.at[at], across(dx),
        )

    for dx in RING:
        copy_r(dx).start()
    for h in range(2):
        for dx in RING:
            copy_p(dx, h).start()

    def spot(h, core, chip_x):
        start = (h * CORES + core) * SIDE * half + chip_x * half
        return pl.ds(pl.multiple_of(start, half), half)

    def copy_g(dx, h):
        at = h * SIDE + dx
        here = everyone.at[spot(h, 0, x)]
        return remote(here, here, g_send.at[at], g_recv.at[at], across(dx))

    def copy_s(dx, h):
        at = h * SIDE + dx
        from_x = (x + SIDE - dx) % SIDE
        return remote(
            everyone.at[spot(h, 0, from_x)], everyone.at[spot(h, 1, from_x)], s_send.at[at],
            s_recv.at[at], sibling,
        )

    sums = []
    for h in range(2):
        kept = db_ref[quarter(0, h), :].astype(jnp.float32)
        sums.append(kept * inverse_norm(kept) + total[quarter(0, h), :])
    for dx in RING:
        copy_r(dx).wait_recv()
        across_range = jnp.broadcast_to(ranges_in[dx - 1, 0:1, :], (128, rows_dev))
        ranges_of[dx - 1] = across_range.T

    for h in range(2):
        summed = sums[h]
        for dx in RING:
            copy_p(dx, h).wait_recv()
            part = coded_in[dx - 1, pl.ds(h * half, half), :].astype(jnp.float32)
            summed = summed + part * ranges_of[dx - 1, quarter(0, h), 0:1]
        everyone[spot(h, 0, x), :] = (summed * inverse_norm(summed)).astype(jnp.bfloat16)
        for dx in RING:
            copy_g(dx, h).start()
        copy_s(0, h).start()

    def hand_over(h):
        for dx in RING:
            copy_g(dx, h).wait_recv()
            copy_s(dx, h).start()

    hand_over(0)
    for load in query_loads:
        load.wait()
    for dx in range(SIDE):
        copy_s(dx, 0).wait_recv()

    share = queries_here // CHIPS
    lines = share // 128
    part_rows = CORES * SIDE * half

    def chip_at(k):
        return (x, (chip + k) % CHIPS * CORES + c)

    def copy_m(k):
        return remote(tops.at[k], rivals.at[k], m_send.at[k], m_recv.at[k], chip_at(k))

    def folded_scores(h, k):
        owner = (chip + k) % CHIPS
        panel = q_v[pl.ds(pl.multiple_of(owner * share, share), share), :]
        scores = dot_rows(everyone[pl.ds(h * part_rows, part_rows), :], panel)
        return jnp.max(scores.reshape(part_rows // 8, 8, share), axis=0)

    unroll = 4

    def score_first(i, _):
        for u in range(unroll):
            k = (i * unroll + u + 1) % CHIPS
            first_top[k] = folded_scores(0, k)
        return 0

    def score_second(i, _):
        for u in range(unroll):
            k = (i * unroll + u + 1) % CHIPS
            top = jnp.maximum(first_top[k], folded_scores(1, k))
            top = jnp.max(top, axis=0, keepdims=True)
            for line in range(lines):
                tops[k, pl.ds(line, 1), :] = top[:, line * 128 : (line + 1) * 128]
            if u < unroll - 1:
                copy_m(k).start()
            else:
                @pl.when(i < CHIPS // unroll - 1)
                def _():
                    copy_m(k).start()
        return 0

    lax.fori_loop(0, 1, score_first, 0)
    hand_over(1)
    lax.fori_loop(1, CHIPS // unroll, score_first, 0)
    for dx in range(SIDE):
        copy_s(dx, 1).wait_recv()
    lax.fori_loop(0, CHIPS // unroll, score_second, 0)

    for chip_x in range(SIDE):
        for h in range(2):
            start = h * part_rows + chip_x * half
            aug_ref[pl.ds(chip_x * own_rows + h * half, half), :] = everyone[pl.ds(start, half), :]
    best = tops[0]
    for k in range(1, CHIPS):
        copy_m(k).wait_recv()
        best = jnp.maximum(best, rivals[k])
    here = c * CHIPS + chip
    best_ref[here] = best
    devices = CHIPS * CORES

    def copy_f(k):
        return remote(
            best_ref.at[here], best_ref.at[here], f_send.at[k], f_recv.at[k],
            (x, (d + k) % devices),
        )

    for k in range(1, devices):
        copy_f(k).start()

    for place in range(1, CHIPS):
        arrival(place, 0, a_send, a_recv).wait_send()
        arrival(place, half, b_send, b_recv).wait_send()
    for place in range(CHIPS):
        copy_c(place).wait_send()
    for dx in RING:
        copy_r(dx).wait_send()
    for h in range(2):
        for dx in RING:
            copy_p(dx, h).wait_send()
            copy_g(dx, h).wait_send()
        for dx in range(SIDE):
            copy_s(dx, h).wait_send()
    for k in range(1, CHIPS):
        copy_m(k).wait_send()
    for k in range(1, devices):
        copy_f(k).wait()


def local(database, neighbours, valid_count, queries):
    rows_dev, features = database.shape
    fanout = neighbours.shape[1]
    queries_here = queries.shape[0] // CORES
    own_rows = rows_dev // SIDE
    pool_rows = rows_dev * CHIPS * CORES // SIDE
    share = queries_here // CHIPS
    vmem = pl.BlockSpec(memory_space=pltpu.VMEM)
    anywhere = pl.BlockSpec(memory_space=pl.ANY)
    dma = pltpu.SemaphoreType.DMA
    augmented, best = pl.pallas_call(
        kernel,
        out_shape=(
            jax.ShapeDtypeStruct((rows_dev, features), jnp.bfloat16),
            jax.ShapeDtypeStruct((CORES * CHIPS, share // 128, 128), jnp.float32),
        ),
        in_specs=[anywhere, anywhere, anywhere, anywhere],
        out_specs=(vmem, vmem),
        scratch_shapes=[
            pltpu.VMEM((queries_here, features), jnp.bfloat16),
            pltpu.VMEM((rows_dev, features), jnp.bfloat16),
            pltpu.VMEM((fanout, rows_dev), jnp.int32),
            pltpu.VMEM((1, rows_dev), jnp.int32),
            pltpu.VMEM((pool_rows, features), jnp.bfloat16),
            pltpu.VMEM((8, rows_dev, pool_rows // 8), jnp.bfloat16),
            pltpu.VMEM((fanout, rows_dev), jnp.int32),
            pltpu.VMEM((rows_dev, features), jnp.float32),
            pltpu.VMEM((rows_dev, features), jnp.int16),
            pltpu.VMEM((SIDE - 1, own_rows, features), jnp.int16),
            pltpu.VMEM((8, rows_dev), jnp.float32),
            pltpu.VMEM((SIDE - 1, 8, rows_dev), jnp.float32),
            pltpu.VMEM((SIDE - 1, rows_dev, 128), jnp.float32),
            pltpu.VMEM((CORES * rows_dev, features), jnp.bfloat16),
            pltpu.VMEM((CHIPS, 8, share), jnp.float32),
            pltpu.VMEM((CHIPS, share // 128, 128), jnp.float32),
            pltpu.VMEM((CHIPS, share // 128, 128), jnp.float32),
            pltpu.SMEM((CHIPS * CORES,), jnp.int32),
            dma((4,)),
            dma((4,)),
        ]
        + [dma((CHIPS,))] * 6
        + [dma((2 * SIDE,))] * 2
        + [dma((SIDE,))] * 2
        + [dma((2 * SIDE,))] * 4
        + [dma((CHIPS,))] * 2
        + [dma((CHIPS * CORES,))] * 2,
        compiler_params=pltpu.CompilerParams(
            collective_id=0, has_side_effects=True, vmem_limit_bytes=56 * 2**20
        ),
        name="expand_and_score",
    )(database, neighbours.T, valid_count.reshape(1, rows_dev), queries)
    return augmented, best.reshape(queries.shape[0])


def solution(mesh):
    return jax.shard_map(
        local,
        mesh=mesh,
        in_specs=(P("db", None), P("db", None), P("db"), P("pb", None)),
        out_specs=(P("db", None), P("pb")),
        check_vma=False,
    )
```

```python
import functools

import jax
import jax.numpy as jnp
from jax import lax
from jax.experimental import pallas as pl
from jax.experimental.pallas import tpu as pltpu
from jax.sharding import PartitionSpec as P

epsilon = 1e-06
MESH = pl.DeviceIdType.MESH
SIDE = 4
CORES = 2
CHIPS = SIDE * SIDE
SLOTS = (
    (0, 0), (0, 1), (0, 3), (1, 0), (3, 0), (0, 2), (2, 0), (1, 1),
    (1, 3), (3, 1), (3, 3), (1, 2), (2, 1), (3, 2), (2, 3), (2, 2),
)
SLOT_AT = {offset: place for place, offset in enumerate(SLOTS)}
RING = (1, 3, 2)


def inverse_norm(values):
    return lax.rsqrt(jnp.sum(values * values, axis=-1, keepdims=True) + epsilon)


def dot_rows(left, right):
    return lax.dot_general(
        left, right, (((1,), (1,)), ((), ())), preferred_element_type=jnp.float32
    )


def kernel(
    db_hbm, nb_hbm, vc_hbm, q_ref, aug_ref, best_ref,
    q_v, db_ref, nb_ref, vc_ref, pool, mask_ref, wanted, total, coded, coded_in, ranges, ranges_in, ranges_of,
    everyone, first_top, tops, rivals, bases,
    q_sem, l_sem, a_recv, b_recv, c_recv, p_recv, g_recv, s_recv, ab_send, c_send, r_send, r_recv,
    p_send, g_send, s_send, m_send, m_recv, f_send, f_recv,
):
    rows_dev, features = db_ref.shape
    fanout = nb_ref.shape[0]
    own_rows = rows_dev // SIDE
    half = own_rows // 2
    parity_rows = CHIPS * own_rows
    span = 4 * own_rows
    x = lax.axis_index("pb")
    d = lax.axis_index("db")
    c = d % CORES
    chip = d // CORES
    y = chip % SIDE
    z = chip // SIDE
    mine = pl.multiple_of(x * own_rows, own_rows)

    def plane(dz, dy):
        return (x, ((z + dz) % SIDE * SIDE + (y + dy) % SIDE) * CORES + c)

    sibling = (x, chip * CORES + (1 - c))

    def across(dx):
        return ((x + dx) % SIDE, d)

    def remote(src, dst, send, recv, to):
        return pltpu.make_async_remote_copy(
            src_ref=src, dst_ref=dst, send_sem=send, recv_sem=recv, device_id=to,
            device_id_type=MESH,
        )

    loads = [
        pltpu.make_async_copy(
            db_hbm.at[pl.ds(mine, own_rows)], pool.at[pl.ds(0, own_rows)], l_sem.at[0]
        ),
        pltpu.make_async_copy(nb_hbm, nb_ref, l_sem.at[1]),
        pltpu.make_async_copy(vc_hbm, vc_ref, l_sem.at[2]),
        pltpu.make_async_copy(db_hbm, db_ref, l_sem.at[3]),
    ]
    loads[0].start()

    barrier = pltpu.get_barrier_semaphore()
    partners = [plane(0, step) for step in RING] + [plane(step, 0) for step in RING]
    partners += [sibling] + [across(step) for step in RING]
    for partner in partners:
        pl.semaphore_signal(barrier, inc=1, device_id=partner, device_id_type=MESH)

    for load in loads[1:]:
        load.start()

    loads[0].wait()
    pl.semaphore_wait(barrier, len(partners))

    def block(place, core, start, rows):
        return pool.at[pl.ds(core * parity_rows + place * own_rows + start, rows)]

    def copy_a(dz, dy):
        src = SLOT_AT[(0, dy if dz else 0)]
        dst = SLOT_AT[(dz, dy)]
        to = plane(dz, 0) if dz else plane(0, dy)
        return remote(
            block(src, 0, 0, half), block(dst, 0, 0, half), ab_send, a_recv.at[dst], to
        )

    def copy_b(dz, dy):
        src = SLOT_AT[(dz if dy else 0, 0)]
        dst = SLOT_AT[(dz, dy)]
        to = plane(0, dy) if dy else plane(dz, 0)
        return remote(
            block(src, 0, half, half), block(dst, 0, half, half), ab_send,
            (a_recv if dz and dy else b_recv).at[dst], to,
        )

    def copy_c(place):
        return remote(
            block(place, 0, 0, own_rows), block(place, 1, 0, own_rows), c_send,
            c_recv.at[place // 4], sibling,
        )

    for step in RING:
        copy_a(0, step).start()
        copy_b(step, 0).start()
    copy_c(0).start()
    for step in RING:
        copy_a(step, 0).start()
        copy_b(0, step).start()

    queries_here = q_v.shape[0]
    piece = queries_here // 4
    query_loads = [
        pltpu.make_async_copy(
            q_ref.at[pl.ds(pl.multiple_of(c * queries_here + k * piece, piece), piece)],
            q_v.at[pl.ds(k * piece, piece)],
            q_sem.at[k],
        )
        for k in range(4)
    ]
    for load in query_loads:
        load.start()
    for load in loads[1:]:
        load.wait()

    place_of = lax.broadcasted_iota(jnp.int32, (fanout, rows_dev), 0)
    wanted[...] = jnp.where(place_of < vc_ref[...], nb_ref[...], -1)
    for place, (dz, dy) in enumerate(SLOTS):
        for core in range(CORES):
            owner = ((z - dz) % SIDE * SIDE + (y - dy) % SIDE) * CORES + (c + core) % CORES
            bases[core * CHIPS + place] = owner * rows_dev + x * own_rows

    def build_mask(part):
        for u in range(2):
            counts = []
            for v in range(2):
                base = bases[part * 4 + u * 2 + v]
                number = base + lax.broadcasted_iota(jnp.int32, (own_rows, rows_dev), 0)
                count = jnp.zeros((own_rows, rows_dev), jnp.float32)
                for k in range(fanout):
                    count = count + jnp.where(wanted[pl.ds(k, 1), :] == number, 1.0, 0.0)
                counts.append(count)
            both = jnp.concatenate(counts, axis=0)
            mask_ref[part, :, pl.ds(u * 2 * own_rows, 2 * own_rows)] = both.T.astype(jnp.bfloat16)

    def first_masks(i, _):
        build_mask(4 * i)
        return 0

    def other_masks(i, _):
        build_mask(i + 1 + i // 3)
        return 0

    lax.fori_loop(0, 2, first_masks, 0)

    for step in RING:
        copy_a(0, step).wait_recv()
        for far in RING:
            copy_a(far, step).start()
        copy_b(step, 0).wait_recv()
        for far in RING:
            copy_b(step, far).start()

    lax.fori_loop(0, 6, other_masks, 0)

    for step in RING:
        copy_b(0, step).wait_recv()
        copy_c(SLOT_AT[(0, step)]).start()
        copy_a(step, 0).wait_recv()
        copy_c(SLOT_AT[(step, 0)]).start()

    def pass_on(place):
        here = block(place, 0, 0, own_rows)
        remote(here, here, ab_send, a_recv.at[place], sibling).wait_recv()
        copy_c(place).start()

    total[...] = jnp.zeros_like(total)
    own = db_ref[...]
    own_inverse = inverse_norm(own.astype(jnp.float32))

    def take(g):
        rows = pool[pl.ds(pl.multiple_of(g * span, span), span), :]
        squares = rows.astype(jnp.float32)
        squares = squares * squares
        folded = squares[:, 0:128]
        for k in range(1, features // 128):
            folded = folded + squares[:, k * 128 : (k + 1) * 128]
        far_inverse = lax.rsqrt(jnp.sum(folded.T, axis=0, keepdims=True) + epsilon)
        cosine = dot_rows(own, rows) * own_inverse * far_inverse
        halfway = (1.0 + cosine) * 0.5
        weight = halfway * halfway * halfway
        coefficient = (weight * far_inverse).astype(jnp.bfloat16).astype(jnp.float32)
        count = mask_ref[g].astype(jnp.float32)
        spread = jnp.where(count > 0.0, count * coefficient, 0.0)
        total[...] += jnp.dot(
            spread.astype(jnp.bfloat16), rows, preferred_element_type=jnp.float32
        )

    def step_over(i, _):
        part = jnp.where(i < 4, i // 2 + i % 2 * 4, jnp.where(i < 6, i - 2, i))

        @pl.when(i == 2)
        def _():
            pass_on(7)

        @pl.when((i == 4) | (i == 5))
        def _():
            for u in range(4):
                pass_on(part * 4 + u)

        @pl.when(part >= 4)
        def _():
            here = pool.at[pl.ds(pl.multiple_of(part * span, span), span)]
            remote(here, here, c_send, c_recv.at[part - 4], sibling).wait_recv()

        take(part)
        return 0

    lax.fori_loop(0, 8, step_over, 0)

    partial = total[...]
    largest = jnp.max(jnp.abs(partial), axis=-1, keepdims=True)
    largest = jnp.maximum(largest, 1e-30)
    coded[...] = jnp.round(partial * (32760.0 / largest)).astype(jnp.int32).astype(jnp.int16)
    spread_range = jnp.broadcast_to(largest * (1.0 / 32760.0), (rows_dev, 128))
    ranges[...] = spread_range.T[0:8, :]

    def quarter(dx, h):
        start = (x + dx) % SIDE * own_rows + h * half
        return pl.ds(pl.multiple_of(start, half), half)

    def copy_r(dx):
        return remote(ranges, ranges_in.at[dx - 1], r_send, r_recv, across(dx))

    def copy_p(dx, h):
        return remote(
            coded.at[quarter(dx, h)], coded_in.at[h, dx - 1], p_send, p_recv.at[h], across(dx)
        )

    for dx in RING:
        copy_p(dx, 0).start()
    for dx in RING:
        copy_r(dx).start()
    for dx in RING:
        copy_p(dx, 1).start()

    def spot(h, core, chip_x):
        start = (h * CORES + core) * SIDE * half + chip_x * half
        return pl.ds(pl.multiple_of(start, half), half)

    def copy_g(dx, h):
        at = h * SIDE + dx
        here = everyone.at[spot(h, 0, x)]
        return remote(here, here, g_send, g_recv.at[at], across(dx))

    def copy_s(dx, h):
        from_x = (x + SIDE - dx) % SIDE
        return remote(
            everyone.at[spot(h, 0, from_x)], everyone.at[spot(h, 1, from_x)], s_send,
            s_recv.at[h], sibling,
        )

    def sibling_rows(h):
        start = (h * CORES + 1) * SIDE * half
        here = everyone.at[pl.ds(start, SIDE * half)]
        return remote(here, here, s_send, s_recv.at[h], sibling)

    sums = []
    for h in range(2):
        kept = db_ref[quarter(0, h), :].astype(jnp.float32)
        sums.append(kept * inverse_norm(kept) + total[quarter(0, h), :])
    remote(ranges_in, ranges_in, r_send, r_recv, sibling).wait_recv()
    for dx in RING:
        across_range = jnp.broadcast_to(ranges_in[dx - 1, 0:1, :], (128, rows_dev))
        ranges_of[dx - 1] = across_range.T

    for h in range(2):
        summed = sums[h]
        here = coded_in.at[h]
        remote(here, here, p_send, p_recv.at[h], sibling).wait_recv()
        for dx in RING:
            part = coded_in[h, dx - 1].astype(jnp.float32)
            summed = summed + part * ranges_of[dx - 1, quarter(0, h), 0:1]
        everyone[spot(h, 0, x), :] = (summed * inverse_norm(summed)).astype(jnp.bfloat16)
        for dx in RING:
            copy_g(dx, h).start()
        copy_s(0, h).start()

    def hand_over(h):
        for dx in RING:
            copy_g(dx, h).wait_recv()
            copy_s(dx, h).start()

    hand_over(0)
    for load in query_loads:
        load.wait()
    sibling_rows(0).wait_recv()

    share = queries_here // CHIPS
    lines = share // 128
    part_rows = CORES * SIDE * half

    def chip_at(k):
        return (x, (chip + k) % CHIPS * CORES + c)

    def copy_m(k):
        return remote(tops.at[k], rivals.at[k], m_send, m_recv, chip_at(k))

    def folded_scores(h, k):
        owner = (chip + k) % CHIPS
        panel = q_v[pl.ds(pl.multiple_of(owner * share, share), share), :]
        scores = dot_rows(everyone[pl.ds(h * part_rows, part_rows), :], panel)
        return jnp.max(scores.reshape(part_rows // 8, 8, share), axis=0)

    unroll = 4

    def score_first(i, _):
        for u in range(unroll):
            k = (i * unroll + u + 1) % CHIPS
            first_top[k] = folded_scores(0, k)
        return 0

    def score_second(i, _):
        for u in range(unroll):
            k = (i * unroll + u + 1) % CHIPS
            top = jnp.maximum(first_top[k], folded_scores(1, k))
            top = jnp.max(top, axis=0, keepdims=True)
            for line in range(lines):
                tops[k, pl.ds(line, 1), :] = top[:, line * 128 : (line + 1) * 128]
        for u in range(unroll - 1):
            copy_m(i * unroll + u + 1).start()

        @pl.when(i < CHIPS // unroll - 1)
        def _():
            copy_m((i + 1) * unroll).start()

        return 0

    lax.fori_loop(0, 1, score_first, 0)
    hand_over(1)
    lax.fori_loop(1, CHIPS // unroll, score_first, 0)
    sibling_rows(1).wait_recv()
    lax.fori_loop(0, CHIPS // unroll, score_second, 0)

    for chip_x in range(SIDE):
        for h in range(2):
            start = h * part_rows + chip_x * half
            aug_ref[pl.ds(chip_x * own_rows + h * half, half), :] = everyone[pl.ds(start, half), :]
    others = pl.ds(1, CHIPS - 1)
    remote(tops.at[others], rivals.at[others], m_send, m_recv, sibling).wait_recv()
    best = tops[0]
    for k in range(1, CHIPS):
        best = jnp.maximum(best, rivals[k])
    here = c * CHIPS + chip
    best_ref[here] = best
    devices = CHIPS * CORES

    def copy_f(k):
        return remote(
            best_ref.at[here], best_ref.at[here], f_send, f_recv, (x, (d + k) % devices)
        )

    for k in range(1, devices):
        copy_f(k).start()

    def sent(ref, sem):
        remote(ref, ref, sem, sem, sibling).wait_send()

    sent(pool.at[pl.ds(0, 2 * (CHIPS - 1) * half)], ab_send)
    sent(pool.at[pl.ds(0, parity_rows)], c_send)
    sent(ranges_in, r_send)
    sent(coded_in, p_send)
    sent(everyone.at[pl.ds(0, 6 * half)], g_send)
    sent(everyone.at[pl.ds(0, 8 * half)], s_send)
    sent(tops.at[others], m_send)
    arrived = best_ref.at[pl.ds(0, devices - 1)]
    remote(arrived, arrived, f_send, f_recv, sibling).wait()


def deliver(rows_in, best_in, rows_out, best_out):
    rows_out[...] = rows_in[...]
    best_out[...] = best_in[...]


def local(database, neighbours, valid_count, queries):
    rows_dev, features = database.shape
    fanout = neighbours.shape[1]
    queries_here = queries.shape[0] // CORES
    own_rows = rows_dev // SIDE
    pool_rows = rows_dev * CHIPS * CORES // SIDE
    share = queries_here // CHIPS
    vmem = pl.BlockSpec(memory_space=pltpu.VMEM)
    anywhere = pl.BlockSpec(memory_space=pl.ANY)
    dma = pltpu.SemaphoreType.DMA
    augmented, best = pl.pallas_call(
        kernel,
        out_shape=(
            jax.ShapeDtypeStruct((rows_dev, features), jnp.bfloat16),
            jax.ShapeDtypeStruct((CORES * CHIPS, share // 128, 128), jnp.float32),
        ),
        in_specs=[anywhere, anywhere, anywhere, anywhere],
        out_specs=(vmem, vmem),
        scratch_shapes=[
            pltpu.VMEM((queries_here, features), jnp.bfloat16),
            pltpu.VMEM((rows_dev, features), jnp.bfloat16),
            pltpu.VMEM((fanout, rows_dev), jnp.int32),
            pltpu.VMEM((1, rows_dev), jnp.int32),
            pltpu.VMEM((pool_rows, features), jnp.bfloat16),
            pltpu.VMEM((8, rows_dev, pool_rows // 8), jnp.bfloat16),
            pltpu.VMEM((fanout, rows_dev), jnp.int32),
            pltpu.VMEM((rows_dev, features), jnp.float32),
            pltpu.VMEM((rows_dev, features), jnp.int16),
            pltpu.VMEM((2, SIDE - 1, own_rows // 2, features), jnp.int16),
            pltpu.VMEM((8, rows_dev), jnp.float32),
            pltpu.VMEM((SIDE - 1, 8, rows_dev), jnp.float32),
            pltpu.VMEM((SIDE - 1, rows_dev, 128), jnp.float32),
            pltpu.VMEM((CORES * rows_dev, features), jnp.bfloat16),
            pltpu.VMEM((CHIPS, 8, share), jnp.float32),
            pltpu.VMEM((CHIPS, share // 128, 128), jnp.float32),
            pltpu.VMEM((CHIPS, share // 128, 128), jnp.float32),
            pltpu.SMEM((CHIPS * CORES,), jnp.int32),
            dma((4,)),
            dma((4,)),
        ]
        + [dma((CHIPS,))] * 2
        + [dma((4,)), dma((2,)), dma((2 * SIDE,)), dma((2,))]
        + [dma] * 11,
        compiler_params=pltpu.CompilerParams(
            collective_id=0, has_side_effects=True, vmem_limit_bytes=56 * 2**20
        ),
        name="expand_and_score",
    )(database, neighbours.T, valid_count.reshape(1, rows_dev), queries)
    augmented, best = pl.pallas_call(
        deliver,
        out_shape=(
            jax.ShapeDtypeStruct(augmented.shape, augmented.dtype),
            jax.ShapeDtypeStruct(best.shape, best.dtype),
        ),
        in_specs=[vmem, vmem],
        out_specs=(vmem, vmem),
        name="deliver",
    )(augmented, best)
    return augmented, best.reshape(queries.shape[0])


def solution(mesh):
    return jax.shard_map(
        local,
        mesh=mesh,
        in_specs=(P("db", None), P("db", None), P("db"), P("pb", None)),
        out_specs=(P("db", None), P("pb")),
        check_vma=False,
    )
```

```python
import functools

import jax
import jax.numpy as jnp
from jax import lax
from jax.experimental import pallas as pl
from jax.experimental.pallas import tpu as pltpu
from jax.sharding import PartitionSpec as P

epsilon = 1e-06
MESH = pl.DeviceIdType.MESH
SIDE = 4
CORES = 2
CHIPS = SIDE * SIDE
SLOTS = (
    (0, 0), (0, 1), (0, 3), (1, 0), (3, 0), (0, 2), (2, 0), (1, 1),
    (1, 3), (3, 1), (3, 3), (1, 2), (2, 1), (3, 2), (2, 3), (2, 2),
)
SLOT_AT = {offset: place for place, offset in enumerate(SLOTS)}
RING = (1, 3, 2)


def inverse_norm(values):
    return lax.rsqrt(jnp.sum(values * values, axis=-1, keepdims=True) + epsilon)


def dot_rows(left, right):
    return lax.dot_general(
        left, right, (((1,), (1,)), ((), ())), preferred_element_type=jnp.float32
    )


def kernel(
    db_hbm, nb_hbm, vc_hbm, q_ref, aug_ref, best_ref,
    q_v, db_ref, nb_ref, vc_ref, pool, mask_ref, wanted, total, coded, coded_in, ranges, ranges_in, ranges_of,
    everyone, first_top, tops, y_in, y_best, z_in, bases,
    q_sem, l_sem, a_recv, b_recv, c_recv, p_send, p_recv, g_recv, s_recv, y_recv, z_recv, ab_send,
    c_send, r_send, r_recv, g_send, s_send, y_send, z_send, f_send, f_recv,
):
    rows_dev, features = db_ref.shape
    fanout = nb_ref.shape[0]
    own_rows = rows_dev // SIDE
    half = own_rows // 2
    parity_rows = CHIPS * own_rows
    span = 4 * own_rows
    x = lax.axis_index("pb")
    d = lax.axis_index("db")
    c = d % CORES
    chip = d // CORES
    y = chip % SIDE
    z = chip // SIDE
    mine = pl.multiple_of(x * own_rows, own_rows)

    def plane(dz, dy):
        return (x, ((z + dz) % SIDE * SIDE + (y + dy) % SIDE) * CORES + c)

    sibling = (x, chip * CORES + (1 - c))

    def across(dx):
        return ((x + dx) % SIDE, d)

    def remote(src, dst, send, recv, to):
        return pltpu.make_async_remote_copy(
            src_ref=src, dst_ref=dst, send_sem=send, recv_sem=recv, device_id=to,
            device_id_type=MESH,
        )

    loads = [
        pltpu.make_async_copy(
            db_hbm.at[pl.ds(mine, own_rows)], pool.at[pl.ds(0, own_rows)], l_sem.at[0]
        ),
        pltpu.make_async_copy(nb_hbm, nb_ref, l_sem.at[1]),
        pltpu.make_async_copy(vc_hbm, vc_ref, l_sem.at[2]),
        pltpu.make_async_copy(db_hbm, db_ref, l_sem.at[3]),
    ]
    loads[0].start()

    barrier = pltpu.get_barrier_semaphore()
    partners = [plane(0, step) for step in RING] + [plane(step, 0) for step in RING]
    partners += [sibling] + [across(step) for step in RING]
    for partner in partners:
        pl.semaphore_signal(barrier, inc=1, device_id=partner, device_id_type=MESH)

    for load in loads[1:]:
        load.start()

    loads[0].wait()
    pl.semaphore_wait(barrier, len(partners))

    def block(place, core, start, rows):
        return pool.at[pl.ds(core * parity_rows + place * own_rows + start, rows)]

    def copy_a(dz, dy):
        src = SLOT_AT[(0, dy if dz else 0)]
        dst = SLOT_AT[(dz, dy)]
        to = plane(dz, 0) if dz else plane(0, dy)
        return remote(
            block(src, 0, 0, half), block(dst, 0, 0, half), ab_send, a_recv.at[dst], to
        )

    def copy_b(dz, dy):
        src = SLOT_AT[(dz if dy else 0, 0)]
        dst = SLOT_AT[(dz, dy)]
        to = plane(0, dy) if dy else plane(dz, 0)
        return remote(
            block(src, 0, half, half), block(dst, 0, half, half), ab_send,
            (a_recv if dz and dy else b_recv).at[dst], to,
        )

    def copy_c(place):
        return remote(
            block(place, 0, 0, own_rows), block(place, 1, 0, own_rows), c_send,
            c_recv.at[place // 4], sibling,
        )

    for step in RING:
        copy_a(0, step).start()
        copy_b(step, 0).start()
    copy_c(0).start()
    for step in RING:
        copy_a(step, 0).start()
        copy_b(0, step).start()

    queries_here = q_v.shape[0]
    piece = queries_here // 4
    query_loads = [
        pltpu.make_async_copy(
            q_ref.at[pl.ds(pl.multiple_of(c * queries_here + k * piece, piece), piece)],
            q_v.at[pl.ds(k * piece, piece)],
            q_sem.at[k],
        )
        for k in range(4)
    ]
    for load in query_loads:
        load.start()
    for load in loads[1:]:
        load.wait()

    place_of = lax.broadcasted_iota(jnp.int32, (fanout, rows_dev), 0)
    wanted[...] = jnp.where(place_of < vc_ref[...], nb_ref[...], -1)
    for place, (dz, dy) in enumerate(SLOTS):
        for core in range(CORES):
            owner = ((z - dz) % SIDE * SIDE + (y - dy) % SIDE) * CORES + (c + core) % CORES
            bases[core * CHIPS + place] = owner * rows_dev + x * own_rows

    def build_mask(part):
        for u in range(2):
            counts = []
            for v in range(2):
                base = bases[part * 4 + u * 2 + v]
                number = base + lax.broadcasted_iota(jnp.int32, (own_rows, rows_dev), 0)
                count = jnp.zeros((own_rows, rows_dev), jnp.float32)
                for k in range(fanout):
                    count = count + jnp.where(wanted[pl.ds(k, 1), :] == number, 1.0, 0.0)
                counts.append(count)
            both = jnp.concatenate(counts, axis=0)
            mask_ref[part, :, pl.ds(u * 2 * own_rows, 2 * own_rows)] = both.T.astype(jnp.bfloat16)

    def first_masks(i, _):
        build_mask(4 * i)
        return 0

    def other_masks(i, _):
        build_mask(i + 1 + i // 3)
        return 0

    lax.fori_loop(0, 2, first_masks, 0)

    for step in RING:
        copy_a(0, step).wait_recv()
        for far in RING:
            copy_a(far, step).start()
        copy_b(step, 0).wait_recv()
        for far in RING:
            copy_b(step, far).start()

    lax.fori_loop(0, 6, other_masks, 0)

    for step in RING:
        copy_b(0, step).wait_recv()
        copy_c(SLOT_AT[(0, step)]).start()
        copy_a(step, 0).wait_recv()
        copy_c(SLOT_AT[(step, 0)]).start()

    def pass_on(place):
        here = block(place, 0, 0, own_rows)
        remote(here, here, ab_send, a_recv.at[place], sibling).wait_recv()
        copy_c(place).start()

    total[...] = jnp.zeros_like(total)
    own = db_ref[...]
    own_inverse = inverse_norm(own.astype(jnp.float32))

    def take(g):
        rows = pool[pl.ds(pl.multiple_of(g * span, span), span), :]
        squares = rows.astype(jnp.float32)
        squares = squares * squares
        folded = squares[:, 0:128]
        for k in range(1, features // 128):
            folded = folded + squares[:, k * 128 : (k + 1) * 128]
        far_inverse = lax.rsqrt(jnp.sum(folded.T, axis=0, keepdims=True) + epsilon)
        cosine = dot_rows(own, rows) * own_inverse * far_inverse
        halfway = (1.0 + cosine) * 0.5
        weight = halfway * halfway * halfway
        coefficient = (weight * far_inverse).astype(jnp.bfloat16).astype(jnp.float32)
        count = mask_ref[g].astype(jnp.float32)
        spread = jnp.where(count > 0.0, count * coefficient, 0.0)
        total[...] += jnp.dot(
            spread.astype(jnp.bfloat16), rows, preferred_element_type=jnp.float32
        )

    def step_over(i, _):
        part = jnp.where(i < 4, i // 2 + i % 2 * 4, jnp.where(i < 6, i - 2, i))

        @pl.when(i == 2)
        def _():
            pass_on(7)

        @pl.when((i == 4) | (i == 5))
        def _():
            for u in range(4):
                pass_on(part * 4 + u)

        @pl.when(part >= 4)
        def _():
            here = pool.at[pl.ds(pl.multiple_of(part * span, span), span)]
            remote(here, here, c_send, c_recv.at[part - 4], sibling).wait_recv()

        take(part)
        return 0

    lax.fori_loop(0, 8, step_over, 0)

    partial = total[...]
    largest = jnp.max(jnp.abs(partial), axis=-1, keepdims=True)
    largest = jnp.maximum(largest, 1e-30)
    coded[...] = jnp.round(partial * (32760.0 / largest)).astype(jnp.int32).astype(jnp.int16)
    spread_range = jnp.broadcast_to(largest * (1.0 / 32760.0), (rows_dev, 128))
    ranges[...] = spread_range.T[0:8, :]

    def quarter(dx, h):
        start = (x + dx) % SIDE * own_rows + h * half
        return pl.ds(pl.multiple_of(start, half), half)

    def copy_r(dx):
        return remote(ranges, ranges_in.at[dx - 1], r_send, r_recv, across(dx))

    def copy_p(dx, h):
        return remote(
            coded.at[quarter(dx, h)], coded_in.at[h, dx - 1], p_send.at[h], p_recv.at[h], across(dx)
        )

    def sent(ref, sem):
        remote(ref, ref, sem, sem, sibling).wait_send()

    for dx in RING:
        copy_p(dx, 0).start()
    for dx in RING:
        copy_r(dx).start()
    sent(coded_in.at[0], p_send.at[0])
    for dx in RING:
        copy_p(dx, 1).start()

    def spot(h, core, chip_x):
        start = (h * CORES + core) * SIDE * half + chip_x * half
        return pl.ds(pl.multiple_of(start, half), half)

    def copy_g(dx, h):
        at = h * SIDE + dx
        here = everyone.at[spot(h, 0, x)]
        return remote(here, here, g_send, g_recv.at[at], across(dx))

    def copy_s(h):
        rows = SIDE * half
        start = h * CORES * rows
        return remote(
            everyone.at[pl.ds(start, rows)], everyone.at[pl.ds(start + rows, rows)], s_send,
            s_recv.at[h], sibling,
        )

    sums = []
    for h in range(2):
        kept = db_ref[quarter(0, h), :].astype(jnp.float32)
        sums.append(kept * inverse_norm(kept) + total[quarter(0, h), :])
    remote(ranges_in, ranges_in, r_send, r_recv, sibling).wait_recv()
    for dx in RING:
        across_range = jnp.broadcast_to(ranges_in[dx - 1, 0:1, :], (128, rows_dev))
        ranges_of[dx - 1] = across_range.T

    for h in range(2):
        summed = sums[h]
        here = coded_in.at[h]
        remote(here, here, p_send.at[h], p_recv.at[h], sibling).wait_recv()
        for dx in RING:
            part = coded_in[h, dx - 1].astype(jnp.float32)
            summed = summed + part * ranges_of[dx - 1, quarter(0, h), 0:1]
        everyone[spot(h, 0, x), :] = (summed * inverse_norm(summed)).astype(jnp.bfloat16)
        for dx in RING:
            copy_g(dx, h).start()

    def hand_over(h):
        for dx in RING:
            copy_g(dx, h).wait_recv()
        copy_s(h).start()

    hand_over(0)
    for load in query_loads:
        load.wait()
    copy_s(0).wait_recv()

    shares = tops.shape[0]
    share = queries_here // shares
    lines = share // 128
    part_rows = CORES * SIDE * half

    def folded_scores(h, k):
        panel = q_v[pl.ds(k * share, share), :]
        scores = dot_rows(everyone[pl.ds(h * part_rows, part_rows), :], panel)
        return jnp.max(scores.reshape(part_rows // 8, 8, share), axis=0)

    def score_first(begin, end):
        for k in range(begin, end):
            first_top[k] = folded_scores(0, k)

    def score_second(begin, end):
        for k in range(begin, end):
            top = jnp.maximum(first_top[k], folded_scores(1, k))
            top = jnp.max(top, axis=0, keepdims=True)
            for line in range(lines):
                tops[k, pl.ds(line, 1), :] = top[:, line * 128 : (line + 1) * 128]

    bounds = (0, shares * 3 // 4, shares)
    spans = [pl.ds(begin, end - begin) for begin, end in zip(bounds[:-1], bounds[1:])]

    def copy_y(i, n):
        return remote(
            tops.at[spans[n]], y_in.at[i, spans[n]], y_send, y_recv.at[n], plane(0, RING[i])
        )

    def copy_z(i, n):
        return remote(
            y_best.at[spans[n]], z_in.at[i, spans[n]], z_send, z_recv.at[n], plane(RING[i], 0)
        )

    def arrived(buffer, n, sem):
        here = buffer.at[:, spans[n]]
        remote(here, here, y_send, sem.at[n], sibling).wait_recv()

    score_first(0, shares // 4)
    hand_over(1)
    score_first(shares // 4, shares)
    copy_s(1).wait_recv()
    for n in range(2):
        score_second(bounds[n], bounds[n + 1])
        for i in range(SIDE - 1):
            copy_y(i, n).start()

    for chip_x in range(SIDE):
        for h in range(2):
            start = h * part_rows + chip_x * half
            aug_ref[pl.ds(chip_x * own_rows + h * half, half), :] = everyone[pl.ds(start, half), :]

    for n in range(2):
        arrived(y_in, n, y_recv)
        best = tops[spans[n]]
        for i in range(SIDE - 1):
            best = jnp.maximum(best, y_in[i, spans[n]])
        y_best[spans[n]] = best
        for i in range(SIDE - 1):
            copy_z(i, n).start()
    for n in range(2):
        arrived(z_in, n, z_recv)
        best = y_best[spans[n]]
        for i in range(SIDE - 1):
            best = jnp.maximum(best, z_in[i, spans[n]])
        here = pl.ds(pl.multiple_of(c * shares, shares) + bounds[n], bounds[n + 1] - bounds[n])
        best_ref[here] = best
        remote(best_ref.at[here], best_ref.at[here], f_send, f_recv, sibling).start()

    sent(pool.at[pl.ds(0, 2 * (CHIPS - 1) * half)], ab_send)
    sent(pool.at[pl.ds(0, parity_rows)], c_send)
    sent(ranges_in, r_send)
    sent(coded_in.at[1], p_send.at[1])
    sent(everyone.at[pl.ds(0, 6 * half)], g_send)
    sent(everyone.at[pl.ds(0, 8 * half)], s_send)
    sent(y_in, y_send)
    sent(z_in, z_send)
    here = best_ref.at[pl.ds(0, shares)]
    remote(here, here, f_send, f_recv, sibling).wait()


def deliver(rows_in, best_in, rows_out, best_out):
    rows_out[...] = rows_in[...]
    best_out[...] = best_in[...]


def local(database, neighbours, valid_count, queries):
    rows_dev, features = database.shape
    fanout = neighbours.shape[1]
    queries_here = queries.shape[0] // CORES
    own_rows = rows_dev // SIDE
    pool_rows = rows_dev * CHIPS * CORES // SIDE
    share = queries_here // CHIPS
    vmem = pl.BlockSpec(memory_space=pltpu.VMEM)
    anywhere = pl.BlockSpec(memory_space=pl.ANY)
    dma = pltpu.SemaphoreType.DMA
    augmented, best = pl.pallas_call(
        kernel,
        out_shape=(
            jax.ShapeDtypeStruct((rows_dev, features), jnp.bfloat16),
            jax.ShapeDtypeStruct((CORES * CHIPS, share // 128, 128), jnp.float32),
        ),
        in_specs=[anywhere, anywhere, anywhere, anywhere],
        out_specs=(vmem, vmem),
        scratch_shapes=[
            pltpu.VMEM((queries_here, features), jnp.bfloat16),
            pltpu.VMEM((rows_dev, features), jnp.bfloat16),
            pltpu.VMEM((fanout, rows_dev), jnp.int32),
            pltpu.VMEM((1, rows_dev), jnp.int32),
            pltpu.VMEM((pool_rows, features), jnp.bfloat16),
            pltpu.VMEM((8, rows_dev, pool_rows // 8), jnp.bfloat16),
            pltpu.VMEM((fanout, rows_dev), jnp.int32),
            pltpu.VMEM((rows_dev, features), jnp.float32),
            pltpu.VMEM((rows_dev, features), jnp.int16),
            pltpu.VMEM((2, SIDE - 1, own_rows // 2, features), jnp.int16),
            pltpu.VMEM((8, rows_dev), jnp.float32),
            pltpu.VMEM((SIDE - 1, 8, rows_dev), jnp.float32),
            pltpu.VMEM((SIDE - 1, rows_dev, 128), jnp.float32),
            pltpu.VMEM((CORES * rows_dev, features), jnp.bfloat16),
            pltpu.VMEM((CHIPS, 8, share), jnp.float32),
            pltpu.VMEM((CHIPS, share // 128, 128), jnp.float32),
            pltpu.VMEM((SIDE - 1, CHIPS, share // 128, 128), jnp.float32),
            pltpu.VMEM((CHIPS, share // 128, 128), jnp.float32),
            pltpu.VMEM((SIDE - 1, CHIPS, share // 128, 128), jnp.float32),
            pltpu.SMEM((CHIPS * CORES,), jnp.int32),
            dma((4,)),
            dma((4,)),
        ]
        + [dma((CHIPS,))] * 2
        + [dma((4,)), dma((2,)), dma((2,)), dma((2 * SIDE,)), dma((2,)), dma((2,)), dma((2,))]
        + [dma] * 10,
        compiler_params=pltpu.CompilerParams(
            collective_id=0, has_side_effects=True, vmem_limit_bytes=56 * 2**20
        ),
        name="expand_and_score",
    )(database, neighbours.T, valid_count.reshape(1, rows_dev), queries)
    augmented, best = pl.pallas_call(
        deliver,
        out_shape=(
            jax.ShapeDtypeStruct(augmented.shape, augmented.dtype),
            jax.ShapeDtypeStruct(best.shape, best.dtype),
        ),
        in_specs=[vmem, vmem],
        out_specs=(vmem, vmem),
        name="deliver",
    )(augmented, best)
    return augmented, best.reshape(queries.shape[0])


def solution(mesh):
    return jax.shard_map(
        local,
        mesh=mesh,
        in_specs=(P("db", None), P("db", None), P("db"), P("pb", None)),
        out_specs=(P("db", None), P("pb")),
        check_vma=False,
    )
```

```python
import functools

import jax
import jax.numpy as jnp
from jax import lax
from jax.experimental import pallas as pl
from jax.experimental.pallas import tpu as pltpu
from jax.sharding import PartitionSpec as P

epsilon = 1e-06
MESH = pl.DeviceIdType.MESH
SIDE = 4
CORES = 2
CHIPS = SIDE * SIDE
SLOTS = (
    (0, 0), (0, 1), (0, 3), (1, 0), (3, 0), (0, 2), (2, 0), (1, 1),
    (1, 3), (3, 1), (3, 3), (1, 2), (2, 1), (3, 2), (2, 3), (2, 2),
)
SLOT_AT = {offset: place for place, offset in enumerate(SLOTS)}
RING = (1, 3, 2)


def inverse_norm(values):
    return lax.rsqrt(jnp.sum(values * values, axis=-1, keepdims=True) + epsilon)


def dot_rows(left, right):
    return lax.dot_general(
        left, right, (((1,), (1,)), ((), ())), preferred_element_type=jnp.float32
    )


def kernel(
    db_hbm, nb_hbm, vc_hbm, q_ref, aug_ref, best_ref,
    q_v, q_t, db_ref, nb_ref, vc_ref, pool, mask_ref, wanted, total, coded, coded_in, ranges, ranges_in, ranges_of,
    everyone, first_top, tops, y_in, y_best, z_in, bases,
    q_sem, l_sem, a_recv, b_recv, c_recv, p_send, p_recv, g_recv, s_recv, y_recv, z_recv, ab_send,
    c_send, r_send, r_recv, g_send, s_send, y_send, z_send, f_send, f_recv,
):
    rows_dev, features = db_ref.shape
    fanout = nb_ref.shape[0]
    own_rows = rows_dev // SIDE
    half = own_rows // 2
    parity_rows = CHIPS * own_rows
    span = 4 * own_rows
    x = lax.axis_index("pb")
    d = lax.axis_index("db")
    c = d % CORES
    chip = d // CORES
    y = chip % SIDE
    z = chip // SIDE
    mine = pl.multiple_of(x * own_rows, own_rows)

    def plane(dz, dy):
        return (x, ((z + dz) % SIDE * SIDE + (y + dy) % SIDE) * CORES + c)

    sibling = (x, chip * CORES + (1 - c))

    def across(dx):
        return ((x + dx) % SIDE, d)

    def remote(src, dst, send, recv, to):
        return pltpu.make_async_remote_copy(
            src_ref=src, dst_ref=dst, send_sem=send, recv_sem=recv, device_id=to,
            device_id_type=MESH,
        )

    loads = [
        pltpu.make_async_copy(
            db_hbm.at[pl.ds(mine, own_rows)], pool.at[pl.ds(0, own_rows)], l_sem.at[0]
        ),
        pltpu.make_async_copy(nb_hbm, nb_ref, l_sem.at[1]),
        pltpu.make_async_copy(vc_hbm, vc_ref, l_sem.at[2]),
        pltpu.make_async_copy(db_hbm, db_ref, l_sem.at[3]),
    ]
    loads[0].start()

    barrier = pltpu.get_barrier_semaphore()
    partners = [plane(0, step) for step in RING] + [plane(step, 0) for step in RING]
    partners += [sibling] + [across(step) for step in RING]
    for partner in partners:
        pl.semaphore_signal(barrier, inc=1, device_id=partner, device_id_type=MESH)

    for load in loads[1:]:
        load.start()

    loads[0].wait()
    pl.semaphore_wait(barrier, len(partners))

    def block(place, core, start, rows):
        return pool.at[pl.ds(core * parity_rows + place * own_rows + start, rows)]

    def copy_a(dz, dy):
        src = SLOT_AT[(0, dy if dz else 0)]
        dst = SLOT_AT[(dz, dy)]
        to = plane(dz, 0) if dz else plane(0, dy)
        return remote(
            block(src, 0, 0, half), block(dst, 0, 0, half), ab_send, a_recv.at[dst], to
        )

    def copy_b(dz, dy):
        src = SLOT_AT[(dz if dy else 0, 0)]
        dst = SLOT_AT[(dz, dy)]
        to = plane(0, dy) if dy else plane(dz, 0)
        return remote(
            block(src, 0, half, half), block(dst, 0, half, half), ab_send,
            (a_recv if dz and dy else b_recv).at[dst], to,
        )

    def copy_c(place):
        return remote(
            block(place, 0, 0, own_rows), block(place, 1, 0, own_rows), c_send,
            c_recv.at[place // 4], sibling,
        )

    for step in RING:
        copy_a(0, step).start()
        copy_b(step, 0).start()
    copy_c(0).start()
    for step in RING:
        copy_a(step, 0).start()
        copy_b(0, step).start()

    queries_here = q_v.shape[0]
    piece = queries_here // 4
    query_loads = [
        pltpu.make_async_copy(
            q_ref.at[pl.ds(pl.multiple_of(c * queries_here + k * piece, piece), piece)],
            q_v.at[pl.ds(k * piece, piece)],
            q_sem.at[k],
        )
        for k in range(4)
    ]
    for load in query_loads:
        load.start()
    for load in loads[1:]:
        load.wait()

    place_of = lax.broadcasted_iota(jnp.int32, (fanout, rows_dev), 0)
    wanted[...] = jnp.where(place_of < vc_ref[...], nb_ref[...], -1)
    for place, (dz, dy) in enumerate(SLOTS):
        for core in range(CORES):
            owner = ((z - dz) % SIDE * SIDE + (y - dy) % SIDE) * CORES + (c + core) % CORES
            bases[core * CHIPS + place] = owner * rows_dev + x * own_rows

    def build_mask(part):
        for u in range(2):
            counts = []
            for v in range(2):
                base = bases[part * 4 + u * 2 + v]
                number = base + lax.broadcasted_iota(jnp.int32, (own_rows, rows_dev), 0)
                count = jnp.zeros((own_rows, rows_dev), jnp.float32)
                for k in range(fanout):
                    count = count + jnp.where(wanted[pl.ds(k, 1), :] == number, 1.0, 0.0)
                counts.append(count)
            both = jnp.concatenate(counts, axis=0)
            mask_ref[part, :, pl.ds(u * 2 * own_rows, 2 * own_rows)] = both.T.astype(jnp.bfloat16)

    def first_masks(i, _):
        build_mask(4 * i)
        return 0

    def other_masks(i, _):
        build_mask(i + 1 + i // 3)
        return 0

    lax.fori_loop(0, 2, first_masks, 0)

    for step in RING:
        copy_a(0, step).wait_recv()
        for far in RING:
            copy_a(far, step).start()
        copy_b(step, 0).wait_recv()
        for far in RING:
            copy_b(step, far).start()

    lax.fori_loop(0, 6, other_masks, 0)

    for step in RING:
        copy_b(0, step).wait_recv()
        copy_c(SLOT_AT[(0, step)]).start()
        copy_a(step, 0).wait_recv()
        copy_c(SLOT_AT[(step, 0)]).start()

    def pass_on(place):
        here = block(place, 0, 0, own_rows)
        remote(here, here, ab_send, a_recv.at[place], sibling).wait_recv()
        copy_c(place).start()

    total[...] = jnp.zeros_like(total)
    own = db_ref[...]
    own_inverse = inverse_norm(own.astype(jnp.float32))

    def take(g):
        rows = pool[pl.ds(pl.multiple_of(g * span, span), span), :]
        squares = rows.astype(jnp.float32)
        squares = squares * squares
        folded = squares[:, 0:128]
        for k in range(1, features // 128):
            folded = folded + squares[:, k * 128 : (k + 1) * 128]
        far_inverse = lax.rsqrt(jnp.sum(folded.T, axis=0, keepdims=True) + epsilon)
        cosine = dot_rows(own, rows) * own_inverse * far_inverse
        halfway = (1.0 + cosine) * 0.5
        weight = halfway * halfway * halfway
        coefficient = (weight * far_inverse).astype(jnp.bfloat16).astype(jnp.float32)
        count = mask_ref[g].astype(jnp.float32)
        spread = jnp.where(count > 0.0, count * coefficient, 0.0)
        total[...] += jnp.dot(
            spread.astype(jnp.bfloat16), rows, preferred_element_type=jnp.float32
        )

    def step_over(i, _):
        part = jnp.where(i < 4, i // 2 + i % 2 * 4, jnp.where(i < 6, i - 2, i))

        @pl.when(i == 2)
        def _():
            pass_on(7)

        @pl.when((i == 4) | (i == 5))
        def _():
            for u in range(4):
                pass_on(part * 4 + u)

        @pl.when(part >= 4)
        def _():
            here = pool.at[pl.ds(pl.multiple_of(part * span, span), span)]
            remote(here, here, c_send, c_recv.at[part - 4], sibling).wait_recv()

        take(part)
        return 0

    lax.fori_loop(0, 8, step_over, 0)

    partial = total[...]
    largest = jnp.max(jnp.abs(partial), axis=-1, keepdims=True)
    largest = jnp.maximum(largest, 1e-30)
    coded[...] = jnp.round(partial * (32760.0 / largest)).astype(jnp.int32).astype(jnp.int16)
    spread_range = jnp.broadcast_to(largest * (1.0 / 32760.0), (rows_dev, 128))
    ranges[...] = spread_range.T[0:8, :]

    def quarter(dx, h):
        start = (x + SIDE + dx) % SIDE * own_rows + h * half
        return pl.ds(pl.multiple_of(start, half), half)

    def copy_r(dx):
        return remote(ranges, ranges_in.at[dx - 1], r_send, r_recv, across(dx))

    def copy_p(dx, h):
        return remote(
            coded.at[quarter(dx, h)], coded_in.at[h, dx - 1], p_send.at[h], p_recv.at[h], across(dx)
        )

    def sent(ref, sem):
        remote(ref, ref, sem, sem, sibling).wait_send()

    for dx in RING:
        copy_p(dx, 0).start()
    for dx in RING:
        copy_r(dx).start()
    for load in query_loads:
        load.wait()
    panel_rows = 512

    def turn(i, _):
        for u in range(4):
            rows = pl.ds(pl.multiple_of((i * 4 + u) * panel_rows, panel_rows), panel_rows)
            q_t[:, rows] = q_v[rows, :].T
        return 0

    turns = queries_here // (4 * panel_rows)
    lax.fori_loop(0, turns // 2, turn, 0)
    sent(coded_in.at[0], p_send.at[0])
    for dx in RING:
        copy_p(dx, 1).start()
    lax.fori_loop(turns // 2, turns, turn, 0)

    others = (SIDE - 1) * half
    starts = (0, 2 * own_rows, 2 * own_rows + 2 * others)
    sizes = (own_rows, others, others)

    def copy_g(i, h):
        return remote(
            everyone.at[pl.ds(h * half, half)], everyone.at[pl.ds(starts[1 + h] + i * half, half)],
            g_send, g_recv.at[h], across(RING[i]),
        )

    def copy_s(n):
        return remote(
            everyone.at[pl.ds(starts[n], sizes[n])],
            everyone.at[pl.ds(starts[n] + sizes[n], sizes[n])], s_send, s_recv.at[n], sibling,
        )

    sums = []
    for h in range(2):
        kept = db_ref[quarter(0, h), :].astype(jnp.float32)
        sums.append(kept * inverse_norm(kept) + total[quarter(0, h), :])
    remote(ranges_in, ranges_in, r_send, r_recv, sibling).wait_recv()
    for dx in RING:
        across_range = jnp.broadcast_to(ranges_in[dx - 1, 0:1, :], (128, rows_dev))
        ranges_of[dx - 1] = across_range.T

    for h in range(2):
        summed = sums[h]
        here = coded_in.at[h]
        remote(here, here, p_send.at[h], p_recv.at[h], sibling).wait_recv()
        for dx in RING:
            part = coded_in[h, dx - 1].astype(jnp.float32)
            summed = summed + part * ranges_of[dx - 1, quarter(0, h), 0:1]
        everyone[pl.ds(h * half, half), :] = (summed * inverse_norm(summed)).astype(jnp.bfloat16)
        for i in range(SIDE - 1):
            copy_g(i, h).start()
    copy_s(0).start()

    def hand_over(h):
        here = everyone.at[pl.ds(starts[1 + h], others)]
        remote(here, here, g_send, g_recv.at[h], sibling).wait_recv()
        copy_s(1 + h).start()

    shares = tops.shape[0]
    share = queries_here // shares
    lines = share // 128

    def folded_scores(n, k):
        rows = everyone[pl.ds(starts[n], 2 * sizes[n]), :]
        panel = q_t[:, pl.ds(k * share, share)]
        scores = jnp.dot(rows, panel, preferred_element_type=jnp.float32)
        return jnp.max(scores.reshape(2 * sizes[n] // 8, 8, share), axis=0)

    def score_last(begin, end):
        for k in range(begin, end):
            top = jnp.maximum(first_top[k], folded_scores(2, k))
            top = jnp.max(top, axis=0, keepdims=True)
            for line in range(lines):
                tops[k, pl.ds(line, 1), :] = top[:, line * 128 : (line + 1) * 128]

    bounds = (0, shares * 3 // 4, shares)
    spans = [pl.ds(begin, end - begin) for begin, end in zip(bounds[:-1], bounds[1:])]

    def copy_y(i, n):
        return remote(
            tops.at[spans[n]], y_in.at[i, spans[n]], y_send, y_recv.at[n], plane(0, RING[i])
        )

    def copy_z(i, n):
        return remote(
            y_best.at[spans[n]], z_in.at[i, spans[n]], z_send, z_recv.at[n], plane(RING[i], 0)
        )

    def arrived(buffer, n, sem):
        here = buffer.at[:, spans[n]]
        remote(here, here, y_send, sem.at[n], sibling).wait_recv()

    copy_s(0).wait_recv()
    for k in range(shares):
        first_top[k] = folded_scores(0, k)
    hand_over(0)
    copy_s(1).wait_recv()
    for k in range(shares // 2):
        first_top[k] = jnp.maximum(first_top[k], folded_scores(1, k))
    hand_over(1)
    for k in range(shares // 2, shares):
        first_top[k] = jnp.maximum(first_top[k], folded_scores(1, k))
    copy_s(2).wait_recv()
    for n in range(2):
        score_last(bounds[n], bounds[n + 1])
        for i in range(SIDE - 1):
            copy_y(i, n).start()

    aug_ref[pl.ds(mine, own_rows), :] = everyone[pl.ds(0, own_rows), :]
    for h in range(2):
        for i in range(SIDE - 1):
            start = starts[1 + h] + i * half
            aug_ref[quarter(-RING[i], h), :] = everyone[pl.ds(start, half), :]

    for n in range(2):
        arrived(y_in, n, y_recv)
        best = tops[spans[n]]
        for i in range(SIDE - 1):
            best = jnp.maximum(best, y_in[i, spans[n]])
        y_best[spans[n]] = best
        for i in range(SIDE - 1):
            copy_z(i, n).start()
    for n in range(2):
        arrived(z_in, n, z_recv)
        best = y_best[spans[n]]
        for i in range(SIDE - 1):
            best = jnp.maximum(best, z_in[i, spans[n]])
        here = pl.ds(pl.multiple_of(c * shares, shares) + bounds[n], bounds[n + 1] - bounds[n])
        best_ref[here] = best
        remote(best_ref.at[here], best_ref.at[here], f_send, f_recv, sibling).start()

    sent(pool.at[pl.ds(0, 2 * (CHIPS - 1) * half)], ab_send)
    sent(pool.at[pl.ds(0, parity_rows)], c_send)
    sent(ranges_in, r_send)
    sent(coded_in.at[1], p_send.at[1])
    sent(everyone.at[pl.ds(0, 6 * half)], g_send)
    sent(everyone.at[pl.ds(0, 8 * half)], s_send)
    sent(y_in, y_send)
    sent(z_in, z_send)
    here = best_ref.at[pl.ds(0, shares)]
    remote(here, here, f_send, f_recv, sibling).wait()


def deliver(rows_in, best_in, rows_out, best_out):
    rows_out[...] = rows_in[...]
    best_out[...] = best_in[...]


def local(database, neighbours, valid_count, queries):
    rows_dev, features = database.shape
    fanout = neighbours.shape[1]
    queries_here = queries.shape[0] // CORES
    own_rows = rows_dev // SIDE
    pool_rows = rows_dev * CHIPS * CORES // SIDE
    share = queries_here // CHIPS
    vmem = pl.BlockSpec(memory_space=pltpu.VMEM)
    anywhere = pl.BlockSpec(memory_space=pl.ANY)
    dma = pltpu.SemaphoreType.DMA
    augmented, best = pl.pallas_call(
        kernel,
        out_shape=(
            jax.ShapeDtypeStruct((rows_dev, features), jnp.bfloat16),
            jax.ShapeDtypeStruct((CORES * CHIPS, share // 128, 128), jnp.float32),
        ),
        in_specs=[anywhere, anywhere, anywhere, anywhere],
        out_specs=(vmem, vmem),
        scratch_shapes=[
            pltpu.VMEM((queries_here, features), jnp.bfloat16),
            pltpu.VMEM((features, queries_here), jnp.bfloat16),
            pltpu.VMEM((rows_dev, features), jnp.bfloat16),
            pltpu.VMEM((fanout, rows_dev), jnp.int32),
            pltpu.VMEM((1, rows_dev), jnp.int32),
            pltpu.VMEM((pool_rows, features), jnp.bfloat16),
            pltpu.VMEM((8, rows_dev, pool_rows // 8), jnp.bfloat16),
            pltpu.VMEM((fanout, rows_dev), jnp.int32),
            pltpu.VMEM((rows_dev, features), jnp.float32),
            pltpu.VMEM((rows_dev, features), jnp.int16),
            pltpu.VMEM((2, SIDE - 1, own_rows // 2, features), jnp.int16),
            pltpu.VMEM((8, rows_dev), jnp.float32),
            pltpu.VMEM((SIDE - 1, 8, rows_dev), jnp.float32),
            pltpu.VMEM((SIDE - 1, rows_dev, 128), jnp.float32),
            pltpu.VMEM((CORES * rows_dev, features), jnp.bfloat16),
            pltpu.VMEM((CHIPS, 8, share), jnp.float32),
            pltpu.VMEM((CHIPS, share // 128, 128), jnp.float32),
            pltpu.VMEM((SIDE - 1, CHIPS, share // 128, 128), jnp.float32),
            pltpu.VMEM((CHIPS, share // 128, 128), jnp.float32),
            pltpu.VMEM((SIDE - 1, CHIPS, share // 128, 128), jnp.float32),
            pltpu.SMEM((CHIPS * CORES,), jnp.int32),
            dma((4,)),
            dma((4,)),
        ]
        + [dma((CHIPS,))] * 2
        + [dma((4,)), dma((2,)), dma((2,)), dma((2,)), dma((3,)), dma((2,)), dma((2,))]
        + [dma] * 10,
        compiler_params=pltpu.CompilerParams(
            collective_id=0, has_side_effects=True, vmem_limit_bytes=56 * 2**20
        ),
        name="expand_and_score",
    )(database, neighbours.T, valid_count.reshape(1, rows_dev), queries)
    augmented, best = pl.pallas_call(
        deliver,
        out_shape=(
            jax.ShapeDtypeStruct(augmented.shape, augmented.dtype),
            jax.ShapeDtypeStruct(best.shape, best.dtype),
        ),
        in_specs=[vmem, vmem],
        out_specs=(vmem, vmem),
        name="deliver",
    )(augmented, best)
    return augmented, best.reshape(queries.shape[0])


def solution(mesh):
    return jax.shard_map(
        local,
        mesh=mesh,
        in_specs=(P("db", None), P("db", None), P("db"), P("pb", None)),
        out_specs=(P("db", None), P("pb")),
        check_vma=False,
    )
```

```python
import functools

import jax
import jax.numpy as jnp
from jax import lax
from jax.experimental import pallas as pl
from jax.experimental.pallas import tpu as pltpu
from jax.sharding import PartitionSpec as P

epsilon = 1e-06
MESH = pl.DeviceIdType.MESH
SIDE = 4
CORES = 2
CHIPS = SIDE * SIDE
SLOTS = (
    (0, 0), (0, 1), (0, 3), (1, 0), (3, 0), (0, 2), (2, 0), (1, 1),
    (1, 3), (3, 1), (3, 3), (1, 2), (2, 1), (3, 2), (2, 3), (2, 2),
)
SLOT_AT = {offset: place for place, offset in enumerate(SLOTS)}
RING = (1, 3, 2)
FAR_FIRST = (2, 1, 3)


def inverse_norm(values):
    return lax.rsqrt(jnp.sum(values * values, axis=-1, keepdims=True) + epsilon)


def dot_rows(left, right):
    return lax.dot_general(
        left, right, (((1,), (1,)), ((), ())), preferred_element_type=jnp.float32
    )


def kernel(
    db_hbm, nb_hbm, vc_hbm, q_ref, aug_ref, best_ref,
    q_v, q_t, db_ref, nb_ref, vc_ref, pool, mask_ref, wanted, total, coded, coded_in, ranges, ranges_in, ranges_of,
    everyone, first_top, tops, y_in, y_best, z_in, bases,
    q_sem, l_sem, a_recv, b_recv, c_recv, p_send, p_recv, g_recv, s_recv, y_recv, z_recv, ab_send,
    c_send, r_send, r_recv, g_send, s_send, y_send, z_send,
):
    rows_dev, features = db_ref.shape
    fanout = nb_ref.shape[0]
    own_rows = rows_dev // SIDE
    half = own_rows // 2
    parity_rows = CHIPS * own_rows
    span = 4 * own_rows
    x = lax.axis_index("pb")
    d = lax.axis_index("db")
    c = d % CORES
    chip = d // CORES
    y = chip % SIDE
    z = chip // SIDE
    mine = pl.multiple_of(x * own_rows, own_rows)

    def plane(dz, dy):
        return (x, ((z + dz) % SIDE * SIDE + (y + dy) % SIDE) * CORES + c)

    sibling = (x, chip * CORES + (1 - c))

    def across(dx):
        return ((x + dx) % SIDE, d)

    def remote(src, dst, send, recv, to):
        return pltpu.make_async_remote_copy(
            src_ref=src, dst_ref=dst, send_sem=send, recv_sem=recv, device_id=to,
            device_id_type=MESH,
        )

    loads = [
        pltpu.make_async_copy(
            db_hbm.at[pl.ds(mine, own_rows)], pool.at[pl.ds(0, own_rows)], l_sem.at[0]
        ),
        pltpu.make_async_copy(nb_hbm, nb_ref, l_sem.at[1]),
        pltpu.make_async_copy(vc_hbm, vc_ref, l_sem.at[2]),
        pltpu.make_async_copy(db_hbm, db_ref, l_sem.at[3]),
    ]
    loads[0].start()

    barrier = pltpu.get_barrier_semaphore()
    partners = [plane(0, step) for step in RING] + [plane(step, 0) for step in RING]
    partners += [sibling] + [across(step) for step in RING]
    for partner in partners:
        pl.semaphore_signal(barrier, inc=1, device_id=partner, device_id_type=MESH)

    for load in loads[1:]:
        load.start()

    loads[0].wait()
    pl.semaphore_wait(barrier, len(partners))

    def block(place, core, start, rows):
        return pool.at[pl.ds(core * parity_rows + place * own_rows + start, rows)]

    def copy_a(dz, dy):
        src = SLOT_AT[(0, dy if dz else 0)]
        dst = SLOT_AT[(dz, dy)]
        to = plane(dz, 0) if dz else plane(0, dy)
        return remote(
            block(src, 0, 0, half), block(dst, 0, 0, half), ab_send, a_recv.at[dst], to
        )

    def copy_b(dz, dy):
        src = SLOT_AT[(dz if dy else 0, 0)]
        dst = SLOT_AT[(dz, dy)]
        to = plane(0, dy) if dy else plane(dz, 0)
        return remote(
            block(src, 0, half, half), block(dst, 0, half, half), ab_send,
            (a_recv if dz and dy else b_recv).at[dst], to,
        )

    def copy_c(place):
        return remote(
            block(place, 0, 0, own_rows), block(place, 1, 0, own_rows), c_send,
            c_recv.at[place // 4], sibling,
        )

    for step in RING:
        copy_a(0, step).start()
        copy_b(step, 0).start()
    copy_c(0).start()
    for step in RING:
        copy_a(step, 0).start()
        copy_b(0, step).start()

    queries_here = q_v.shape[0]
    piece = queries_here // 4
    query_loads = [
        pltpu.make_async_copy(
            q_ref.at[pl.ds(pl.multiple_of(c * queries_here + k * piece, piece), piece)],
            q_v.at[pl.ds(k * piece, piece)],
            q_sem.at[k],
        )
        for k in range(4)
    ]
    for load in query_loads:
        load.start()
    for load in loads[1:]:
        load.wait()

    place_of = lax.broadcasted_iota(jnp.int32, (fanout, rows_dev), 0)
    wanted[...] = jnp.where(place_of < vc_ref[...], nb_ref[...], -1)
    for place, (dz, dy) in enumerate(SLOTS):
        for core in range(CORES):
            owner = ((z - dz) % SIDE * SIDE + (y - dy) % SIDE) * CORES + (c + core) % CORES
            bases[core * CHIPS + place] = owner * rows_dev + x * own_rows

    def build_mask(part):
        for u in range(2):
            counts = []
            for v in range(2):
                base = bases[part * 4 + u * 2 + v]
                number = base + lax.broadcasted_iota(jnp.int32, (own_rows, rows_dev), 0)
                count = jnp.zeros((own_rows, rows_dev), jnp.float32)
                for k in range(fanout):
                    count = count + jnp.where(wanted[pl.ds(k, 1), :] == number, 1.0, 0.0)
                counts.append(count)
            both = jnp.concatenate(counts, axis=0)
            mask_ref[part, :, pl.ds(u * 2 * own_rows, 2 * own_rows)] = both.T.astype(jnp.bfloat16)

    def first_masks(i, _):
        build_mask(4 * i)
        return 0

    def other_masks(i, _):
        build_mask(i + 1 + i // 3)
        return 0

    lax.fori_loop(0, 2, first_masks, 0)

    for step in RING:
        copy_a(0, step).wait_recv()
        for far in RING:
            copy_a(far, step).start()
        copy_b(step, 0).wait_recv()
        for far in RING:
            copy_b(step, far).start()

    lax.fori_loop(0, 6, other_masks, 0)

    for step in RING:
        copy_b(0, step).wait_recv()
        copy_c(SLOT_AT[(0, step)]).start()
        copy_a(step, 0).wait_recv()
        copy_c(SLOT_AT[(step, 0)]).start()

    def pass_on(place):
        here = block(place, 0, 0, own_rows)
        remote(here, here, ab_send, a_recv.at[place], sibling).wait_recv()
        copy_c(place).start()

    total[...] = jnp.zeros_like(total)
    own = db_ref[...]
    own_inverse = inverse_norm(own.astype(jnp.float32))

    def take(g):
        rows = pool[pl.ds(pl.multiple_of(g * span, span), span), :]
        squares = rows.astype(jnp.float32)
        squares = squares * squares
        folded = squares[:, 0:128]
        for k in range(1, features // 128):
            folded = folded + squares[:, k * 128 : (k + 1) * 128]
        far_inverse = lax.rsqrt(jnp.sum(folded.T, axis=0, keepdims=True) + epsilon)
        cosine = dot_rows(own, rows) * own_inverse * far_inverse
        halfway = (1.0 + cosine) * 0.5
        weight = halfway * halfway * halfway
        coefficient = (weight * far_inverse).astype(jnp.bfloat16).astype(jnp.float32)
        count = mask_ref[g].astype(jnp.float32)
        spread = jnp.where(count > 0.0, count * coefficient, 0.0)
        total[...] += jnp.dot(
            spread.astype(jnp.bfloat16), rows, preferred_element_type=jnp.float32
        )

    def step_over(i, _):
        part = jnp.where(i < 4, i // 2 + i % 2 * 4, jnp.where(i < 6, i - 2, i))

        @pl.when(i == 2)
        def _():
            pass_on(7)

        @pl.when((i == 4) | (i == 5))
        def _():
            for u in range(4):
                here = block(part * 4 + u, 0, 0, own_rows)
                remote(here, here, ab_send, a_recv.at[part * 4 + u], sibling).wait_recv()
            remote(
                block(part * 4, 0, 0, span), block(part * 4, 1, 0, span), c_send,
                c_recv.at[part], sibling,
            ).start()

        @pl.when(part >= 4)
        def _():
            here = pool.at[pl.ds(pl.multiple_of(part * span, span), span)]
            remote(here, here, c_send, c_recv.at[part - 4], sibling).wait_recv()

        take(part)
        return 0

    lax.fori_loop(0, 8, step_over, 0)

    partial = total[...]
    largest = jnp.max(jnp.abs(partial), axis=-1, keepdims=True)
    largest = jnp.maximum(largest, 1e-30)
    coded[...] = jnp.round(partial * (32760.0 / largest)).astype(jnp.int32).astype(jnp.int16)
    spread_range = jnp.broadcast_to(largest * (1.0 / 32760.0), (rows_dev, 128))
    ranges[...] = spread_range.T[0:8, :]

    def quarter(dx, h):
        start = (x + SIDE + dx) % SIDE * own_rows + h * half
        return pl.ds(pl.multiple_of(start, half), half)

    def copy_r(dx):
        return remote(ranges, ranges_in.at[dx - 1], r_send, r_recv, across(dx))

    def copy_p(dx, h):
        return remote(
            coded.at[quarter(dx, h)], coded_in.at[h, dx - 1], p_send.at[h], p_recv.at[h], across(dx)
        )

    def sent(ref, sem):
        remote(ref, ref, sem, sem, sibling).wait_send()

    for dx in FAR_FIRST:
        copy_p(dx, 0).start()
    for dx in FAR_FIRST:
        copy_r(dx).start()
    for load in query_loads:
        load.wait()
    panel_rows = 512

    def turn(i, _):
        for u in range(4):
            rows = pl.ds(pl.multiple_of((i * 4 + u) * panel_rows, panel_rows), panel_rows)
            q_t[:, rows] = q_v[rows, :].T
        return 0

    turns = queries_here // (4 * panel_rows)
    lax.fori_loop(0, turns // 2, turn, 0)
    sent(coded_in.at[0], p_send.at[0])
    for dx in FAR_FIRST:
        copy_p(dx, 1).start()
    lax.fori_loop(turns // 2, turns, turn, 0)

    others = (SIDE - 1) * half
    starts = (0, 2 * own_rows, 2 * own_rows + 2 * others)
    sizes = (own_rows, others, others)

    def copy_g(i, h):
        return remote(
            everyone.at[pl.ds(h * half, half)], everyone.at[pl.ds(starts[1 + h] + i * half, half)],
            g_send, g_recv.at[h], across(FAR_FIRST[i]),
        )

    def copy_s(n):
        return remote(
            everyone.at[pl.ds(starts[n], sizes[n])],
            everyone.at[pl.ds(starts[n] + sizes[n], sizes[n])], s_send, s_recv.at[n], sibling,
        )

    sums = []
    for h in range(2):
        kept = db_ref[quarter(0, h), :].astype(jnp.float32)
        sums.append(kept * inverse_norm(kept) + total[quarter(0, h), :])
    remote(ranges_in, ranges_in, r_send, r_recv, sibling).wait_recv()
    for dx in FAR_FIRST:
        across_range = jnp.broadcast_to(ranges_in[dx - 1, 0:1, :], (128, rows_dev))
        ranges_of[dx - 1] = across_range.T

    for h in range(2):
        summed = sums[h]
        here = coded_in.at[h]
        remote(here, here, p_send.at[h], p_recv.at[h], sibling).wait_recv()
        for dx in FAR_FIRST:
            part = coded_in[h, dx - 1].astype(jnp.float32)
            summed = summed + part * ranges_of[dx - 1, quarter(0, h), 0:1]
        everyone[pl.ds(h * half, half), :] = (summed * inverse_norm(summed)).astype(jnp.bfloat16)
        for i in range(SIDE - 1):
            copy_g(i, h).start()
    copy_s(0).start()

    def hand_over(h):
        here = everyone.at[pl.ds(starts[1 + h], others)]
        remote(here, here, g_send, g_recv.at[h], sibling).wait_recv()
        copy_s(1 + h).start()

    shares = tops.shape[0]
    share = queries_here // shares
    lines = share // 128

    def folded_scores(n, k):
        rows = everyone[pl.ds(starts[n], 2 * sizes[n]), :]
        panel = q_t[:, pl.ds(k * share, share)]
        scores = jnp.dot(rows, panel, preferred_element_type=jnp.float32)
        return jnp.max(scores.reshape(2 * sizes[n] // 8, 8, share), axis=0)

    def score_last(begin, end):
        for k in range(begin, end):
            top = jnp.maximum(first_top[k], folded_scores(2, k))
            top = jnp.max(top, axis=0, keepdims=True)
            for line in range(lines):
                tops[k, pl.ds(line, 1), :] = top[:, line * 128 : (line + 1) * 128]

    bounds = (0, shares * 3 // 4, shares)
    spans = [pl.ds(begin, end - begin) for begin, end in zip(bounds[:-1], bounds[1:])]

    def copy_y(i, n):
        return remote(
            tops.at[spans[n]], y_in.at[i, spans[n]], y_send, y_recv.at[n], plane(0, FAR_FIRST[i])
        )

    def copy_z(i, n, other):
        to_x, to_d = plane(FAR_FIRST[i], 0)
        if other:
            to_d = to_d + 1 - 2 * c
        return remote(
            y_best.at[spans[n]], z_in.at[other * (SIDE - 1) + i, spans[n]], z_send, z_recv.at[n],
            (to_x, to_d),
        )

    def arrived(buffer, n, sem):
        here = buffer.at[:, spans[n]]
        remote(here, here, y_send, sem.at[n], sibling).wait_recv()

    copy_s(0).wait_recv()
    for k in range(12):
        first_top[k] = folded_scores(0, k)
    hand_over(0)
    for k in range(12, shares):
        first_top[k] = folded_scores(0, k)
    copy_s(1).wait_recv()
    for k in range(shares // 2):
        first_top[k] = jnp.maximum(first_top[k], folded_scores(1, k))
    hand_over(1)
    for k in range(shares // 2, shares):
        first_top[k] = jnp.maximum(first_top[k], folded_scores(1, k))
    copy_s(2).wait_recv()
    for n in range(2):
        score_last(bounds[n], bounds[n + 1])
        for i in range(SIDE - 1):
            copy_y(i, n).start()

    aug_ref[pl.ds(mine, own_rows), :] = everyone[pl.ds(0, own_rows), :]
    for h in range(2):
        for i in range(SIDE - 1):
            start = starts[1 + h] + i * half
            aug_ref[quarter(-FAR_FIRST[i], h), :] = everyone[pl.ds(start, half), :]

    for n in range(2):
        arrived(y_in, n, y_recv)
        best = tops[spans[n]]
        for i in range(SIDE - 1):
            best = jnp.maximum(best, y_in[i, spans[n]])
        y_best[spans[n]] = best
        for other in range(CORES):
            for i in range(SIDE - 1):
                copy_z(i, n, other).start()
        remote(
            y_best.at[spans[n]], z_in.at[2 * (SIDE - 1), spans[n]], z_send, z_recv.at[n], sibling
        ).start()
    for n in range(2):
        arrived(z_in, n, z_recv)
        for other in range(CORES):
            best = z_in[2 * (SIDE - 1), spans[n]] if other else y_best[spans[n]]
            for i in range(SIDE - 1):
                best = jnp.maximum(best, z_in[other * (SIDE - 1) + i, spans[n]])
            first = (1 - c if other else c) * shares
            here = pl.ds(pl.multiple_of(first, shares) + bounds[n], bounds[n + 1] - bounds[n])
            best_ref[here] = best

    sent(pool.at[pl.ds(0, 2 * (CHIPS - 1) * half)], ab_send)
    sent(pool.at[pl.ds(0, parity_rows)], c_send)
    sent(ranges_in, r_send)
    sent(coded_in.at[1], p_send.at[1])
    sent(everyone.at[pl.ds(0, 6 * half)], g_send)
    sent(everyone.at[pl.ds(0, 8 * half)], s_send)
    sent(y_in, y_send)
    sent(z_in, z_send)


def deliver(rows_in, best_in, rows_out, best_out):
    rows_out[...] = rows_in[...]
    best_out[...] = best_in[...]


def local(database, neighbours, valid_count, queries):
    rows_dev, features = database.shape
    fanout = neighbours.shape[1]
    queries_here = queries.shape[0] // CORES
    own_rows = rows_dev // SIDE
    pool_rows = rows_dev * CHIPS * CORES // SIDE
    share = queries_here // CHIPS
    vmem = pl.BlockSpec(memory_space=pltpu.VMEM)
    anywhere = pl.BlockSpec(memory_space=pl.ANY)
    dma = pltpu.SemaphoreType.DMA
    augmented, best = pl.pallas_call(
        kernel,
        out_shape=(
            pltpu.VMEM((rows_dev, features), jnp.bfloat16),
            pltpu.VMEM((CORES * CHIPS, share // 128, 128), jnp.float32),
        ),
        in_specs=[anywhere, anywhere, anywhere, anywhere],
        out_specs=(vmem, vmem),
        scratch_shapes=[
            pltpu.VMEM((queries_here, features), jnp.bfloat16),
            pltpu.VMEM((features, queries_here), jnp.bfloat16),
            pltpu.VMEM((rows_dev, features), jnp.bfloat16),
            pltpu.VMEM((fanout, rows_dev), jnp.int32),
            pltpu.VMEM((1, rows_dev), jnp.int32),
            pltpu.VMEM((pool_rows, features), jnp.bfloat16),
            pltpu.VMEM((8, rows_dev, pool_rows // 8), jnp.bfloat16),
            pltpu.VMEM((fanout, rows_dev), jnp.int32),
            pltpu.VMEM((rows_dev, features), jnp.float32),
            pltpu.VMEM((rows_dev, features), jnp.int16),
            pltpu.VMEM((2, SIDE - 1, own_rows // 2, features), jnp.int16),
            pltpu.VMEM((8, rows_dev), jnp.float32),
            pltpu.VMEM((SIDE - 1, 8, rows_dev), jnp.float32),
            pltpu.VMEM((SIDE - 1, rows_dev, 128), jnp.float32),
            pltpu.VMEM((CORES * rows_dev, features), jnp.bfloat16),
            pltpu.VMEM((CHIPS, 8, share), jnp.float32),
            pltpu.VMEM((CHIPS, share // 128, 128), jnp.float32),
            pltpu.VMEM((SIDE - 1, CHIPS, share // 128, 128), jnp.float32),
            pltpu.VMEM((CHIPS, share // 128, 128), jnp.float32),
            pltpu.VMEM((2 * SIDE - 1, CHIPS, share // 128, 128), jnp.float32),
            pltpu.SMEM((CHIPS * CORES,), jnp.int32),
            dma((4,)),
            dma((4,)),
        ]
        + [dma((CHIPS,))] * 2
        + [dma((4,)), dma((2,)), dma((2,)), dma((2,)), dma((3,)), dma((2,)), dma((2,))]
        + [dma] * 8,
        compiler_params=pltpu.CompilerParams(
            collective_id=0, has_side_effects=True, vmem_limit_bytes=56 * 2**20
        ),
        name="expand_and_score",
    )(database, neighbours.T, valid_count.reshape(1, rows_dev), queries)
    augmented, best = pl.pallas_call(
        deliver,
        out_shape=(
            jax.ShapeDtypeStruct(augmented.shape, augmented.dtype),
            jax.ShapeDtypeStruct(best.shape, best.dtype),
        ),
        in_specs=[vmem, vmem],
        out_specs=(vmem, vmem),
        name="deliver",
    )(
        pltpu.with_memory_space_constraint(augmented, pltpu.VMEM),
        pltpu.with_memory_space_constraint(best, pltpu.VMEM),
    )
    return augmented, best.reshape(queries.shape[0])


def solution(mesh):
    return jax.shard_map(
        local,
        mesh=mesh,
        in_specs=(P("db", None), P("db", None), P("db"), P("pb", None)),
        out_specs=(P("db", None), P("pb")),
        check_vma=False,
    )
```

```python
import functools

import jax
import jax.numpy as jnp
from jax import lax
from jax.experimental import pallas as pl
from jax.experimental.pallas import tpu as pltpu
from jax.sharding import PartitionSpec as P

epsilon = 1e-06
MESH = pl.DeviceIdType.MESH
SIDE = 4
CORES = 2
CHIPS = SIDE * SIDE
SLOTS = (
    (0, 0), (0, 1), (0, 3), (1, 0), (3, 0), (0, 2), (2, 0), (1, 1),
    (1, 3), (3, 1), (3, 3), (1, 2), (2, 1), (3, 2), (2, 3), (2, 2),
)
SLOT_AT = {offset: place for place, offset in enumerate(SLOTS)}
RING = (1, 3, 2)
FAR_FIRST = (2, 1, 3)
EARLY = 12


def inverse_norm(values):
    return lax.rsqrt(jnp.sum(values * values, axis=-1, keepdims=True) + epsilon)


def dot_rows(left, right):
    return lax.dot_general(
        left, right, (((1,), (1,)), ((), ())), preferred_element_type=jnp.float32
    )


def kernel(
    db_hbm, nb_hbm, vc_hbm, q_ref, aug_ref, best_ref,
    q_v, q_t, db_ref, nb_ref, vc_ref, pool, mask_ref, wanted, total, coded, coded_in, ranges, ranges_in, ranges_of,
    everyone, first_top, tops, y_in, y_best, z_in, late_in, bases,
    q_sem, l_sem, a_recv, b_recv, c_recv, p_send, p_recv, g_recv, s_recv, ab_send, c_send,
    r_send, r_recv, g_send, s_send, y_send, y_recv, z_send, z_recv, t_send, t_recv, f_send, f_recv,
):
    rows_dev, features = db_ref.shape
    fanout = nb_ref.shape[0]
    own_rows = rows_dev // SIDE
    half = own_rows // 2
    parity_rows = CHIPS * own_rows
    span = 4 * own_rows
    x = lax.axis_index("pb")
    d = lax.axis_index("db")
    c = d % CORES
    chip = d // CORES
    y = chip % SIDE
    z = chip // SIDE
    mine = pl.multiple_of(x * own_rows, own_rows)

    def plane(dz, dy):
        return (x, ((z + dz) % SIDE * SIDE + (y + dy) % SIDE) * CORES + c)

    sibling = (x, chip * CORES + (1 - c))

    def across(dx):
        return ((x + dx) % SIDE, d)

    def remote(src, dst, send, recv, to):
        return pltpu.make_async_remote_copy(
            src_ref=src, dst_ref=dst, send_sem=send, recv_sem=recv, device_id=to,
            device_id_type=MESH,
        )

    loads = [
        pltpu.make_async_copy(
            db_hbm.at[pl.ds(mine, own_rows)], pool.at[pl.ds(0, own_rows)], l_sem.at[0]
        ),
        pltpu.make_async_copy(nb_hbm, nb_ref, l_sem.at[1]),
        pltpu.make_async_copy(vc_hbm, vc_ref, l_sem.at[2]),
        pltpu.make_async_copy(db_hbm, db_ref, l_sem.at[3]),
    ]
    loads[0].start()

    barrier = pltpu.get_barrier_semaphore()
    partners = [plane(0, step) for step in RING] + [plane(step, 0) for step in RING]
    partners += [sibling] + [across(step) for step in RING]
    for partner in partners:
        pl.semaphore_signal(barrier, inc=1, device_id=partner, device_id_type=MESH)

    for load in loads[1:]:
        load.start()

    loads[0].wait()
    pl.semaphore_wait(barrier, len(partners))

    def block(place, core, start, rows):
        return pool.at[pl.ds(core * parity_rows + place * own_rows + start, rows)]

    def copy_a(dz, dy):
        src = SLOT_AT[(0, dy if dz else 0)]
        dst = SLOT_AT[(dz, dy)]
        to = plane(dz, 0) if dz else plane(0, dy)
        return remote(
            block(src, 0, 0, half), block(dst, 0, 0, half), ab_send, a_recv.at[dst], to
        )

    def copy_b(dz, dy):
        src = SLOT_AT[(dz if dy else 0, 0)]
        dst = SLOT_AT[(dz, dy)]
        to = plane(0, dy) if dy else plane(dz, 0)
        return remote(
            block(src, 0, half, half), block(dst, 0, half, half), ab_send,
            (a_recv if dz and dy else b_recv).at[dst], to,
        )

    def copy_c(place):
        return remote(
            block(place, 0, 0, own_rows), block(place, 1, 0, own_rows), c_send,
            c_recv.at[place // 4], sibling,
        )

    for step in RING:
        copy_a(0, step).start()
        copy_b(step, 0).start()
    copy_c(0).start()
    for step in RING:
        copy_a(step, 0).start()
        copy_b(0, step).start()

    queries_here = q_v.shape[0]
    piece = queries_here // 4
    query_loads = [
        pltpu.make_async_copy(
            q_ref.at[pl.ds(pl.multiple_of(c * queries_here + k * piece, piece), piece)],
            q_v.at[pl.ds(k * piece, piece)],
            q_sem.at[k],
        )
        for k in range(4)
    ]
    for load in query_loads:
        load.start()
    for load in loads[1:]:
        load.wait()

    place_of = lax.broadcasted_iota(jnp.int32, (fanout, rows_dev), 0)
    wanted[...] = jnp.where(place_of < vc_ref[...], nb_ref[...], -1)
    for place, (dz, dy) in enumerate(SLOTS):
        for core in range(CORES):
            owner = ((z - dz) % SIDE * SIDE + (y - dy) % SIDE) * CORES + (c + core) % CORES
            bases[core * CHIPS + place] = owner * rows_dev + x * own_rows

    def build_mask(part):
        for u in range(2):
            counts = []
            for v in range(2):
                base = bases[part * 4 + u * 2 + v]
                number = base + lax.broadcasted_iota(jnp.int32, (own_rows, rows_dev), 0)
                count = jnp.zeros((own_rows, rows_dev), jnp.float32)
                for k in range(fanout):
                    count = count + jnp.where(wanted[pl.ds(k, 1), :] == number, 1.0, 0.0)
                counts.append(count)
            both = jnp.concatenate(counts, axis=0)
            mask_ref[part, :, pl.ds(u * 2 * own_rows, 2 * own_rows)] = both.T.astype(jnp.bfloat16)

    def first_masks(i, _):
        build_mask(4 * i)
        return 0

    def other_masks(i, _):
        build_mask(i + 1 + i // 3)
        return 0

    lax.fori_loop(0, 2, first_masks, 0)

    for step in RING:
        copy_a(0, step).wait_recv()
        for far in RING:
            copy_a(far, step).start()
        copy_b(step, 0).wait_recv()
        for far in RING:
            copy_b(step, far).start()

    lax.fori_loop(0, 6, other_masks, 0)

    for step in RING:
        copy_b(0, step).wait_recv()
        copy_c(SLOT_AT[(0, step)]).start()
        copy_a(step, 0).wait_recv()
        copy_c(SLOT_AT[(step, 0)]).start()

    def pass_on(place):
        here = block(place, 0, 0, own_rows)
        remote(here, here, ab_send, a_recv.at[place], sibling).wait_recv()
        copy_c(place).start()

    total[...] = jnp.zeros_like(total)
    own = db_ref[...]
    own_inverse = inverse_norm(own.astype(jnp.float32))

    def take(g):
        rows = pool[pl.ds(pl.multiple_of(g * span, span), span), :]
        squares = rows.astype(jnp.float32)
        squares = squares * squares
        folded = squares[:, 0:128]
        for k in range(1, features // 128):
            folded = folded + squares[:, k * 128 : (k + 1) * 128]
        far_inverse = lax.rsqrt(jnp.sum(folded.T, axis=0, keepdims=True) + epsilon)
        cosine = dot_rows(own, rows) * own_inverse * far_inverse
        halfway = (1.0 + cosine) * 0.5
        weight = halfway * halfway * halfway
        coefficient = (weight * far_inverse).astype(jnp.bfloat16).astype(jnp.float32)
        count = mask_ref[g].astype(jnp.float32)
        spread = jnp.where(count > 0.0, count * coefficient, 0.0)
        total[...] += jnp.dot(
            spread.astype(jnp.bfloat16), rows, preferred_element_type=jnp.float32
        )

    def step_over(i, _):
        part = jnp.where(i < 4, i // 2 + i % 2 * 4, jnp.where(i < 6, i - 2, i))

        @pl.when(i == 2)
        def _():
            pass_on(7)

        @pl.when((i == 4) | (i == 5))
        def _():
            for u in range(4):
                here = block(part * 4 + u, 0, 0, own_rows)
                remote(here, here, ab_send, a_recv.at[part * 4 + u], sibling).wait_recv()
            remote(
                block(part * 4, 0, 0, span), block(part * 4, 1, 0, span), c_send,
                c_recv.at[part], sibling,
            ).start()

        @pl.when(part >= 4)
        def _():
            here = pool.at[pl.ds(pl.multiple_of(part * span, span), span)]
            remote(here, here, c_send, c_recv.at[part - 4], sibling).wait_recv()

        take(part)
        return 0

    lax.fori_loop(0, 8, step_over, 0)

    partial = total[...]
    largest = jnp.max(jnp.abs(partial), axis=-1, keepdims=True)
    largest = jnp.maximum(largest, 1e-30)
    coded[...] = jnp.round(partial * (32760.0 / largest)).astype(jnp.int32).astype(jnp.int16)
    spread_range = jnp.broadcast_to(largest * (1.0 / 32760.0), (rows_dev, 128))
    ranges[...] = spread_range.T[0:8, :]

    def quarter(dx, h):
        start = (x + SIDE + dx) % SIDE * own_rows + h * half
        return pl.ds(pl.multiple_of(start, half), half)

    def copy_r(dx):
        return remote(ranges, ranges_in.at[dx - 1], r_send, r_recv, across(dx))

    def copy_p(dx, h):
        return remote(
            coded.at[quarter(dx, h)], coded_in.at[h, dx - 1], p_send.at[h], p_recv.at[h], across(dx)
        )

    def sent(ref, sem):
        remote(ref, ref, sem, sem, sibling).wait_send()

    for dx in FAR_FIRST:
        copy_p(dx, 0).start()
    for dx in FAR_FIRST:
        copy_r(dx).start()
    for load in query_loads:
        load.wait()
    panel_rows = 512

    def turn(i, _):
        for u in range(4):
            rows = pl.ds(pl.multiple_of((i * 4 + u) * panel_rows, panel_rows), panel_rows)
            q_t[:, rows] = q_v[rows, :].T
        return 0

    turns = queries_here // (4 * panel_rows)
    lax.fori_loop(0, turns // 2, turn, 0)
    sent(coded_in.at[0], p_send.at[0])
    for dx in FAR_FIRST:
        copy_p(dx, 1).start()
    lax.fori_loop(turns // 2, turns, turn, 0)

    others = (SIDE - 1) * half
    starts = (0, 2 * own_rows, 2 * own_rows + 2 * others)
    sizes = (own_rows, others, others)

    def copy_g(i, h):
        return remote(
            everyone.at[pl.ds(h * half, half)], everyone.at[pl.ds(starts[1 + h] + i * half, half)],
            g_send, g_recv.at[h], across(FAR_FIRST[i]),
        )

    def copy_s(n):
        return remote(
            everyone.at[pl.ds(starts[n], sizes[n])],
            everyone.at[pl.ds(starts[n] + sizes[n], sizes[n])], s_send, s_recv.at[n], sibling,
        )

    sums = []
    for h in range(2):
        kept = db_ref[quarter(0, h), :].astype(jnp.float32)
        sums.append(kept * inverse_norm(kept) + total[quarter(0, h), :])
    remote(ranges_in, ranges_in, r_send, r_recv, sibling).wait_recv()
    for dx in FAR_FIRST:
        across_range = jnp.broadcast_to(ranges_in[dx - 1, 0:1, :], (128, rows_dev))
        ranges_of[dx - 1] = across_range.T

    for h in range(2):
        summed = sums[h]
        here = coded_in.at[h]
        remote(here, here, p_send.at[h], p_recv.at[h], sibling).wait_recv()
        for dx in FAR_FIRST:
            part = coded_in[h, dx - 1].astype(jnp.float32)
            summed = summed + part * ranges_of[dx - 1, quarter(0, h), 0:1]
        everyone[pl.ds(h * half, half), :] = (summed * inverse_norm(summed)).astype(jnp.bfloat16)
        for i in range(SIDE - 1):
            copy_g(i, h).start()
    copy_s(0).start()

    def hand_over(h):
        here = everyone.at[pl.ds(starts[1 + h], others)]
        remote(here, here, g_send, g_recv.at[h], sibling).wait_recv()
        copy_s(1 + h).start()

    shares = tops.shape[0]
    share = queries_here // shares
    lines = share // 128

    def folded_scores(begin, end, k):
        panel = q_t[:, pl.ds(k * share, share)]
        scores = jnp.dot(
            everyone[pl.ds(begin, end - begin), :], panel, preferred_element_type=jnp.float32
        )
        return jnp.max(scores.reshape((end - begin) // 8, 8, share), axis=0)

    first, second, third = starts
    stop = 2 * rows_dev

    def finish(k, begin):
        top = jnp.maximum(first_top[k], folded_scores(begin, stop, k))
        top = jnp.max(top, axis=0, keepdims=True)
        for line in range(lines):
            tops[k, pl.ds(line, 1), :] = top[:, line * 128 : (line + 1) * 128]

    early = y_best.shape[0]
    early_shares, late_shares = pl.ds(0, early), pl.ds(early, shares - early)

    def copy_y(i):
        return remote(
            tops.at[early_shares], y_in.at[i], y_send, y_recv, plane(0, FAR_FIRST[i])
        )

    def copy_z(i, other):
        to_x, to_d = plane(FAR_FIRST[i], 0)
        if other:
            to_d = to_d + 1 - 2 * c
        return remote(
            y_best, z_in.at[other * (SIDE - 1) + i], z_send, z_recv, (to_x, to_d)
        )

    def copy_l(place):
        return remote(
            tops.at[late_shares], late_in.at[place - 1], t_send, t_recv, plane(*SLOTS[place])
        )

    def arrived(buffer, sem):
        remote(buffer, buffer, y_send, sem, sibling).wait_recv()

    copy_s(0).wait_recv()
    for k in range(shares):
        if k == shares * 3 // 4:
            hand_over(0)
        first_top[k] = folded_scores(first, second, k)
    copy_s(1).wait_recv()
    for k in range(early):
        if k == early // 2:
            hand_over(1)
        first_top[k] = jnp.maximum(first_top[k], folded_scores(second, third, k))
    copy_s(2).wait_recv()
    for k in range(early):
        finish(k, third)
    for i in range(SIDE - 1):
        copy_y(i).start()
    for k in range(early, shares):
        finish(k, second)
    for place in reversed(range(1, CHIPS)):
        copy_l(place).start()

    arrived(y_in, y_recv)
    best = tops[early_shares]
    for i in range(SIDE - 1):
        best = jnp.maximum(best, y_in[i])
    y_best[...] = best
    for other in range(CORES):
        for i in range(SIDE - 1):
            copy_z(i, other).start()
    remote(y_best, z_in.at[2 * (SIDE - 1)], z_send, z_recv, sibling).start()

    aug_ref[pl.ds(mine, own_rows), :] = everyone[pl.ds(0, own_rows), :]
    for h in range(2):
        for i in range(SIDE - 1):
            start = starts[1 + h] + i * half
            aug_ref[quarter(-FAR_FIRST[i], h), :] = everyone[pl.ds(start, half), :]

    arrived(late_in, t_recv)
    best = tops[late_shares]
    for i in range(CHIPS - 1):
        best = jnp.maximum(best, late_in[i])
    here = pl.ds(pl.multiple_of(c * shares, shares) + early, shares - early)
    best_ref[here] = best
    copy_f = remote(best_ref.at[here], best_ref.at[here], f_send, f_recv, sibling)
    copy_f.start()

    arrived(z_in, z_recv)
    for other in range(CORES):
        best = z_in[2 * (SIDE - 1)] if other else y_best[...]
        for i in range(SIDE - 1):
            best = jnp.maximum(best, z_in[other * (SIDE - 1) + i])
        start = (1 - c if other else c) * shares
        best_ref[pl.ds(pl.multiple_of(start, shares), early)] = best

    sent(pool.at[pl.ds(0, 2 * (CHIPS - 1) * half)], ab_send)
    sent(pool.at[pl.ds(0, parity_rows)], c_send)
    sent(ranges_in, r_send)
    sent(coded_in.at[1], p_send.at[1])
    sent(everyone.at[pl.ds(0, 6 * half)], g_send)
    sent(everyone.at[pl.ds(0, 8 * half)], s_send)
    sent(y_in, y_send)
    sent(z_in, z_send)
    sent(late_in, t_send)
    copy_f.wait()


def deliver(rows_in, best_in, rows_out, best_out):
    rows_out[...] = rows_in[...]
    best_out[...] = best_in[...]


def local(database, neighbours, valid_count, queries):
    rows_dev, features = database.shape
    fanout = neighbours.shape[1]
    queries_here = queries.shape[0] // CORES
    own_rows = rows_dev // SIDE
    pool_rows = rows_dev * CHIPS * CORES // SIDE
    share = queries_here // CHIPS
    vmem = pl.BlockSpec(memory_space=pltpu.VMEM)
    anywhere = pl.BlockSpec(memory_space=pl.ANY)
    dma = pltpu.SemaphoreType.DMA
    augmented, best = pl.pallas_call(
        kernel,
        out_shape=(
            pltpu.VMEM((rows_dev, features), jnp.bfloat16),
            pltpu.VMEM((CORES * CHIPS, share // 128, 128), jnp.float32),
        ),
        in_specs=[anywhere, anywhere, anywhere, anywhere],
        out_specs=(vmem, vmem),
        scratch_shapes=[
            pltpu.VMEM((queries_here, features), jnp.bfloat16),
            pltpu.VMEM((features, queries_here), jnp.bfloat16),
            pltpu.VMEM((rows_dev, features), jnp.bfloat16),
            pltpu.VMEM((fanout, rows_dev), jnp.int32),
            pltpu.VMEM((1, rows_dev), jnp.int32),
            pltpu.VMEM((pool_rows, features), jnp.bfloat16),
            pltpu.VMEM((8, rows_dev, pool_rows // 8), jnp.bfloat16),
            pltpu.VMEM((fanout, rows_dev), jnp.int32),
            pltpu.VMEM((rows_dev, features), jnp.float32),
            pltpu.VMEM((rows_dev, features), jnp.int16),
            pltpu.VMEM((2, SIDE - 1, own_rows // 2, features), jnp.int16),
            pltpu.VMEM((8, rows_dev), jnp.float32),
            pltpu.VMEM((SIDE - 1, 8, rows_dev), jnp.float32),
            pltpu.VMEM((SIDE - 1, rows_dev, 128), jnp.float32),
            pltpu.VMEM((CORES * rows_dev, features), jnp.bfloat16),
            pltpu.VMEM((CHIPS, 8, share), jnp.float32),
            pltpu.VMEM((CHIPS, share // 128, 128), jnp.float32),
            pltpu.VMEM((SIDE - 1, EARLY, share // 128, 128), jnp.float32),
            pltpu.VMEM((EARLY, share // 128, 128), jnp.float32),
            pltpu.VMEM((2 * SIDE - 1, EARLY, share // 128, 128), jnp.float32),
            pltpu.VMEM((CHIPS - 1, CHIPS - EARLY, share // 128, 128), jnp.float32),
            pltpu.SMEM((CHIPS * CORES,), jnp.int32),
            dma((4,)),
            dma((4,)),
        ]
        + [dma((CHIPS,))] * 2
        + [dma((4,)), dma((2,)), dma((2,)), dma((2,)), dma((3,))]
        + [dma] * 14,
        compiler_params=pltpu.CompilerParams(
            collective_id=0, has_side_effects=True, vmem_limit_bytes=56 * 2**20
        ),
        name="expand_and_score",
    )(database, neighbours.T, valid_count.reshape(1, rows_dev), queries)
    augmented, best = pl.pallas_call(
        deliver,
        out_shape=(
            jax.ShapeDtypeStruct(augmented.shape, augmented.dtype),
            jax.ShapeDtypeStruct(best.shape, best.dtype),
        ),
        in_specs=[vmem, vmem],
        out_specs=(vmem, vmem),
        name="deliver",
    )(
        pltpu.with_memory_space_constraint(augmented, pltpu.VMEM),
        pltpu.with_memory_space_constraint(best, pltpu.VMEM),
    )
    return augmented, best.reshape(queries.shape[0])


def solution(mesh):
    return jax.shard_map(
        local,
        mesh=mesh,
        in_specs=(P("db", None), P("db", None), P("db"), P("pb", None)),
        out_specs=(P("db", None), P("pb")),
        check_vma=False,
    )
```

```python
import functools

import jax
import jax.numpy as jnp
from jax import lax
from jax.experimental import pallas as pl
from jax.experimental.pallas import tpu as pltpu
from jax.sharding import PartitionSpec as P

epsilon = 1e-06
MESH = pl.DeviceIdType.MESH
SIDE = 4
CORES = 2
CHIPS = SIDE * SIDE
SLOTS = (
    (0, 0), (0, 1), (0, 3), (1, 0), (3, 0), (0, 2), (2, 0), (1, 1),
    (1, 3), (3, 1), (3, 3), (1, 2), (2, 1), (3, 2), (2, 3), (2, 2),
)
SLOT_AT = {offset: place for place, offset in enumerate(SLOTS)}
RING = (1, 3, 2)
FAR_FIRST = (2, 1, 3)
EARLY = 12
PIECES = 4


def inverse_norm(values):
    return lax.rsqrt(jnp.sum(values * values, axis=-1, keepdims=True) + epsilon)


def dot_rows(left, right):
    return lax.dot_general(
        left, right, (((1,), (1,)), ((), ())), preferred_element_type=jnp.float32
    )


def kernel(
    db_hbm, nb_hbm, vc_hbm, q_ref, aug_ref, best_ref,
    q_v, q_t, db_ref, nb_ref, vc_ref, pool, mask_ref, wanted, total, coded, coded_in, row_range, ranges, ranges_in, ranges_of,
    everyone, first_top, tops, y_in, y_best, z_in, late_in, bases,
    q_sem, l_sem, a_recv, b_recv, c_recv, p_recv, g_recv, s_recv, ab_send, c_send, p_send,
    r_send, r_recv, g_send, s_send, y_send, y_recv, z_send, z_recv, t_send, t_recv, f_send, f_recv,
):
    rows_dev, features = db_ref.shape
    fanout = nb_ref.shape[0]
    own_rows = rows_dev // SIDE
    half = own_rows // 2
    parity_rows = CHIPS * own_rows
    span = 4 * own_rows
    x = lax.axis_index("pb")
    d = lax.axis_index("db")
    c = d % CORES
    chip = d // CORES
    y = chip % SIDE
    z = chip // SIDE
    mine = pl.multiple_of(x * own_rows, own_rows)

    def plane(dz, dy):
        return (x, ((z + dz) % SIDE * SIDE + (y + dy) % SIDE) * CORES + c)

    sibling = (x, chip * CORES + (1 - c))

    def across(dx):
        return ((x + dx) % SIDE, d)

    def remote(src, dst, send, recv, to):
        return pltpu.make_async_remote_copy(
            src_ref=src, dst_ref=dst, send_sem=send, recv_sem=recv, device_id=to,
            device_id_type=MESH,
        )

    loads = [
        pltpu.make_async_copy(
            db_hbm.at[pl.ds(mine, own_rows)], pool.at[pl.ds(0, own_rows)], l_sem.at[0]
        ),
        pltpu.make_async_copy(nb_hbm, nb_ref, l_sem.at[1]),
        pltpu.make_async_copy(vc_hbm, vc_ref, l_sem.at[2]),
        pltpu.make_async_copy(db_hbm, db_ref, l_sem.at[3]),
    ]
    loads[0].start()

    barrier = pltpu.get_barrier_semaphore()
    partners = [plane(0, step) for step in RING] + [plane(step, 0) for step in RING]
    partners += [sibling] + [across(step) for step in RING]
    for partner in partners:
        pl.semaphore_signal(barrier, inc=1, device_id=partner, device_id_type=MESH)

    for load in loads[1:]:
        load.start()

    loads[0].wait()
    pl.semaphore_wait(barrier, len(partners))

    def block(place, core, start, rows):
        return pool.at[pl.ds(core * parity_rows + place * own_rows + start, rows)]

    def copy_a(dz, dy):
        src = SLOT_AT[(0, dy if dz else 0)]
        dst = SLOT_AT[(dz, dy)]
        to = plane(dz, 0) if dz else plane(0, dy)
        return remote(
            block(src, 0, 0, half), block(dst, 0, 0, half), ab_send, a_recv.at[dst], to
        )

    def copy_b(dz, dy):
        src = SLOT_AT[(dz if dy else 0, 0)]
        dst = SLOT_AT[(dz, dy)]
        to = plane(0, dy) if dy else plane(dz, 0)
        return remote(
            block(src, 0, half, half), block(dst, 0, half, half), ab_send,
            (a_recv if dz and dy else b_recv).at[dst], to,
        )

    def copy_c(place):
        return remote(
            block(place, 0, 0, own_rows), block(place, 1, 0, own_rows), c_send,
            c_recv.at[place // 4], sibling,
        )

    for step in RING:
        copy_a(0, step).start()
        copy_b(step, 0).start()
    copy_c(0).start()
    for step in RING:
        copy_a(step, 0).start()
        copy_b(0, step).start()

    queries_here = q_v.shape[0]
    piece = queries_here // 4
    query_loads = [
        pltpu.make_async_copy(
            q_ref.at[pl.ds(pl.multiple_of(c * queries_here + k * piece, piece), piece)],
            q_v.at[pl.ds(k * piece, piece)],
            q_sem.at[k],
        )
        for k in range(4)
    ]
    for load in query_loads:
        load.start()
    for load in loads[1:]:
        load.wait()

    place_of = lax.broadcasted_iota(jnp.int32, (fanout, rows_dev), 0)
    wanted[...] = jnp.where(place_of < vc_ref[...], nb_ref[...], -1)
    for place, (dz, dy) in enumerate(SLOTS):
        for core in range(CORES):
            owner = ((z - dz) % SIDE * SIDE + (y - dy) % SIDE) * CORES + (c + core) % CORES
            bases[core * CHIPS + place] = owner * rows_dev + x * own_rows

    def build_mask(part):
        for u in range(2):
            counts = []
            for v in range(2):
                base = bases[part * 4 + u * 2 + v]
                number = base + lax.broadcasted_iota(jnp.int32, (own_rows, rows_dev), 0)
                count = jnp.zeros((own_rows, rows_dev), jnp.float32)
                for k in range(fanout):
                    count = count + jnp.where(wanted[pl.ds(k, 1), :] == number, 1.0, 0.0)
                counts.append(count)
            both = jnp.concatenate(counts, axis=0)
            mask_ref[part, :, pl.ds(u * 2 * own_rows, 2 * own_rows)] = both.T.astype(jnp.bfloat16)

    def first_masks(i, _):
        build_mask(4 * i)
        return 0

    def other_masks(i, _):
        build_mask(i + 1 + i // 3)
        return 0

    lax.fori_loop(0, 2, first_masks, 0)

    for step in RING:
        copy_a(0, step).wait_recv()
        for far in RING:
            copy_a(far, step).start()
        copy_b(step, 0).wait_recv()
        for far in RING:
            copy_b(step, far).start()

    lax.fori_loop(0, 6, other_masks, 0)

    for step in RING:
        copy_b(0, step).wait_recv()
        copy_c(SLOT_AT[(0, step)]).start()
        copy_a(step, 0).wait_recv()
        copy_c(SLOT_AT[(step, 0)]).start()

    def pass_on(place):
        here = block(place, 0, 0, own_rows)
        remote(here, here, ab_send, a_recv.at[place], sibling).wait_recv()
        copy_c(place).start()

    total[...] = jnp.zeros_like(total)
    own = db_ref[...]
    own_inverse = inverse_norm(own.astype(jnp.float32))

    def take(g):
        rows = pool[pl.ds(pl.multiple_of(g * span, span), span), :]
        squares = rows.astype(jnp.float32)
        squares = squares * squares
        folded = squares[:, 0:128]
        for k in range(1, features // 128):
            folded = folded + squares[:, k * 128 : (k + 1) * 128]
        far_inverse = lax.rsqrt(jnp.sum(folded.T, axis=0, keepdims=True) + epsilon)
        cosine = dot_rows(own, rows) * own_inverse * far_inverse
        halfway = (1.0 + cosine) * 0.5
        weight = halfway * halfway * halfway
        coefficient = (weight * far_inverse).astype(jnp.bfloat16).astype(jnp.float32)
        count = mask_ref[g].astype(jnp.float32)
        spread = jnp.where(count > 0.0, count * coefficient, 0.0)
        total[...] += jnp.dot(
            spread.astype(jnp.bfloat16), rows, preferred_element_type=jnp.float32
        )

    def step_over(i, _):
        part = jnp.where(i < 4, i // 2 + i % 2 * 4, jnp.where(i < 6, i - 2, i))

        @pl.when(i == 2)
        def _():
            pass_on(7)

        @pl.when((i == 4) | (i == 5))
        def _():
            for u in range(4):
                here = block(part * 4 + u, 0, 0, own_rows)
                remote(here, here, ab_send, a_recv.at[part * 4 + u], sibling).wait_recv()
            remote(
                block(part * 4, 0, 0, span), block(part * 4, 1, 0, span), c_send,
                c_recv.at[part], sibling,
            ).start()

        @pl.when(part >= 4)
        def _():
            here = pool.at[pl.ds(pl.multiple_of(part * span, span), span)]
            remote(here, here, c_send, c_recv.at[part - 4], sibling).wait_recv()

        take(part)
        return 0

    lax.fori_loop(0, 8, step_over, 0)

    pieces = coded_in.shape[0]
    piece_rows = own_rows // pieces

    def quarter(dx, n, rows):
        start = (x + SIDE + dx) % SIDE * own_rows + n * rows
        return pl.ds(pl.multiple_of(start, rows), rows)

    def copy_r(dx):
        return remote(ranges, ranges_in.at[dx - 1], r_send, r_recv, across(dx))

    def copy_p(dx, n):
        return remote(
            coded.at[quarter(dx, n, piece_rows)], coded_in.at[n, dx - 1], p_send, p_recv.at[n],
            across(dx),
        )

    def sent(ref, sem):
        remote(ref, ref, sem, sem, sibling).wait_send()

    for n in range(pieces):
        for q in range(SIDE):
            rows = pl.ds(q * own_rows + n * piece_rows, piece_rows)
            partial = total[rows, :]
            largest = jnp.max(jnp.abs(partial), axis=-1, keepdims=True)
            largest = jnp.maximum(largest, 1e-30)
            scaled = jnp.round(partial * (32760.0 / largest))
            coded[rows, :] = scaled.astype(jnp.int32).astype(jnp.int16)
            row_range[rows, :] = jnp.broadcast_to(largest * (1.0 / 32760.0), (piece_rows, 128))
        if n == 0:
            for dx in FAR_FIRST:
                copy_p(dx, n).start()
    ranges[...] = row_range[...].T[0:8, :]
    for dx in FAR_FIRST:
        copy_r(dx).start()
    for n in range(1, pieces):
        for dx in FAR_FIRST:
            copy_p(dx, n).start()

    for load in query_loads:
        load.wait()
    panel_rows = 512

    def turn(i, _):
        for u in range(4):
            rows = pl.ds(pl.multiple_of((i * 4 + u) * panel_rows, panel_rows), panel_rows)
            q_t[:, rows] = q_v[rows, :].T
        return 0

    turns = queries_here // (4 * panel_rows)
    lax.fori_loop(0, turns, turn, 0)

    others = (SIDE - 1) * half
    starts = (0, 2 * own_rows, 2 * own_rows + 2 * others)
    sizes = (own_rows, others, others)

    def copy_g(i, n):
        h, start = n * piece_rows // half, n * piece_rows % half
        return remote(
            everyone.at[pl.ds(n * piece_rows, piece_rows)],
            everyone.at[pl.ds(starts[1 + h] + i * half + start, piece_rows)],
            g_send, g_recv.at[h], across(FAR_FIRST[i]),
        )

    def copy_s(n):
        return remote(
            everyone.at[pl.ds(starts[n], sizes[n])],
            everyone.at[pl.ds(starts[n] + sizes[n], sizes[n])], s_send, s_recv.at[n], sibling,
        )

    sums = []
    for n in range(pieces):
        rows = quarter(0, n, piece_rows)
        kept = db_ref[rows, :].astype(jnp.float32)
        sums.append(kept * inverse_norm(kept) + total[rows, :])
    remote(ranges_in, ranges_in, r_send, r_recv, sibling).wait_recv()
    for dx in FAR_FIRST:
        across_range = jnp.broadcast_to(ranges_in[dx - 1, 0:1, :], (128, rows_dev))
        ranges_of[dx - 1] = across_range.T

    for n in range(pieces):
        summed = sums[n]
        here = coded_in.at[n]
        remote(here, here, p_send, p_recv.at[n], sibling).wait_recv()
        for dx in FAR_FIRST:
            part = coded_in[n, dx - 1].astype(jnp.float32)
            summed = summed + part * ranges_of[dx - 1, quarter(0, n, piece_rows), 0:1]
        rows = pl.ds(n * piece_rows, piece_rows)
        everyone[rows, :] = (summed * inverse_norm(summed)).astype(jnp.bfloat16)
        for i in range(SIDE - 1):
            copy_g(i, n).start()
    copy_s(0).start()

    def hand_over(h):
        here = everyone.at[pl.ds(starts[1 + h], others)]
        remote(here, here, g_send, g_recv.at[h], sibling).wait_recv()
        copy_s(1 + h).start()

    shares = tops.shape[0]
    share = queries_here // shares
    lines = share // 128

    def folded_scores(begin, end, k):
        panel = q_t[:, pl.ds(k * share, share)]
        scores = jnp.dot(
            everyone[pl.ds(begin, end - begin), :], panel, preferred_element_type=jnp.float32
        )
        return jnp.max(scores.reshape((end - begin) // 8, 8, share), axis=0)

    first, second, third = starts
    stop = 2 * rows_dev

    def finish(k, begin):
        top = jnp.maximum(first_top[k], folded_scores(begin, stop, k))
        top = jnp.max(top, axis=0, keepdims=True)
        for line in range(lines):
            tops[k, pl.ds(line, 1), :] = top[:, line * 128 : (line + 1) * 128]

    early = y_best.shape[0]
    early_shares, late_shares = pl.ds(0, early), pl.ds(early, shares - early)

    def copy_y(i):
        return remote(
            tops.at[early_shares], y_in.at[i], y_send, y_recv, plane(0, FAR_FIRST[i])
        )

    def copy_z(i, other):
        to_x, to_d = plane(FAR_FIRST[i], 0)
        if other:
            to_d = to_d + 1 - 2 * c
        return remote(
            y_best, z_in.at[other * (SIDE - 1) + i], z_send, z_recv, (to_x, to_d)
        )

    def copy_l(place):
        return remote(
            tops.at[late_shares], late_in.at[place - 1], t_send, t_recv, plane(*SLOTS[place])
        )

    def arrived(buffer, sem):
        remote(buffer, buffer, y_send, sem, sibling).wait_recv()

    copy_s(0).wait_recv()
    for k in range(shares):
        if k == shares * 3 // 4:
            hand_over(0)
        first_top[k] = folded_scores(first, second, k)
    copy_s(1).wait_recv()
    for k in range(early):
        if k == early // 2:
            hand_over(1)
        first_top[k] = jnp.maximum(first_top[k], folded_scores(second, third, k))
    copy_s(2).wait_recv()
    for k in range(early):
        finish(k, third)
    for i in range(SIDE - 1):
        copy_y(i).start()
    for k in range(early, shares):
        finish(k, second)
    for place in reversed(range(1, CHIPS)):
        copy_l(place).start()

    arrived(y_in, y_recv)
    best = tops[early_shares]
    for i in range(SIDE - 1):
        best = jnp.maximum(best, y_in[i])
    y_best[...] = best
    for other in range(CORES):
        for i in range(SIDE - 1):
            copy_z(i, other).start()
    remote(y_best, z_in.at[2 * (SIDE - 1)], z_send, z_recv, sibling).start()

    aug_ref[pl.ds(mine, own_rows), :] = everyone[pl.ds(0, own_rows), :]
    for h in range(2):
        for i in range(SIDE - 1):
            start = starts[1 + h] + i * half
            aug_ref[quarter(-FAR_FIRST[i], h, half), :] = everyone[pl.ds(start, half), :]

    arrived(late_in, t_recv)
    best = tops[late_shares]
    for i in range(CHIPS - 1):
        best = jnp.maximum(best, late_in[i])
    here = pl.ds(pl.multiple_of(c * shares, shares) + early, shares - early)
    best_ref[here] = best
    copy_f = remote(best_ref.at[here], best_ref.at[here], f_send, f_recv, sibling)
    copy_f.start()

    arrived(z_in, z_recv)
    for other in range(CORES):
        best = z_in[2 * (SIDE - 1)] if other else y_best[...]
        for i in range(SIDE - 1):
            best = jnp.maximum(best, z_in[other * (SIDE - 1) + i])
        start = (1 - c if other else c) * shares
        best_ref[pl.ds(pl.multiple_of(start, shares), early)] = best

    sent(pool.at[pl.ds(0, 2 * (CHIPS - 1) * half)], ab_send)
    sent(pool.at[pl.ds(0, parity_rows)], c_send)
    sent(ranges_in, r_send)
    sent(coded_in, p_send)
    sent(everyone.at[pl.ds(0, 6 * half)], g_send)
    sent(everyone.at[pl.ds(0, 8 * half)], s_send)
    sent(y_in, y_send)
    sent(z_in, z_send)
    sent(late_in, t_send)
    copy_f.wait()


def deliver(rows_in, best_in, rows_out, best_out):
    rows_out[...] = rows_in[...]
    best_out[...] = best_in[...]


def local(database, neighbours, valid_count, queries):
    rows_dev, features = database.shape
    fanout = neighbours.shape[1]
    queries_here = queries.shape[0] // CORES
    own_rows = rows_dev // SIDE
    pool_rows = rows_dev * CHIPS * CORES // SIDE
    share = queries_here // CHIPS
    vmem = pl.BlockSpec(memory_space=pltpu.VMEM)
    anywhere = pl.BlockSpec(memory_space=pl.ANY)
    dma = pltpu.SemaphoreType.DMA
    augmented, best = pl.pallas_call(
        kernel,
        out_shape=(
            pltpu.VMEM((rows_dev, features), jnp.bfloat16),
            pltpu.VMEM((CORES * CHIPS, share // 128, 128), jnp.float32),
        ),
        in_specs=[anywhere, anywhere, anywhere, anywhere],
        out_specs=(vmem, vmem),
        scratch_shapes=[
            pltpu.VMEM((queries_here, features), jnp.bfloat16),
            pltpu.VMEM((features, queries_here), jnp.bfloat16),
            pltpu.VMEM((rows_dev, features), jnp.bfloat16),
            pltpu.VMEM((fanout, rows_dev), jnp.int32),
            pltpu.VMEM((1, rows_dev), jnp.int32),
            pltpu.VMEM((pool_rows, features), jnp.bfloat16),
            pltpu.VMEM((8, rows_dev, pool_rows // 8), jnp.bfloat16),
            pltpu.VMEM((fanout, rows_dev), jnp.int32),
            pltpu.VMEM((rows_dev, features), jnp.float32),
            pltpu.VMEM((rows_dev, features), jnp.int16),
            pltpu.VMEM((PIECES, SIDE - 1, own_rows // PIECES, features), jnp.int16),
            pltpu.VMEM((rows_dev, 128), jnp.float32),
            pltpu.VMEM((8, rows_dev), jnp.float32),
            pltpu.VMEM((SIDE - 1, 8, rows_dev), jnp.float32),
            pltpu.VMEM((SIDE - 1, rows_dev, 128), jnp.float32),
            pltpu.VMEM((CORES * rows_dev, features), jnp.bfloat16),
            pltpu.VMEM((CHIPS, 8, share), jnp.float32),
            pltpu.VMEM((CHIPS, share // 128, 128), jnp.float32),
            pltpu.VMEM((SIDE - 1, EARLY, share // 128, 128), jnp.float32),
            pltpu.VMEM((EARLY, share // 128, 128), jnp.float32),
            pltpu.VMEM((2 * SIDE - 1, EARLY, share // 128, 128), jnp.float32),
            pltpu.VMEM((CHIPS - 1, CHIPS - EARLY, share // 128, 128), jnp.float32),
            pltpu.SMEM((CHIPS * CORES,), jnp.int32),
            dma((4,)),
            dma((4,)),
        ]
        + [dma((CHIPS,))] * 2
        + [dma((4,)), dma((PIECES,)), dma((2,)), dma((3,))]
        + [dma] * 15,
        compiler_params=pltpu.CompilerParams(
            collective_id=0, has_side_effects=True, vmem_limit_bytes=56 * 2**20
        ),
        name="expand_and_score",
    )(database, neighbours.T, valid_count.reshape(1, rows_dev), queries)
    augmented, best = pl.pallas_call(
        deliver,
        out_shape=(
            jax.ShapeDtypeStruct(augmented.shape, augmented.dtype),
            jax.ShapeDtypeStruct(best.shape, best.dtype),
        ),
        in_specs=[vmem, vmem],
        out_specs=(vmem, vmem),
        name="deliver",
    )(
        pltpu.with_memory_space_constraint(augmented, pltpu.VMEM),
        pltpu.with_memory_space_constraint(best, pltpu.VMEM),
    )
    return augmented, best.reshape(queries.shape[0])


def solution(mesh):
    return jax.shard_map(
        local,
        mesh=mesh,
        in_specs=(P("db", None), P("db", None), P("db"), P("pb", None)),
        out_specs=(P("db", None), P("pb")),
        check_vma=False,
    )
```

```python
import functools

import jax
import jax.numpy as jnp
from jax import lax
from jax.experimental import pallas as pl
from jax.experimental.pallas import tpu as pltpu
from jax.sharding import PartitionSpec as P

epsilon = 1e-06
MESH = pl.DeviceIdType.MESH
SIDE = 4
CORES = 2
CHIPS = SIDE * SIDE
SLOTS = (
    (0, 0), (0, 1), (0, 3), (1, 0), (3, 0), (0, 2), (2, 0), (1, 1),
    (1, 3), (3, 1), (3, 3), (1, 2), (2, 1), (3, 2), (2, 3), (2, 2),
)
SLOT_AT = {offset: place for place, offset in enumerate(SLOTS)}
RING = (1, 3, 2)
FAR_FIRST = (2, 1, 3)
EARLY = 12
MASKS_FIRST = 4
PIECES = 4


def inverse_norm(values):
    return lax.rsqrt(jnp.sum(values * values, axis=-1, keepdims=True) + epsilon)


def dot_rows(left, right):
    return lax.dot_general(
        left, right, (((1,), (1,)), ((), ())), preferred_element_type=jnp.float32
    )


def kernel(
    db_hbm, nb_hbm, vc_hbm, q_ref, aug_ref, best_ref,
    q_v, q_t, db_ref, nb_ref, vc_ref, pool, mask_ref, wanted, total, coded, coded_in, row_range, ranges, ranges_in, ranges_of,
    own_scale, everyone, first_top, tops, y_in, y_best, z_in, late_in, bases,
    q_sem, l_sem, a_recv, b_recv, c_recv, p_recv, g_recv, s_recv, ab_send, c_send, p_send,
    r_send, r_recv, g_send, s_send, y_send, y_recv, z_send, z_recv, t_send, t_recv, f_send, f_recv,
):
    rows_dev, features = db_ref.shape
    fanout = nb_ref.shape[0]
    own_rows = rows_dev // SIDE
    half = own_rows // 2
    parity_rows = CHIPS * own_rows
    span = 4 * own_rows
    x = lax.axis_index("pb")
    d = lax.axis_index("db")
    c = d % CORES
    chip = d // CORES
    y = chip % SIDE
    z = chip // SIDE
    mine = pl.multiple_of(x * own_rows, own_rows)

    def plane(dz, dy):
        return (x, ((z + dz) % SIDE * SIDE + (y + dy) % SIDE) * CORES + c)

    sibling = (x, chip * CORES + (1 - c))

    def across(dx):
        return ((x + dx) % SIDE, d)

    def remote(src, dst, send, recv, to):
        return pltpu.make_async_remote_copy(
            src_ref=src, dst_ref=dst, send_sem=send, recv_sem=recv, device_id=to,
            device_id_type=MESH,
        )

    loads = [
        pltpu.make_async_copy(
            db_hbm.at[pl.ds(mine, own_rows)], pool.at[pl.ds(0, own_rows)], l_sem.at[0]
        ),
        pltpu.make_async_copy(nb_hbm, nb_ref, l_sem.at[1]),
        pltpu.make_async_copy(vc_hbm, vc_ref, l_sem.at[2]),
        pltpu.make_async_copy(db_hbm, db_ref, l_sem.at[3]),
    ]
    loads[0].start()

    barrier = pltpu.get_barrier_semaphore()
    partners = [plane(0, step) for step in RING] + [plane(step, 0) for step in RING]
    partners += [sibling] + [across(step) for step in RING]
    for partner in partners:
        pl.semaphore_signal(barrier, inc=1, device_id=partner, device_id_type=MESH)

    for load in loads[1:]:
        load.start()

    loads[0].wait()
    pl.semaphore_wait(barrier, len(partners))

    def block(place, core, start, rows):
        return pool.at[pl.ds(core * parity_rows + place * own_rows + start, rows)]

    def copy_a(dz, dy):
        src = SLOT_AT[(0, dy if dz else 0)]
        dst = SLOT_AT[(dz, dy)]
        to = plane(dz, 0) if dz else plane(0, dy)
        return remote(
            block(src, 0, 0, half), block(dst, 0, 0, half), ab_send, a_recv.at[dst], to
        )

    def copy_b(dz, dy):
        src = SLOT_AT[(dz if dy else 0, 0)]
        dst = SLOT_AT[(dz, dy)]
        to = plane(0, dy) if dy else plane(dz, 0)
        return remote(
            block(src, 0, half, half), block(dst, 0, half, half), ab_send,
            (a_recv if dz and dy else b_recv).at[dst], to,
        )

    def copy_c(place):
        return remote(
            block(place, 0, 0, own_rows), block(place, 1, 0, own_rows), c_send,
            c_recv.at[place // 4], sibling,
        )

    for step in RING:
        copy_a(0, step).start()
        copy_b(step, 0).start()
    copy_c(0).start()
    for step in RING:
        copy_a(step, 0).start()
        copy_b(0, step).start()

    queries_here = q_v.shape[0]
    piece = queries_here // 4
    query_loads = [
        pltpu.make_async_copy(
            q_ref.at[pl.ds(pl.multiple_of(c * queries_here + k * piece, piece), piece)],
            q_v.at[pl.ds(k * piece, piece)],
            q_sem.at[k],
        )
        for k in range(4)
    ]
    for load in query_loads:
        load.start()
    for load in loads[1:]:
        load.wait()

    place_of = lax.broadcasted_iota(jnp.int32, (fanout, rows_dev), 0)
    wanted[...] = jnp.where(place_of < vc_ref[...], nb_ref[...], -1)
    for place, (dz, dy) in enumerate(SLOTS):
        for core in range(CORES):
            owner = ((z - dz) % SIDE * SIDE + (y - dy) % SIDE) * CORES + (c + core) % CORES
            bases[core * CHIPS + place] = owner * rows_dev + x * own_rows

    def build_mask(part):
        for u in range(2):
            counts = []
            for v in range(2):
                base = bases[part * 4 + u * 2 + v]
                number = (base + lax.broadcasted_iota(jnp.int32, (own_rows, rows_dev), 0)).astype(jnp.int16)
                count = jnp.zeros((own_rows, rows_dev), jnp.int16)
                for k in range(fanout):
                    here = jnp.broadcast_to(wanted[pl.ds(k, 1), :], (16, rows_dev)).astype(jnp.int16)
                    here = jnp.concatenate([here] * (own_rows // 16), axis=0)
                    count = count + jnp.where(here == number, jnp.int16(1), jnp.int16(0))
                counts.append(count.astype(jnp.int32).astype(jnp.float32))
            both = jnp.concatenate(counts, axis=0)
            mask_ref[part, :, pl.ds(u * 2 * own_rows, 2 * own_rows)] = both.T.astype(jnp.bfloat16)

    def mask_step(i, _):
        build_mask(jnp.where(i < 2, 4 * i, i - 1 + (i - 2) // 3))
        return 0

    total[...] = jnp.zeros_like(total)
    own_scale[...] = inverse_norm(db_ref[...].astype(jnp.float32))
    groups = 8
    lax.fori_loop(0, MASKS_FIRST, mask_step, 0)

    for step in RING:
        copy_a(0, step).wait_recv()
        for far in RING:
            copy_a(far, step).start()
        copy_b(step, 0).wait_recv()
        for far in RING:
            copy_b(step, far).start()

    lax.fori_loop(MASKS_FIRST, groups, mask_step, 0)

    for step in RING:
        copy_b(0, step).wait_recv()
        copy_a(step, 0).wait_recv()
    remote(
        block(1, 0, 0, 3 * own_rows), block(1, 1, 0, 3 * own_rows), c_send, c_recv.at[0], sibling
    ).start()
    remote(
        block(4, 0, 0, 3 * own_rows), block(4, 1, 0, 3 * own_rows), c_send, c_recv.at[1], sibling
    ).start()

    def pass_on(place):
        here = block(place, 0, 0, own_rows)
        remote(here, here, ab_send, a_recv.at[place], sibling).wait_recv()
        copy_c(place).start()

    own = db_ref[...]
    own_inverse = own_scale[...]

    def take(g):
        rows = pool[pl.ds(pl.multiple_of(g * span, span), span), :]
        squares = rows.astype(jnp.float32)
        squares = squares * squares
        folded = squares[:, 0:128]
        for k in range(1, features // 128):
            folded = folded + squares[:, k * 128 : (k + 1) * 128]
        far_inverse = lax.rsqrt(jnp.sum(folded.T, axis=0, keepdims=True) + epsilon)
        cosine = dot_rows(own, rows) * own_inverse * far_inverse
        halfway = (1.0 + cosine) * 0.5
        weight = halfway * halfway * halfway
        coefficient = (weight * far_inverse).astype(jnp.bfloat16).astype(jnp.float32)
        count = mask_ref[g].astype(jnp.float32)
        spread = jnp.where(count > 0.0, count * coefficient, 0.0)
        total[...] += jnp.dot(
            spread.astype(jnp.bfloat16), rows, preferred_element_type=jnp.float32
        )

    def step_over(i, _):
        part = jnp.where(i < 4, i // 2 + i % 2 * 4, jnp.where(i < 6, i - 2, i))

        @pl.when(i == 2)
        def _():
            pass_on(7)

        @pl.when((i == 4) | (i == 5))
        def _():
            for u in range(4):
                here = block(part * 4 + u, 0, 0, own_rows)
                remote(here, here, ab_send, a_recv.at[part * 4 + u], sibling).wait_recv()
            remote(
                block(part * 4, 0, 0, span), block(part * 4, 1, 0, span), c_send,
                c_recv.at[part], sibling,
            ).start()

        @pl.when(part >= 4)
        def _():
            here = pool.at[pl.ds(pl.multiple_of(part * span, span), span)]
            remote(here, here, c_send, c_recv.at[part - 4], sibling).wait_recv()

        take(part)
        return 0

    lax.fori_loop(0, 8, step_over, 0)

    pieces = coded_in.shape[0]
    piece_rows = own_rows // pieces

    def quarter(dx, n, rows):
        start = (x + SIDE + dx) % SIDE * own_rows + n * rows
        return pl.ds(pl.multiple_of(start, rows), rows)

    def copy_r(dx):
        return remote(ranges, ranges_in.at[dx - 1], r_send, r_recv, across(dx))

    def copy_p(dx, n):
        return remote(
            coded.at[quarter(dx, n, piece_rows)], coded_in.at[n, dx - 1], p_send, p_recv.at[n],
            across(dx),
        )

    def sent(ref, sem):
        remote(ref, ref, sem, sem, sibling).wait_send()

    for n in range(pieces):
        for q in range(SIDE):
            rows = pl.ds(q * own_rows + n * piece_rows, piece_rows)
            partial = total[rows, :]
            largest = jnp.max(jnp.abs(partial), axis=-1, keepdims=True)
            largest = jnp.maximum(largest, 1e-30)
            scaled = jnp.round(partial * (32760.0 / largest))
            coded[rows, :] = scaled.astype(jnp.int32).astype(jnp.int16)
            row_range[rows, :] = jnp.broadcast_to(largest * (1.0 / 32760.0), (piece_rows, 128))
        if n == 0:
            for dx in FAR_FIRST:
                copy_p(dx, n).start()
    ranges[...] = row_range[...].T[0:8, :]
    for dx in FAR_FIRST:
        copy_r(dx).start()
    for n in range(1, pieces):
        for dx in FAR_FIRST:
            copy_p(dx, n).start()

    for load in query_loads:
        load.wait()
    panel_rows = 512

    def turn(i, _):
        for u in range(4):
            rows = pl.ds(pl.multiple_of((i * 4 + u) * panel_rows, panel_rows), panel_rows)
            q_t[:, rows] = q_v[rows, :].T
        return 0

    turns = queries_here // (4 * panel_rows)
    lax.fori_loop(0, turns, turn, 0)

    others = (SIDE - 1) * half
    starts = (0, 2 * own_rows, 2 * own_rows + 2 * others)
    sizes = (own_rows, others, others)

    def copy_g(i, n):
        h, start = n * piece_rows // half, n * piece_rows % half
        return remote(
            everyone.at[pl.ds(n * piece_rows, piece_rows)],
            everyone.at[pl.ds(starts[1 + h] + i * half + start, piece_rows)],
            g_send, g_recv.at[h], across(FAR_FIRST[i]),
        )

    def copy_s(n):
        return remote(
            everyone.at[pl.ds(starts[n], sizes[n])],
            everyone.at[pl.ds(starts[n] + sizes[n], sizes[n])], s_send, s_recv.at[n], sibling,
        )

    sums = []
    for n in range(pieces):
        rows = quarter(0, n, piece_rows)
        kept = db_ref[rows, :].astype(jnp.float32)
        sums.append(kept * inverse_norm(kept) + total[rows, :])
    remote(ranges_in, ranges_in, r_send, r_recv, sibling).wait_recv()
    for dx in FAR_FIRST:
        across_range = jnp.broadcast_to(ranges_in[dx - 1, 0:1, :], (128, rows_dev))
        ranges_of[dx - 1] = across_range.T

    for n in range(pieces):
        summed = sums[n]
        here = coded_in.at[n]
        remote(here, here, p_send, p_recv.at[n], sibling).wait_recv()
        for dx in FAR_FIRST:
            part = coded_in[n, dx - 1].astype(jnp.float32)
            summed = summed + part * ranges_of[dx - 1, quarter(0, n, piece_rows), 0:1]
        rows = pl.ds(n * piece_rows, piece_rows)
        everyone[rows, :] = (summed * inverse_norm(summed)).astype(jnp.bfloat16)
        for i in range(SIDE - 1):
            copy_g(i, n).start()
    copy_s(0).start()

    def hand_over(h):
        here = everyone.at[pl.ds(starts[1 + h], others)]
        remote(here, here, g_send, g_recv.at[h], sibling).wait_recv()
        copy_s(1 + h).start()

    shares = tops.shape[0]
    share = queries_here // shares
    lines = share // 128

    def folded_scores(begin, end, k):
        panel = q_t[:, pl.ds(k * share, share)]
        scores = jnp.dot(
            everyone[pl.ds(begin, end - begin), :], panel, preferred_element_type=jnp.float32
        )
        return jnp.max(scores.reshape((end - begin) // 8, 8, share), axis=0)

    first, second, third = starts
    stop = 2 * rows_dev

    def finish(k, begin):
        top = jnp.maximum(first_top[k], folded_scores(begin, stop, k))
        top = jnp.max(top, axis=0, keepdims=True)
        for line in range(lines):
            tops[k, pl.ds(line, 1), :] = top[:, line * 128 : (line + 1) * 128]

    early = y_best.shape[0]
    early_shares, late_shares = pl.ds(0, early), pl.ds(early, shares - early)

    def copy_y(i):
        return remote(
            tops.at[early_shares], y_in.at[i], y_send, y_recv, plane(0, FAR_FIRST[i])
        )

    def copy_z(i, other):
        to_x, to_d = plane(FAR_FIRST[i], 0)
        if other:
            to_d = to_d + 1 - 2 * c
        return remote(
            y_best, z_in.at[other * (SIDE - 1) + i], z_send, z_recv, (to_x, to_d)
        )

    def copy_l(place):
        return remote(
            tops.at[late_shares], late_in.at[place - 1], t_send, t_recv, plane(*SLOTS[place])
        )

    def arrived(buffer, sem):
        remote(buffer, buffer, y_send, sem, sibling).wait_recv()

    copy_s(0).wait_recv()
    for k in range(shares):
        if k == shares * 3 // 4:
            hand_over(0)
        first_top[k] = folded_scores(first, second, k)
    copy_s(1).wait_recv()
    for k in range(early):
        if k == early // 2:
            hand_over(1)
        first_top[k] = jnp.maximum(first_top[k], folded_scores(second, third, k))
    copy_s(2).wait_recv()
    for k in range(early):
        finish(k, third)
    for i in range(SIDE - 1):
        copy_y(i).start()
    for k in range(early, shares):
        finish(k, second)
    for place in reversed(range(1, CHIPS)):
        copy_l(place).start()

    arrived(y_in, y_recv)
    best = tops[early_shares]
    for i in range(SIDE - 1):
        best = jnp.maximum(best, y_in[i])
    y_best[...] = best
    for other in range(CORES):
        for i in range(SIDE - 1):
            copy_z(i, other).start()
    remote(y_best, z_in.at[2 * (SIDE - 1)], z_send, z_recv, sibling).start()

    aug_ref[pl.ds(mine, own_rows), :] = everyone[pl.ds(0, own_rows), :]
    for h in range(2):
        for i in range(SIDE - 1):
            start = starts[1 + h] + i * half
            aug_ref[quarter(-FAR_FIRST[i], h, half), :] = everyone[pl.ds(start, half), :]

    arrived(late_in, t_recv)
    best = tops[late_shares]
    for i in range(CHIPS - 1):
        best = jnp.maximum(best, late_in[i])
    here = pl.ds(pl.multiple_of(c * shares, shares) + early, shares - early)
    best_ref[here] = best
    copy_f = remote(best_ref.at[here], best_ref.at[here], f_send, f_recv, sibling)
    copy_f.start()

    arrived(z_in, z_recv)
    for other in range(CORES):
        best = z_in[2 * (SIDE - 1)] if other else y_best[...]
        for i in range(SIDE - 1):
            best = jnp.maximum(best, z_in[other * (SIDE - 1) + i])
        start = (1 - c if other else c) * shares
        best_ref[pl.ds(pl.multiple_of(start, shares), early)] = best

    sent(pool.at[pl.ds(0, 2 * (CHIPS - 1) * half)], ab_send)
    sent(pool.at[pl.ds(0, parity_rows)], c_send)
    sent(ranges_in, r_send)
    sent(coded_in, p_send)
    sent(everyone.at[pl.ds(0, 6 * half)], g_send)
    sent(everyone.at[pl.ds(0, 8 * half)], s_send)
    sent(y_in, y_send)
    sent(z_in, z_send)
    sent(late_in, t_send)
    copy_f.wait()


def deliver(rows_in, best_in, rows_out, best_out):
    rows_out[...] = rows_in[...]
    best_out[...] = best_in[...]


def local(database, neighbours, valid_count, queries):
    rows_dev, features = database.shape
    fanout = neighbours.shape[1]
    queries_here = queries.shape[0] // CORES
    own_rows = rows_dev // SIDE
    pool_rows = rows_dev * CHIPS * CORES // SIDE
    share = queries_here // CHIPS
    vmem = pl.BlockSpec(memory_space=pltpu.VMEM)
    anywhere = pl.BlockSpec(memory_space=pl.ANY)
    dma = pltpu.SemaphoreType.DMA
    augmented, best = pl.pallas_call(
        kernel,
        out_shape=(
            pltpu.VMEM((rows_dev, features), jnp.bfloat16),
            pltpu.VMEM((CORES * CHIPS, share // 128, 128), jnp.float32),
        ),
        in_specs=[anywhere, anywhere, anywhere, anywhere],
        out_specs=(vmem, vmem),
        scratch_shapes=[
            pltpu.VMEM((queries_here, features), jnp.bfloat16),
            pltpu.VMEM((features, queries_here), jnp.bfloat16),
            pltpu.VMEM((rows_dev, features), jnp.bfloat16),
            pltpu.VMEM((fanout, rows_dev), jnp.int32),
            pltpu.VMEM((1, rows_dev), jnp.int32),
            pltpu.VMEM((pool_rows, features), jnp.bfloat16),
            pltpu.VMEM((8, rows_dev, pool_rows // 8), jnp.bfloat16),
            pltpu.VMEM((fanout, rows_dev), jnp.int32),
            pltpu.VMEM((rows_dev, features), jnp.float32),
            pltpu.VMEM((rows_dev, features), jnp.int16),
            pltpu.VMEM((PIECES, SIDE - 1, own_rows // PIECES, features), jnp.int16),
            pltpu.VMEM((rows_dev, 128), jnp.float32),
            pltpu.VMEM((8, rows_dev), jnp.float32),
            pltpu.VMEM((SIDE - 1, 8, rows_dev), jnp.float32),
            pltpu.VMEM((SIDE - 1, rows_dev, 128), jnp.float32),
            pltpu.VMEM((rows_dev, 1), jnp.float32),
            pltpu.VMEM((CORES * rows_dev, features), jnp.bfloat16),
            pltpu.VMEM((CHIPS, 8, share), jnp.float32),
            pltpu.VMEM((CHIPS, share // 128, 128), jnp.float32),
            pltpu.VMEM((SIDE - 1, EARLY, share // 128, 128), jnp.float32),
            pltpu.VMEM((EARLY, share // 128, 128), jnp.float32),
            pltpu.VMEM((2 * SIDE - 1, EARLY, share // 128, 128), jnp.float32),
            pltpu.VMEM((CHIPS - 1, CHIPS - EARLY, share // 128, 128), jnp.float32),
            pltpu.SMEM((CHIPS * CORES,), jnp.int32),
            dma((4,)),
            dma((4,)),
        ]
        + [dma((CHIPS,))] * 2
        + [dma((4,)), dma((PIECES,)), dma((2,)), dma((3,))]
        + [dma] * 15,
        compiler_params=pltpu.CompilerParams(
            collective_id=0, has_side_effects=True, vmem_limit_bytes=56 * 2**20
        ),
        name="expand_and_score",
    )(database, neighbours.T, valid_count.reshape(1, rows_dev), queries)
    augmented, best = pl.pallas_call(
        deliver,
        out_shape=(
            jax.ShapeDtypeStruct(augmented.shape, augmented.dtype),
            jax.ShapeDtypeStruct(best.shape, best.dtype),
        ),
        in_specs=[vmem, vmem],
        out_specs=(vmem, vmem),
        name="deliver",
    )(
        pltpu.with_memory_space_constraint(augmented, pltpu.VMEM),
        pltpu.with_memory_space_constraint(best, pltpu.VMEM),
    )
    return augmented, best.reshape(queries.shape[0])


def solution(mesh):
    return jax.shard_map(
        local,
        mesh=mesh,
        in_specs=(P("db", None), P("db", None), P("db"), P("pb", None)),
        out_specs=(P("db", None), P("pb")),
        check_vma=False,
    )
```

```python
import functools

import jax
import jax.numpy as jnp
from jax import lax
from jax.experimental import pallas as pl
from jax.experimental.pallas import tpu as pltpu
from jax.sharding import PartitionSpec as P

epsilon = 1e-06
MESH = pl.DeviceIdType.MESH
SIDE = 4
CORES = 2
CHIPS = SIDE * SIDE
SLOTS = (
    (0, 0), (0, 1), (0, 3), (1, 0), (3, 0), (0, 2), (2, 0), (1, 1),
    (1, 3), (3, 1), (3, 3), (1, 2), (2, 1), (3, 2), (2, 3), (2, 2),
)
SLOT_AT = {offset: place for place, offset in enumerate(SLOTS)}
RING = (1, 3, 2)
FAR_FIRST = (2, 1, 3)
EARLY = 12
MASKS_FIRST = 4
PIECES = 4


def inverse_norm(values):
    return lax.rsqrt(jnp.sum(values * values, axis=-1, keepdims=True) + epsilon)


def dot_rows(left, right):
    return lax.dot_general(
        left, right, (((1,), (1,)), ((), ())), preferred_element_type=jnp.float32
    )


def kernel(
    db_hbm, nb_hbm, vc_hbm, q_ref, aug_ref, best_ref,
    q_v, q_t, db_ref, nb_ref, vc_ref, pool, mask_ref, wanted, total, coded, coded_in, row_range, ranges, ranges_in, ranges_of,
    own_scale, everyone, first_top, tops, y_in, y_best, z_in, late_in, bases,
    q_sem, l_sem, a_recv, b_recv, c_recv, p_recv, g_recv, s_recv, ab_send, c_send, p_send,
    r_send, r_recv, g_send, s_send, y_send, y_recv, z_send, z_recv, t_send, t_recv, f_send, f_recv,
):
    rows_dev, features = db_ref.shape
    fanout = nb_ref.shape[0]
    own_rows = rows_dev // SIDE
    half = own_rows // 2
    parity_rows = CHIPS * own_rows
    span = 4 * own_rows
    x = lax.axis_index("pb")
    d = lax.axis_index("db")
    c = d % CORES
    chip = d // CORES
    y = chip % SIDE
    z = chip // SIDE
    mine = pl.multiple_of(x * own_rows, own_rows)

    def plane(dz, dy):
        return (x, ((z + dz) % SIDE * SIDE + (y + dy) % SIDE) * CORES + c)

    sibling = (x, chip * CORES + (1 - c))

    def across(dx):
        return ((x + dx) % SIDE, d)

    def remote(src, dst, send, recv, to):
        return pltpu.make_async_remote_copy(
            src_ref=src, dst_ref=dst, send_sem=send, recv_sem=recv, device_id=to,
            device_id_type=MESH,
        )

    loads = [
        pltpu.make_async_copy(
            db_hbm.at[pl.ds(mine, own_rows)], pool.at[pl.ds(0, own_rows)], l_sem.at[0]
        ),
        pltpu.make_async_copy(nb_hbm, nb_ref, l_sem.at[1]),
        pltpu.make_async_copy(vc_hbm, vc_ref, l_sem.at[2]),
        pltpu.make_async_copy(db_hbm, db_ref, l_sem.at[3]),
    ]
    loads[0].start()

    barrier = pltpu.get_barrier_semaphore()
    partners = [plane(0, step) for step in RING] + [plane(step, 0) for step in RING]
    partners += [sibling] + [across(step) for step in RING]
    for partner in partners:
        pl.semaphore_signal(barrier, inc=1, device_id=partner, device_id_type=MESH)

    for load in loads[1:]:
        load.start()

    loads[0].wait()
    pl.semaphore_wait(barrier, len(partners))

    def block(place, core, start, rows):
        return pool.at[pl.ds(core * parity_rows + place * own_rows + start, rows)]

    def copy_a(dz, dy):
        src = SLOT_AT[(0, dy if dz else 0)]
        dst = SLOT_AT[(dz, dy)]
        to = plane(dz, 0) if dz else plane(0, dy)
        return remote(
            block(src, 0, 0, half), block(dst, 0, 0, half), ab_send, a_recv.at[dst], to
        )

    def copy_b(dz, dy):
        src = SLOT_AT[(dz if dy else 0, 0)]
        dst = SLOT_AT[(dz, dy)]
        to = plane(0, dy) if dy else plane(dz, 0)
        return remote(
            block(src, 0, half, half), block(dst, 0, half, half), ab_send,
            (a_recv if dz and dy else b_recv).at[dst], to,
        )

    def copy_c(place):
        return remote(
            block(place, 0, 0, own_rows), block(place, 1, 0, own_rows), c_send,
            c_recv.at[place // 4], sibling,
        )

    for step in RING:
        copy_a(0, step).start()
        copy_b(step, 0).start()
    for step in RING:
        copy_a(step, 0).start()
        copy_b(0, step).start()
    copy_c(0).start()

    queries_here = q_v.shape[0]
    piece = queries_here // 4
    query_loads = [
        pltpu.make_async_copy(
            q_ref.at[pl.ds(pl.multiple_of(c * queries_here + k * piece, piece), piece)],
            q_v.at[pl.ds(k * piece, piece)],
            q_sem.at[k],
        )
        for k in range(4)
    ]
    for load in query_loads:
        load.start()
    for load in loads[1:]:
        load.wait()

    place_of = lax.broadcasted_iota(jnp.int32, (fanout, rows_dev), 0)
    wanted[...] = jnp.where(place_of < vc_ref[...], nb_ref[...], -1)
    for place, (dz, dy) in enumerate(SLOTS):
        for core in range(CORES):
            owner = ((z - dz) % SIDE * SIDE + (y - dy) % SIDE) * CORES + (c + core) % CORES
            bases[core * CHIPS + place] = owner * rows_dev + x * own_rows

    def build_mask(part):
        for u in range(2):
            counts = []
            for v in range(2):
                base = bases[part * 4 + u * 2 + v]
                number = (base + lax.broadcasted_iota(jnp.int32, (own_rows, rows_dev), 0)).astype(jnp.int16)
                count = jnp.zeros((own_rows, rows_dev), jnp.int16)
                for k in range(fanout):
                    here = jnp.broadcast_to(wanted[pl.ds(k, 1), :], (16, rows_dev)).astype(jnp.int16)
                    here = jnp.concatenate([here] * (own_rows // 16), axis=0)
                    count = count + jnp.where(here == number, jnp.int16(1), jnp.int16(0))
                counts.append(count.astype(jnp.int32).astype(jnp.float32))
            both = jnp.concatenate(counts, axis=0)
            mask_ref[part, :, pl.ds(u * 2 * own_rows, 2 * own_rows)] = both.T.astype(jnp.bfloat16)

    def mask_step(i, _):
        build_mask(jnp.where(i < 2, 4 * i, i - 1 + (i - 2) // 3))
        return 0

    total[...] = jnp.zeros_like(total)
    own_scale[...] = inverse_norm(db_ref[...].astype(jnp.float32))
    groups = 8
    lax.fori_loop(0, MASKS_FIRST, mask_step, 0)

    for step in RING:
        copy_a(0, step).wait_recv()
        for far in RING:
            copy_a(far, step).start()
        copy_b(step, 0).wait_recv()
        for far in RING:
            copy_b(step, far).start()

    lax.fori_loop(MASKS_FIRST, groups, mask_step, 0)

    for step in RING:
        copy_b(0, step).wait_recv()
        copy_a(step, 0).wait_recv()
    remote(
        block(1, 0, 0, 3 * own_rows), block(1, 1, 0, 3 * own_rows), c_send, c_recv.at[0], sibling
    ).start()
    remote(
        block(4, 0, 0, 3 * own_rows), block(4, 1, 0, 3 * own_rows), c_send, c_recv.at[1], sibling
    ).start()

    def pass_on(place):
        here = block(place, 0, 0, own_rows)
        remote(here, here, ab_send, a_recv.at[place], sibling).wait_recv()
        copy_c(place).start()

    own = db_ref[...]
    own_inverse = own_scale[...]

    def take(g):
        rows = pool[pl.ds(pl.multiple_of(g * span, span), span), :]
        squares = rows.astype(jnp.float32)
        squares = squares * squares
        folded = squares[:, 0:128]
        for k in range(1, features // 128):
            folded = folded + squares[:, k * 128 : (k + 1) * 128]
        far_inverse = lax.rsqrt(jnp.sum(folded.T, axis=0, keepdims=True) + epsilon)
        cosine = dot_rows(own, rows) * own_inverse * far_inverse
        halfway = (1.0 + cosine) * 0.5
        weight = halfway * halfway * halfway
        coefficient = (weight * far_inverse).astype(jnp.bfloat16).astype(jnp.float32)
        count = mask_ref[g].astype(jnp.float32)
        spread = jnp.where(count > 0.0, count * coefficient, 0.0)
        total[...] += jnp.dot(
            spread.astype(jnp.bfloat16), rows, preferred_element_type=jnp.float32
        )

    def step_over(i, _):
        part = jnp.where(i < 4, i // 2 + i % 2 * 4, jnp.where(i < 6, i - 2, i))

        @pl.when(i == 2)
        def _():
            pass_on(7)

        @pl.when((i == 4) | (i == 5))
        def _():
            for u in range(4):
                here = block(part * 4 + u, 0, 0, own_rows)
                remote(here, here, ab_send, a_recv.at[part * 4 + u], sibling).wait_recv()
                if u % 2:
                    remote(
                        block(part * 4 + u - 1, 0, 0, span // 2),
                        block(part * 4 + u - 1, 1, 0, span // 2), c_send, c_recv.at[part], sibling,
                    ).start()

        @pl.when(part >= 4)
        def _():
            here = pool.at[pl.ds(pl.multiple_of(part * span, span), span)]
            remote(here, here, c_send, c_recv.at[part - 4], sibling).wait_recv()

        take(part)
        return 0

    lax.fori_loop(0, 8, step_over, 0)

    pieces = coded_in.shape[0]
    piece_rows = own_rows // pieces

    def quarter(dx, n, rows):
        start = (x + SIDE + dx) % SIDE * own_rows + n * rows
        return pl.ds(pl.multiple_of(start, rows), rows)

    def copy_r(dx):
        return remote(ranges, ranges_in.at[dx - 1], r_send, r_recv, across(dx))

    def copy_p(dx, n):
        return remote(
            coded.at[quarter(dx, n, piece_rows)], coded_in.at[n, dx - 1], p_send, p_recv.at[n],
            across(dx),
        )

    def sent(ref, sem):
        remote(ref, ref, sem, sem, sibling).wait_send()

    for n in range(pieces):
        for q in range(SIDE):
            rows = pl.ds(q * own_rows + n * piece_rows, piece_rows)
            partial = total[rows, :]
            largest = jnp.max(jnp.abs(partial), axis=-1, keepdims=True)
            largest = jnp.maximum(largest, 1e-30)
            scaled = jnp.round(partial * (32760.0 / largest))
            coded[rows, :] = scaled.astype(jnp.int32).astype(jnp.int16)
            row_range[rows, :] = jnp.broadcast_to(largest * (1.0 / 32760.0), (piece_rows, 128))
        if n == 0:
            for dx in FAR_FIRST:
                copy_p(dx, n).start()
    ranges[...] = row_range[...].T[0:8, :]
    for dx in FAR_FIRST:
        copy_r(dx).start()
    for n in range(1, pieces):
        for dx in FAR_FIRST:
            copy_p(dx, n).start()

    for load in query_loads:
        load.wait()
    panel_rows = 512

    def turn(i, _):
        for u in range(4):
            rows = pl.ds(pl.multiple_of((i * 4 + u) * panel_rows, panel_rows), panel_rows)
            q_t[:, rows] = q_v[rows, :].T
        return 0

    turns = queries_here // (4 * panel_rows)
    lax.fori_loop(0, turns, turn, 0)

    others = (SIDE - 1) * half
    starts = (0, 2 * own_rows, 2 * own_rows + 2 * others)
    sizes = (own_rows, others, others)

    def copy_g(i, n):
        h, start = n * piece_rows // half, n * piece_rows % half
        return remote(
            everyone.at[pl.ds(n * piece_rows, piece_rows)],
            everyone.at[pl.ds(starts[1 + h] + i * half + start, piece_rows)],
            g_send, g_recv.at[h], across(FAR_FIRST[i]),
        )

    def copy_s(n):
        return remote(
            everyone.at[pl.ds(starts[n], sizes[n])],
            everyone.at[pl.ds(starts[n] + sizes[n], sizes[n])], s_send, s_recv.at[n], sibling,
        )

    sums = []
    for n in range(pieces):
        rows = quarter(0, n, piece_rows)
        kept = db_ref[rows, :].astype(jnp.float32)
        sums.append(kept * inverse_norm(kept) + total[rows, :])
    remote(ranges_in, ranges_in, r_send, r_recv, sibling).wait_recv()
    for dx in FAR_FIRST:
        across_range = jnp.broadcast_to(ranges_in[dx - 1, 0:1, :], (128, rows_dev))
        ranges_of[dx - 1] = across_range.T

    for n in range(pieces):
        summed = sums[n]
        here = coded_in.at[n]
        remote(here, here, p_send, p_recv.at[n], sibling).wait_recv()
        for dx in FAR_FIRST:
            part = coded_in[n, dx - 1].astype(jnp.float32)
            summed = summed + part * ranges_of[dx - 1, quarter(0, n, piece_rows), 0:1]
        rows = pl.ds(n * piece_rows, piece_rows)
        everyone[rows, :] = (summed * inverse_norm(summed)).astype(jnp.bfloat16)
        for i in range(SIDE - 1):
            copy_g(i, n).start()
    copy_s(0).start()

    def hand_over(h):
        here = everyone.at[pl.ds(starts[1 + h], others)]
        remote(here, here, g_send, g_recv.at[h], sibling).wait_recv()
        copy_s(1 + h).start()

    shares = tops.shape[0]
    share = queries_here // shares
    lines = share // 128

    def folded_scores(begin, end, k):
        panel = q_t[:, pl.ds(k * share, share)]
        scores = jnp.dot(
            everyone[pl.ds(begin, end - begin), :], panel, preferred_element_type=jnp.float32
        )
        return jnp.max(scores.reshape((end - begin) // 8, 8, share), axis=0)

    first, second, third = starts
    stop = 2 * rows_dev

    def finish(k, begin):
        top = jnp.maximum(first_top[k], folded_scores(begin, stop, k))
        top = jnp.max(top, axis=0, keepdims=True)
        for line in range(lines):
            tops[k, pl.ds(line, 1), :] = top[:, line * 128 : (line + 1) * 128]

    early = y_best.shape[0]
    early_shares, late_shares = pl.ds(0, early), pl.ds(early, shares - early)

    def copy_y(i):
        return remote(
            tops.at[early_shares], y_in.at[i], y_send, y_recv, plane(0, FAR_FIRST[i])
        )

    def copy_z(i, other):
        to_x, to_d = plane(FAR_FIRST[i], 0)
        if other:
            to_d = to_d + 1 - 2 * c
        return remote(
            y_best, z_in.at[other * (SIDE - 1) + i], z_send, z_recv, (to_x, to_d)
        )

    def copy_l(place):
        return remote(
            tops.at[late_shares], late_in.at[place - 1], t_send, t_recv, plane(*SLOTS[place])
        )

    def arrived(buffer, sem):
        remote(buffer, buffer, y_send, sem, sibling).wait_recv()

    copy_s(0).wait_recv()
    for k in range(shares):
        if k == shares * 3 // 4:
            hand_over(0)
        first_top[k] = folded_scores(first, second, k)
    copy_s(1).wait_recv()
    for k in range(early):
        if k == early // 2:
            hand_over(1)
        first_top[k] = jnp.maximum(first_top[k], folded_scores(second, third, k))
    copy_s(2).wait_recv()
    for k in range(early):
        finish(k, third)
    for i in range(SIDE - 1):
        copy_y(i).start()
    for k in range(early, shares):
        finish(k, second)
    for place in reversed(range(1, CHIPS)):
        copy_l(place).start()

    arrived(y_in, y_recv)
    best = tops[early_shares]
    for i in range(SIDE - 1):
        best = jnp.maximum(best, y_in[i])
    y_best[...] = best
    for other in range(CORES):
        for i in range(SIDE - 1):
            copy_z(i, other).start()
    remote(y_best, z_in.at[2 * (SIDE - 1)], z_send, z_recv, sibling).start()

    aug_ref[pl.ds(mine, own_rows), :] = everyone[pl.ds(0, own_rows), :]
    for h in range(2):
        for i in range(SIDE - 1):
            start = starts[1 + h] + i * half
            aug_ref[quarter(-FAR_FIRST[i], h, half), :] = everyone[pl.ds(start, half), :]

    arrived(late_in, t_recv)
    best = tops[late_shares]
    for i in range(CHIPS - 1):
        best = jnp.maximum(best, late_in[i])
    here = pl.ds(pl.multiple_of(c * shares, shares) + early, shares - early)
    best_ref[here] = best
    copy_f = remote(best_ref.at[here], best_ref.at[here], f_send, f_recv, sibling)
    copy_f.start()

    arrived(z_in, z_recv)
    for other in range(CORES):
        best = z_in[2 * (SIDE - 1)] if other else y_best[...]
        for i in range(SIDE - 1):
            best = jnp.maximum(best, z_in[other * (SIDE - 1) + i])
        start = (1 - c if other else c) * shares
        best_ref[pl.ds(pl.multiple_of(start, shares), early)] = best

    sent(pool.at[pl.ds(0, 2 * (CHIPS - 1) * half)], ab_send)
    sent(pool.at[pl.ds(0, parity_rows)], c_send)
    sent(ranges_in, r_send)
    sent(coded_in, p_send)
    sent(everyone.at[pl.ds(0, 6 * half)], g_send)
    sent(everyone.at[pl.ds(0, 8 * half)], s_send)
    sent(y_in, y_send)
    sent(z_in, z_send)
    sent(late_in, t_send)
    copy_f.wait()


def deliver(rows_in, best_in, rows_out, best_out):
    rows_out[...] = rows_in[...]
    best_out[...] = best_in[...]


def local(database, neighbours, valid_count, queries):
    rows_dev, features = database.shape
    fanout = neighbours.shape[1]
    queries_here = queries.shape[0] // CORES
    own_rows = rows_dev // SIDE
    pool_rows = rows_dev * CHIPS * CORES // SIDE
    share = queries_here // CHIPS
    vmem = pl.BlockSpec(memory_space=pltpu.VMEM)
    anywhere = pl.BlockSpec(memory_space=pl.ANY)
    dma = pltpu.SemaphoreType.DMA
    augmented, best = pl.pallas_call(
        kernel,
        out_shape=(
            pltpu.VMEM((rows_dev, features), jnp.bfloat16),
            pltpu.VMEM((CORES * CHIPS, share // 128, 128), jnp.float32),
        ),
        in_specs=[anywhere, anywhere, anywhere, anywhere],
        out_specs=(vmem, vmem),
        scratch_shapes=[
            pltpu.VMEM((queries_here, features), jnp.bfloat16),
            pltpu.VMEM((features, queries_here), jnp.bfloat16),
            pltpu.VMEM((rows_dev, features), jnp.bfloat16),
            pltpu.VMEM((fanout, rows_dev), jnp.int32),
            pltpu.VMEM((1, rows_dev), jnp.int32),
            pltpu.VMEM((pool_rows, features), jnp.bfloat16),
            pltpu.VMEM((8, rows_dev, pool_rows // 8), jnp.bfloat16),
            pltpu.VMEM((fanout, rows_dev), jnp.int32),
            pltpu.VMEM((rows_dev, features), jnp.float32),
            pltpu.VMEM((rows_dev, features), jnp.int16),
            pltpu.VMEM((PIECES, SIDE - 1, own_rows // PIECES, features), jnp.int16),
            pltpu.VMEM((rows_dev, 128), jnp.float32),
            pltpu.VMEM((8, rows_dev), jnp.float32),
            pltpu.VMEM((SIDE - 1, 8, rows_dev), jnp.float32),
            pltpu.VMEM((SIDE - 1, rows_dev, 128), jnp.float32),
            pltpu.VMEM((rows_dev, 1), jnp.float32),
            pltpu.VMEM((CORES * rows_dev, features), jnp.bfloat16),
            pltpu.VMEM((CHIPS, 8, share), jnp.float32),
            pltpu.VMEM((CHIPS, share // 128, 128), jnp.float32),
            pltpu.VMEM((SIDE - 1, EARLY, share // 128, 128), jnp.float32),
            pltpu.VMEM((EARLY, share // 128, 128), jnp.float32),
            pltpu.VMEM((2 * SIDE - 1, EARLY, share // 128, 128), jnp.float32),
            pltpu.VMEM((CHIPS - 1, CHIPS - EARLY, share // 128, 128), jnp.float32),
            pltpu.SMEM((CHIPS * CORES,), jnp.int32),
            dma((4,)),
            dma((4,)),
        ]
        + [dma((CHIPS,))] * 2
        + [dma((4,)), dma((PIECES,)), dma((2,)), dma((3,))]
        + [dma] * 15,
        compiler_params=pltpu.CompilerParams(
            collective_id=0, has_side_effects=True, vmem_limit_bytes=56 * 2**20
        ),
        name="expand_and_score",
    )(database, neighbours.T, valid_count.reshape(1, rows_dev), queries)
    augmented, best = pl.pallas_call(
        deliver,
        out_shape=(
            jax.ShapeDtypeStruct(augmented.shape, augmented.dtype),
            jax.ShapeDtypeStruct(best.shape, best.dtype),
        ),
        in_specs=[vmem, vmem],
        out_specs=(vmem, vmem),
        name="deliver",
    )(
        pltpu.with_memory_space_constraint(augmented, pltpu.VMEM),
        pltpu.with_memory_space_constraint(best, pltpu.VMEM),
    )
    return augmented, best.reshape(queries.shape[0])


def solution(mesh):
    return jax.shard_map(
        local,
        mesh=mesh,
        in_specs=(P("db", None), P("db", None), P("db"), P("pb", None)),
        out_specs=(P("db", None), P("pb")),
        check_vma=False,
    )
```

```python
import functools

import jax
import jax.numpy as jnp
from jax import lax
from jax.experimental import pallas as pl
from jax.experimental.pallas import tpu as pltpu
from jax.sharding import PartitionSpec as P

epsilon = 1e-06
MESH = pl.DeviceIdType.MESH
SIDE = 4
CORES = 2
CHIPS = SIDE * SIDE
SLOTS = (
    (0, 0), (0, 1), (0, 3), (1, 0), (3, 0), (0, 2), (2, 0), (1, 1),
    (1, 3), (3, 1), (3, 3), (1, 2), (2, 1), (3, 2), (2, 3), (2, 2),
)
SLOT_AT = {offset: place for place, offset in enumerate(SLOTS)}
RING = (1, 3, 2)
FAR_FIRST = (2, 1, 3)
EARLY = 12
MASKS_FIRST = 4
PIECES = 4


def inverse_norm(values):
    return lax.rsqrt(jnp.sum(values * values, axis=-1, keepdims=True) + epsilon)


def dot_rows(left, right):
    return lax.dot_general(
        left, right, (((1,), (1,)), ((), ())), preferred_element_type=jnp.float32
    )


def kernel(
    db_hbm, nb_hbm, vc_hbm, q_ref, aug_ref, best_ref,
    q_v, q_t, db_ref, nb_ref, vc_ref, pool, mask_ref, wanted, total, coded, coded_in, row_range, ranges, ranges_in, ranges_of,
    own_scale, everyone, first_top, tops, y_in, y_best, z_in, late_in, bases,
    q_sem, l_sem, a_recv, b_recv, c_recv, p_recv, g_recv, s_recv, ab_send, c_send, p_send,
    r_send, r_recv, g_send, s_send, y_send, y_recv, z_send, z_recv, t_send, t_recv, f_send, f_recv,
):
    rows_dev, features = db_ref.shape
    fanout = nb_ref.shape[0]
    own_rows = rows_dev // SIDE
    half = own_rows // 2
    parity_rows = CHIPS * own_rows
    span = 4 * own_rows
    x = lax.axis_index("pb")
    d = lax.axis_index("db")
    c = d % CORES
    chip = d // CORES
    y = chip % SIDE
    z = chip // SIDE
    mine = pl.multiple_of(x * own_rows, own_rows)

    def plane(dz, dy):
        return (x, ((z + dz) % SIDE * SIDE + (y + dy) % SIDE) * CORES + c)

    sibling = (x, chip * CORES + (1 - c))

    def across(dx):
        return ((x + dx) % SIDE, d)

    def remote(src, dst, send, recv, to):
        return pltpu.make_async_remote_copy(
            src_ref=src, dst_ref=dst, send_sem=send, recv_sem=recv, device_id=to,
            device_id_type=MESH,
        )

    loads = [
        pltpu.make_async_copy(
            db_hbm.at[pl.ds(mine, own_rows)], pool.at[pl.ds(0, own_rows)], l_sem.at[0]
        ),
        pltpu.make_async_copy(nb_hbm, nb_ref, l_sem.at[1]),
        pltpu.make_async_copy(vc_hbm, vc_ref, l_sem.at[2]),
        pltpu.make_async_copy(db_hbm, db_ref, l_sem.at[3]),
    ]
    loads[0].start()

    barrier = pltpu.get_barrier_semaphore()
    partners = [plane(0, step) for step in RING] + [plane(step, 0) for step in RING]
    partners += [sibling] + [across(step) for step in RING]
    for partner in partners:
        pl.semaphore_signal(barrier, inc=1, device_id=partner, device_id_type=MESH)

    for load in loads[1:]:
        load.start()

    loads[0].wait()
    pl.semaphore_wait(barrier, len(partners))

    def block(place, core, start, rows):
        return pool.at[pl.ds(core * parity_rows + place * own_rows + start, rows)]

    def copy_a(dz, dy):
        src = SLOT_AT[(0, dy if dz else 0)]
        dst = SLOT_AT[(dz, dy)]
        to = plane(dz, 0) if dz else plane(0, dy)
        return remote(
            block(src, 0, 0, half), block(dst, 0, 0, half), ab_send, a_recv.at[dst], to
        )

    def copy_b(dz, dy):
        src = SLOT_AT[(dz if dy else 0, 0)]
        dst = SLOT_AT[(dz, dy)]
        to = plane(0, dy) if dy else plane(dz, 0)
        return remote(
            block(src, 0, half, half), block(dst, 0, half, half), ab_send,
            (a_recv if dz and dy else b_recv).at[dst], to,
        )

    def copy_c(place):
        return remote(
            block(place, 0, 0, own_rows), block(place, 1, 0, own_rows), c_send,
            c_recv.at[place // 4], sibling,
        )

    for step in RING:
        copy_a(0, step).start()
        copy_b(step, 0).start()
    for step in RING:
        copy_a(step, 0).start()
        copy_b(0, step).start()
    copy_c(0).start()

    queries_here = q_v.shape[0]
    piece = queries_here // 4
    query_loads = [
        pltpu.make_async_copy(
            q_ref.at[pl.ds(pl.multiple_of(c * queries_here + k * piece, piece), piece)],
            q_v.at[pl.ds(k * piece, piece)],
            q_sem.at[k],
        )
        for k in range(4)
    ]
    for load in query_loads:
        load.start()
    for load in loads[1:]:
        load.wait()

    place_of = lax.broadcasted_iota(jnp.int32, (fanout, rows_dev), 0)
    wanted[...] = jnp.where(place_of < vc_ref[...], nb_ref[...], -1)
    for place, (dz, dy) in enumerate(SLOTS):
        for core in range(CORES):
            owner = ((z - dz) % SIDE * SIDE + (y - dy) % SIDE) * CORES + (c + core) % CORES
            bases[core * CHIPS + place] = owner * rows_dev + x * own_rows

    def build_mask(part):
        for u in range(2):
            counts = []
            for v in range(2):
                base = bases[part * 4 + u * 2 + v]
                number = (base + lax.broadcasted_iota(jnp.int32, (own_rows, rows_dev), 0)).astype(jnp.int16)
                count = jnp.zeros((own_rows, rows_dev), jnp.int16)
                for k in range(fanout):
                    here = jnp.broadcast_to(wanted[pl.ds(k, 1), :], (16, rows_dev)).astype(jnp.int16)
                    here = jnp.concatenate([here] * (own_rows // 16), axis=0)
                    count = count + jnp.where(here == number, jnp.int16(1), jnp.int16(0))
                counts.append(count.astype(jnp.int32).astype(jnp.float32))
            both = jnp.concatenate(counts, axis=0)
            mask_ref[part, :, pl.ds(u * 2 * own_rows, 2 * own_rows)] = both.T.astype(jnp.bfloat16)

    def mask_step(i, _):
        build_mask(jnp.where(i < 2, 4 * i, i - 1 + (i - 2) // 3))
        return 0

    total[...] = jnp.zeros_like(total)
    own_scale[...] = inverse_norm(db_ref[...].astype(jnp.float32))
    groups = 8
    lax.fori_loop(0, MASKS_FIRST, mask_step, 0)

    for step in RING:
        copy_a(0, step).wait_recv()
        for far in RING:
            copy_a(far, step).start()
        copy_b(step, 0).wait_recv()
        for far in RING:
            copy_b(step, far).start()

    lax.fori_loop(MASKS_FIRST, groups, mask_step, 0)

    for step in RING:
        copy_b(0, step).wait_recv()
        copy_a(step, 0).wait_recv()
    remote(
        block(1, 0, 0, 3 * own_rows), block(1, 1, 0, 3 * own_rows), c_send, c_recv.at[0], sibling
    ).start()
    remote(
        block(4, 0, 0, 3 * own_rows), block(4, 1, 0, 3 * own_rows), c_send, c_recv.at[1], sibling
    ).start()

    def pass_on(place):
        here = block(place, 0, 0, own_rows)
        remote(here, here, ab_send, a_recv.at[place], sibling).wait_recv()
        copy_c(place).start()

    own = db_ref[...]
    own_inverse = own_scale[...]

    def take(g):
        rows = pool[pl.ds(pl.multiple_of(g * span, span), span), :]
        squares = rows.astype(jnp.float32)
        squares = squares * squares
        folded = squares[:, 0:128]
        for k in range(1, features // 128):
            folded = folded + squares[:, k * 128 : (k + 1) * 128]
        far_inverse = lax.rsqrt(jnp.sum(folded.T, axis=0, keepdims=True) + epsilon)
        cosine = dot_rows(own, rows) * own_inverse * far_inverse
        halfway = (1.0 + cosine) * 0.5
        weight = halfway * halfway * halfway
        coefficient = (weight * far_inverse).astype(jnp.bfloat16).astype(jnp.float32)
        count = mask_ref[g].astype(jnp.float32)
        spread = jnp.where(count > 0.0, count * coefficient, 0.0)
        total[...] += jnp.dot(
            spread.astype(jnp.bfloat16), rows, preferred_element_type=jnp.float32
        )

    def step_over(i, _):
        part = jnp.where(i < 4, i // 2 + i % 2 * 4, jnp.where(i < 6, i - 2, i))

        @pl.when(i == 2)
        def _():
            pass_on(7)

        @pl.when((i == 4) | (i == 5))
        def _():
            for u in range(4):
                here = block(part * 4 + u, 0, 0, own_rows)
                remote(here, here, ab_send, a_recv.at[part * 4 + u], sibling).wait_recv()
                if u % 2:
                    remote(
                        block(part * 4 + u - 1, 0, 0, span // 2),
                        block(part * 4 + u - 1, 1, 0, span // 2), c_send, c_recv.at[part], sibling,
                    ).start()

        @pl.when(part >= 4)
        def _():
            here = pool.at[pl.ds(pl.multiple_of(part * span, span), span)]
            remote(here, here, c_send, c_recv.at[part - 4], sibling).wait_recv()

        take(part)
        return 0

    lax.fori_loop(0, 8, step_over, 0)

    pieces = coded_in.shape[0]
    piece_rows = own_rows // pieces

    def quarter(dx, n, rows):
        start = (x + SIDE + dx) % SIDE * own_rows + n * rows
        return pl.ds(pl.multiple_of(start, rows), rows)

    def copy_r(dx):
        return remote(ranges, ranges_in.at[dx - 1], r_send, r_recv, across(dx))

    def copy_p(dx, n):
        return remote(
            coded.at[quarter(dx, n, piece_rows)], coded_in.at[n, dx - 1], p_send, p_recv.at[n],
            across(dx),
        )

    def sent(ref, sem):
        remote(ref, ref, sem, sem, sibling).wait_send()

    for n in range(pieces):
        for q in range(SIDE):
            rows = pl.ds(q * own_rows + n * piece_rows, piece_rows)
            partial = total[rows, :]
            largest = jnp.max(jnp.abs(partial), axis=-1, keepdims=True)
            largest = jnp.maximum(largest, 1e-30)
            scaled = jnp.round(partial * (32760.0 / largest))
            coded[rows, :] = scaled.astype(jnp.int32).astype(jnp.int16)
            row_range[rows, :] = jnp.broadcast_to(largest * (1.0 / 32760.0), (piece_rows, 128))
        if n == 0:
            for dx in FAR_FIRST:
                copy_p(dx, n).start()
    ranges[...] = row_range[...].T[0:8, :]
    for dx in FAR_FIRST:
        copy_r(dx).start()
    for n in range(1, pieces):
        for dx in FAR_FIRST:
            copy_p(dx, n).start()

    for load in query_loads:
        load.wait()
    panel_rows = 512

    def turn(i, _):
        for u in range(4):
            rows = pl.ds(pl.multiple_of((i * 4 + u) * panel_rows, panel_rows), panel_rows)
            q_t[:, rows] = q_v[rows, :].T
        return 0

    turns = queries_here // (4 * panel_rows)
    lax.fori_loop(0, turns, turn, 0)

    others = (SIDE - 1) * half
    starts = (0, 2 * own_rows, 2 * own_rows + 2 * others)
    sizes = (own_rows, others, others)

    def copy_g(i, n):
        h, start = n * piece_rows // half, n * piece_rows % half
        return remote(
            everyone.at[pl.ds(n * piece_rows, piece_rows)],
            everyone.at[pl.ds(starts[1 + h] + i * half + start, piece_rows)],
            g_send, g_recv.at[h], across(FAR_FIRST[i]),
        )

    def copy_s(n):
        return remote(
            everyone.at[pl.ds(starts[n], sizes[n])],
            everyone.at[pl.ds(starts[n] + sizes[n], sizes[n])], s_send, s_recv.at[n], sibling,
        )

    sums = []
    for n in range(pieces):
        rows = quarter(0, n, piece_rows)
        kept = db_ref[rows, :].astype(jnp.float32)
        sums.append(kept * inverse_norm(kept) + total[rows, :])
    remote(ranges_in, ranges_in, r_send, r_recv, sibling).wait_recv()
    for dx in FAR_FIRST:
        across_range = jnp.broadcast_to(ranges_in[dx - 1, 0:1, :], (128, rows_dev))
        ranges_of[dx - 1] = across_range.T

    for n in range(pieces):
        summed = sums[n]
        here = coded_in.at[n]
        remote(here, here, p_send, p_recv.at[n], sibling).wait_recv()
        for dx in FAR_FIRST:
            part = coded_in[n, dx - 1].astype(jnp.float32)
            summed = summed + part * ranges_of[dx - 1, quarter(0, n, piece_rows), 0:1]
        rows = pl.ds(n * piece_rows, piece_rows)
        everyone[rows, :] = (summed * inverse_norm(summed)).astype(jnp.bfloat16)
        for i in range(SIDE - 1):
            copy_g(i, n).start()
    copy_s(0).start()

    def hand_over(h):
        here = everyone.at[pl.ds(starts[1 + h], others)]
        remote(here, here, g_send, g_recv.at[h], sibling).wait_recv()
        copy_s(1 + h).start()

    shares = tops.shape[0]
    share = queries_here // shares
    lines = share // 128

    def folded_scores(begin, end, k):
        panel = q_t[:, pl.ds(k * share, share)]
        scores = jnp.dot(
            everyone[pl.ds(begin, end - begin), :], panel, preferred_element_type=jnp.float32
        )
        return jnp.max(scores.reshape((end - begin) // 8, 8, share), axis=0)

    first, second, third = starts
    stop = 2 * rows_dev

    def finish(k, begin):
        top = jnp.maximum(first_top[k], folded_scores(begin, stop, k))
        top = jnp.max(top, axis=0, keepdims=True)
        for line in range(lines):
            tops[k, pl.ds(line, 1), :] = top[:, line * 128 : (line + 1) * 128]

    early = y_best.shape[0]
    early_shares, late_shares = pl.ds(0, early), pl.ds(early, shares - early)

    def copy_y(i):
        return remote(
            tops.at[early_shares], y_in.at[i], y_send, y_recv, plane(0, FAR_FIRST[i])
        )

    def copy_z(i, other):
        to_x, to_d = plane(FAR_FIRST[i], 0)
        if other:
            to_d = to_d + 1 - 2 * c
        return remote(
            y_best, z_in.at[other * (SIDE - 1) + i], z_send, z_recv, (to_x, to_d)
        )

    def copy_l(place):
        return remote(
            tops.at[late_shares], late_in.at[place - 1], t_send, t_recv, plane(*SLOTS[place])
        )

    def arrived(buffer, sem):
        remote(buffer, buffer, y_send, sem, sibling).wait_recv()

    copy_s(0).wait_recv()
    for k in range(shares):
        if k == shares // 2:
            hand_over(0)
        first_top[k] = folded_scores(first, second, k)
    copy_s(1).wait_recv()
    for k in range(early):
        if k == early // 2:
            hand_over(1)
        first_top[k] = jnp.maximum(first_top[k], folded_scores(second, third, k))
    copy_s(2).wait_recv()
    for k in range(early):
        finish(k, third)
    for i in range(SIDE - 1):
        copy_y(i).start()
    for k in range(early, shares):
        finish(k, second)
    for place in reversed(range(1, CHIPS)):
        copy_l(place).start()

    arrived(y_in, y_recv)
    best = tops[early_shares]
    for i in range(SIDE - 1):
        best = jnp.maximum(best, y_in[i])
    y_best[...] = best
    for other in range(CORES):
        for i in range(SIDE - 1):
            copy_z(i, other).start()
    remote(y_best, z_in.at[2 * (SIDE - 1)], z_send, z_recv, sibling).start()

    aug_ref[pl.ds(mine, own_rows), :] = everyone[pl.ds(0, own_rows), :]
    for h in range(2):
        for i in range(SIDE - 1):
            start = starts[1 + h] + i * half
            aug_ref[quarter(-FAR_FIRST[i], h, half), :] = everyone[pl.ds(start, half), :]

    arrived(late_in, t_recv)
    best = tops[late_shares]
    for i in range(CHIPS - 1):
        best = jnp.maximum(best, late_in[i])
    here = pl.ds(pl.multiple_of(c * shares, shares) + early, shares - early)
    best_ref[here] = best
    copy_f = remote(best_ref.at[here], best_ref.at[here], f_send, f_recv, sibling)
    copy_f.start()

    arrived(z_in, z_recv)
    for other in range(CORES):
        best = z_in[2 * (SIDE - 1)] if other else y_best[...]
        for i in range(SIDE - 1):
            best = jnp.maximum(best, z_in[other * (SIDE - 1) + i])
        start = (1 - c if other else c) * shares
        best_ref[pl.ds(pl.multiple_of(start, shares), early)] = best

    sent(pool.at[pl.ds(0, 2 * (CHIPS - 1) * half)], ab_send)
    sent(pool.at[pl.ds(0, parity_rows)], c_send)
    sent(ranges_in, r_send)
    sent(coded_in, p_send)
    sent(everyone.at[pl.ds(0, 6 * half)], g_send)
    sent(everyone.at[pl.ds(0, 8 * half)], s_send)
    sent(y_in, y_send)
    sent(z_in, z_send)
    sent(late_in, t_send)
    copy_f.wait()


def deliver(rows_in, best_in, rows_out, best_out):
    rows_out[...] = rows_in[...]
    best_out[...] = best_in[...]


def local(database, neighbours, valid_count, queries):
    rows_dev, features = database.shape
    fanout = neighbours.shape[1]
    queries_here = queries.shape[0] // CORES
    own_rows = rows_dev // SIDE
    pool_rows = rows_dev * CHIPS * CORES // SIDE
    share = queries_here // CHIPS
    vmem = pl.BlockSpec(memory_space=pltpu.VMEM)
    anywhere = pl.BlockSpec(memory_space=pl.ANY)
    dma = pltpu.SemaphoreType.DMA
    augmented, best = pl.pallas_call(
        kernel,
        out_shape=(
            pltpu.VMEM((rows_dev, features), jnp.bfloat16),
            pltpu.VMEM((CORES * CHIPS, share // 128, 128), jnp.float32),
        ),
        in_specs=[anywhere, anywhere, anywhere, anywhere],
        out_specs=(vmem, vmem),
        scratch_shapes=[
            pltpu.VMEM((queries_here, features), jnp.bfloat16),
            pltpu.VMEM((features, queries_here), jnp.bfloat16),
            pltpu.VMEM((rows_dev, features), jnp.bfloat16),
            pltpu.VMEM((fanout, rows_dev), jnp.int32),
            pltpu.VMEM((1, rows_dev), jnp.int32),
            pltpu.VMEM((pool_rows, features), jnp.bfloat16),
            pltpu.VMEM((8, rows_dev, pool_rows // 8), jnp.bfloat16),
            pltpu.VMEM((fanout, rows_dev), jnp.int32),
            pltpu.VMEM((rows_dev, features), jnp.float32),
            pltpu.VMEM((rows_dev, features), jnp.int16),
            pltpu.VMEM((PIECES, SIDE - 1, own_rows // PIECES, features), jnp.int16),
            pltpu.VMEM((rows_dev, 128), jnp.float32),
            pltpu.VMEM((8, rows_dev), jnp.float32),
            pltpu.VMEM((SIDE - 1, 8, rows_dev), jnp.float32),
            pltpu.VMEM((SIDE - 1, rows_dev, 128), jnp.float32),
            pltpu.VMEM((rows_dev, 1), jnp.float32),
            pltpu.VMEM((CORES * rows_dev, features), jnp.bfloat16),
            pltpu.VMEM((CHIPS, 8, share), jnp.float32),
            pltpu.VMEM((CHIPS, share // 128, 128), jnp.float32),
            pltpu.VMEM((SIDE - 1, EARLY, share // 128, 128), jnp.float32),
            pltpu.VMEM((EARLY, share // 128, 128), jnp.float32),
            pltpu.VMEM((2 * SIDE - 1, EARLY, share // 128, 128), jnp.float32),
            pltpu.VMEM((CHIPS - 1, CHIPS - EARLY, share // 128, 128), jnp.float32),
            pltpu.SMEM((CHIPS * CORES,), jnp.int32),
            dma((4,)),
            dma((4,)),
        ]
        + [dma((CHIPS,))] * 2
        + [dma((4,)), dma((PIECES,)), dma((2,)), dma((3,))]
        + [dma] * 15,
        compiler_params=pltpu.CompilerParams(
            collective_id=0, has_side_effects=True, vmem_limit_bytes=56 * 2**20
        ),
        name="expand_and_score",
    )(database, neighbours.T, valid_count.reshape(1, rows_dev), queries)
    augmented, best = pl.pallas_call(
        deliver,
        out_shape=(
            jax.ShapeDtypeStruct(augmented.shape, augmented.dtype),
            jax.ShapeDtypeStruct(best.shape, best.dtype),
        ),
        in_specs=[vmem, vmem],
        out_specs=(vmem, vmem),
        name="deliver",
    )(
        pltpu.with_memory_space_constraint(augmented, pltpu.VMEM),
        pltpu.with_memory_space_constraint(best, pltpu.VMEM),
    )
    return augmented, best.reshape(queries.shape[0])


def solution(mesh):
    return jax.shard_map(
        local,
        mesh=mesh,
        in_specs=(P("db", None), P("db", None), P("db"), P("pb", None)),
        out_specs=(P("db", None), P("pb")),
        check_vma=False,
    )
```
